32 devices in a mesh: dp: 8 (over z, y), chan: 4 (over x, core).
Axes of the slice: x: 2, y: 2, z: 4, core: 2. Of those that a mesh axis runs over, the one named last changes fastest.
Arguments:
- image_rows: float32 [8, 16, 16, 640], P('dp', 'chan'), may hold values from -6 to 6
- groups: int32 [8], P('dp'), may hold values from 0 to 1, as said below
- conv_first: float32 [3, 3, 640, 640], P(None, None, 'chan'), may hold values from -0.078125 to 0.078125
- conv_second: float32 [3, 3, 640, 640], P(None, None, 'chan'), may hold values from -0.078125 to 0.078125
- gain_first: float32 [640], P('chan'), may hold values from 0.25 to 1.75
- shift_first: float32 [640], P('chan'), may hold values from -3 to 3
- gain_second: float32 [640], P('chan'), may hold values from 0.25 to 1.75
- shift_second: float32 [640], P('chan'), may hold values from -3 to 3
- cotangent: float32 [8, 16, 16, 640], P('dp', None, None, 'chan'), may hold values from -6 to 6
Outputs:
- block_out: float32 [8, 16, 16, 640], P('dp', None, None, 'chan')
- input_grad: float32 [8, 16, 16, 640], P('dp', 'chan')
- conv_first_grad: float32 [3, 3, 640, 640], P(None, None, 'chan')
- conv_second_grad: float32 [3, 3, 640, 640], P(None, None, 'chan')
- gain_first_grad: float32 [640], P('chan')
- shift_first_grad: float32 [640], P('chan')
- gain_second_grad: float32 [640], P('chan')
- shift_second_grad: float32 [640], P('chan')
- grad_norm: float32 [], replicated
The draws below stay inside these ranges and needn't reach their ends.
Inputs may be any that keep to these rules, and one draw needn't show every extreme that they name: `groups`: 1 marks a 16 x 16 map, 0 a map of half that side in the top left corner; each aligned block of 1 images holds at least one 1.
All inputs are finite; a program needn't handle non-finite values.
Results may differ from the reference program's by a relative error of at most 0.0003.
Values sent between devices are 32-bit elements; how exact they have to be, the bound alone decides.
A program may use at most 320 MiB of HBM per device.

```python
import jax
import jax.numpy as jnp
from jax import lax

C = 640
MAP = 16
IMG_DEV = 1
IMAGES = 8


def draw_groups(key, part):
    key = jax.random.fold_in(key, 5)
    first_key, second_key = jax.random.split(key)
    coins = jax.random.randint(first_key, (IMAGES,), 0, 2)
    chosen = jax.random.randint(second_key, (IMAGES // IMG_DEV,), 0, IMG_DEV)
    places = jnp.arange(IMAGES, dtype=jnp.int32)
    forced = places % IMG_DEV == jnp.repeat(chosen, IMG_DEV)
    return jnp.where(forced, 1, coins).astype(jnp.int32)


def block_levels(key, dims, cuts, least, high):
    factor_of = 1.0
    for axis_at, shards_of in cuts:
        draws = jax.random.uniform(jax.random.fold_in(jax.random.fold_in(key, 6), axis_at), (shards_of,), jnp.float32, least / len(cuts), high / len(cuts))
        factor_of = factor_of * jnp.repeat(jnp.exp(draws), dims[axis_at] // shards_of).reshape((-1,) + (1,) * (len(dims) - 1 - axis_at))
    return factor_of


def centred(key, shape, scale, most, cuts=(), kind=jnp.bfloat16):
    result = jax.random.normal(key, shape, jnp.float32) * scale
    if len(cuts) > 0:
        result = block_levels(key, shape, cuts, -0.22, 0.18) * result
    return jnp.clip(result, min=-most, max=most).astype(kind)


def setup_inputs(seed: int = 0) -> dict:
    splits = jax.random.split(jax.random.key(seed), 10)
    image_rows = centred(splits[0], (IMAGES, MAP, MAP, C), 1.0, 6.0, ((0, 8), (1, 4)), jnp.float32)
    groups = draw_groups(jax.random.fold_in(splits[9], 71), 0)
    conv_first = centred(splits[2], (3, 3, C, C), (9 * C) ** -0.5, 0.078125, ((2, 4),), jnp.float32)
    conv_second = centred(splits[3], (3, 3, C, C), (9 * C) ** -0.5, 0.078125, ((2, 4),), jnp.float32)
    gain_first = jnp.clip(1.0 + 0.15 * jax.random.normal(splits[4], (C,), jnp.float32), 0.25, 1.75)
    shift_first = centred(splits[5], (C,), 0.5, 3.0, ((0, 4),), jnp.float32)
    gain_second = jnp.clip(1.0 + 0.15 * jax.random.normal(splits[6], (C,), jnp.float32), 0.25, 1.75)
    shift_second = centred(splits[7], (C,), 0.5, 3.0, ((0, 4),), jnp.float32)
    cotangent = centred(splits[8], (IMAGES, MAP, MAP, C), 1.0, 6.0, ((0, 8), (3, 4)), jnp.float32)
    return dict(image_rows=image_rows, groups=groups, conv_first=conv_first, conv_second=conv_second, gain_first=gain_first, shift_first=shift_first, gain_second=gain_second, shift_second=shift_second, cotangent=cotangent)


@jax.custom_vjp
def low(v):
    return lax.optimization_barrier(v.astype(jnp.bfloat16)).astype(jnp.float32)

@jax.custom_vjp
def low_back(v):
    return v

def low_keep(v):
    return (low(v), None)

def low_pass(kept, grad):
    return (grad,)

def back_keep(v):
    return (v, None)

def back_low(kept, grad):
    return (low(grad),)
low.defvjp(low_keep, low_pass)
low_back.defvjp(back_keep, back_low)
epsilon = 1e-05
sam_radius = 0.05
norm_floor = 1e-06

def valid_pixels(groups, extent_full):
    places = jnp.arange(extent_full, dtype=jnp.int32)
    extent = jnp.where(groups == 1, extent_full, extent_full // 2).astype(jnp.int32)
    inside = places[None, :] < extent[:, None]
    return (inside[:, :, None] & inside[:, None, :]).astype(jnp.float32)[..., None]

def convolve(values, kernel):
    return lax.conv_general_dilated(values, kernel, (1, 1), 'SAME', dimension_numbers=('NHWC', 'HWIO', 'NHWC'), precision=lax.Precision.HIGHEST)

def normalize(values, validity, pixels, gain, shift, frozen):
    if frozen is None:
        center = lax.optimization_barrier(jnp.sum(values * validity, axis=(0, 1, 2))) / pixels
        spread = lax.optimization_barrier(jnp.sum(validity * (values - center) ** 2, axis=(0, 1, 2))) / pixels
    else:
        center, spread = frozen
    scaled = (values - center) * lax.rsqrt(spread + epsilon)
    return (jax.nn.silu(scaled * gain + shift) * validity, (center, spread))

def forward(inputs, params, validity, pixels, frozen):
    kernel_one, kernel_two, gain_one, shift_one, gain_two, shift_two = params
    act_one, stats_one = normalize(inputs, validity, pixels, gain_one, shift_one, frozen[0])
    inner = convolve(act_one, kernel_one) * validity
    act_two, stats_two = normalize(inner, validity, pixels, gain_two, shift_two, frozen[1])
    output = inputs * validity + convolve(act_two, kernel_two) * validity
    return (output, (stats_one, stats_two))

def reference(image_rows, groups, conv_first, conv_second, gain_first, shift_first, gain_second, shift_second, cotangent):
    validity = valid_pixels(groups, MAP)
    pixels = jnp.sum(validity)
    params = (conv_first, conv_second, gain_first, shift_first, gain_second, shift_second)

    def ascent_fn(weights):
        return forward(image_rows, weights, validity, pixels, (None, None))
    block_out, pull, frozen = jax.vjp(ascent_fn, params, has_aux=True)
    ascent = pull(cotangent)[0]
    squares = jnp.float32(0.0)
    for gradient in ascent:
        squares = squares + jnp.sum(gradient * gradient)
    grad_norm = jnp.sqrt(squares)
    factor = sam_radius * lax.rsqrt(squares + norm_floor)
    moved = tuple((weight_value + factor * gradient for weight_value, gradient in zip(params, ascent)))

    def perturbed_fn(inputs, weights):
        return forward(inputs, weights, validity, pixels, frozen)[0]
    shown_out, pull_again = jax.vjp(perturbed_fn, image_rows, moved)
    input_grad, grads = pull_again(cotangent)
    return (block_out, input_grad, grads[0], grads[1], grads[2], grads[3], grads[4], grads[5], grad_norm)
```

```python
import functools

import jax
import jax.numpy as jnp
from jax import lax
from jax.experimental import pallas as pl
from jax.experimental.pallas import tpu as pltpu
from jax.sharding import PartitionSpec as P

epsilon = 1e-05
sam_radius = 0.05
norm_floor = 1e-06
MESH = pl.DeviceIdType.MESH
F32, BF16 = jnp.float32, jnp.bfloat16
VMEM = pltpu.VMEM
DMA = pltpu.SemaphoreType.DMA
LIMIT = 60 << 20


class Plan:
    def __init__(self, nd, nc, channels, side):
        self.nd, self.nc, self.ch, self.side = nd, nc, channels, side
        self.cb, self.db, self.px = channels // nc, channels // nd, side * side
        self.ny = 2
        self.nz = nd // 2
        self.offs = tuple((r, s) for r in (-1, 0, 1) for s in (-1, 0, 1))


def split(v):
    hi = v.astype(BF16)
    return hi, (v - hi.astype(F32)).astype(BF16)


def dot(a, b):
    return lax.dot_general(a, b, (((1,), (0,)), ((), ())), preferred_element_type=F32)


def dot_nt(a, b):
    return lax.dot_general(a, b, (((1,), (1,)), ((), ())), preferred_element_type=F32)


def edge_masks(side, px):
    lane = lax.broadcasted_iota(jnp.int32, (1, px), 1)
    col = lax.rem(lane, side)
    row = lax.div(lane, side)
    one = jnp.ones((1, px), F32)
    zero = jnp.zeros((1, px), F32)
    rows = {-1: jnp.where(row >= 1, one, zero), 0: None, 1: jnp.where(row < side - 1, one, zero)}
    cols = {-1: jnp.where(col >= 1, one, zero), 0: None, 1: jnp.where(col < side - 1, one, zero)}
    return rows, cols


def moved(v, lanes, mask):
    if lanes:
        v = pltpu.roll(v, (-lanes) % v.shape[1], axis=1)
    return v if mask is None else v * mask


def shifts(v, side, sign=1):
    rows, cols = edge_masks(side, v.shape[1])
    by_col = {s: moved(v, s, cols[s]) for s in (-1, 0, 1)}
    return [moved(by_col[sign * s], sign * r * side, rows[sign * r]) for r in (-1, 0, 1) for s in (-1, 0, 1)]


def gather_taps(prod, side, n):
    rows, cols = edge_masks(side, prod.shape[1])
    total = None
    for j, s in enumerate((-1, 0, 1)):
        part = None
        for i, r in enumerate((-1, 0, 1)):
            t = 3 * i + j
            m = moved(prod[t * n : (t + 1) * n], r * side, rows[r])
            part = m if part is None else part + m
        m = moved(part, s, cols[s])
        total = m if total is None else total + m
    return total


def sigmoid(t):
    return 1.0 / (1.0 + jnp.exp(-t))


def slope(pre):
    s = sigmoid(pre)
    return s * (1.0 + pre * (1.0 - s))


def lanes_sum(v):
    return jnp.sum(v, axis=1, keepdims=True)


def valid_map(flag, side, px):
    lane = lax.broadcasted_iota(jnp.int32, (1, px), 1)
    half = (lax.rem(lane, side) < side // 2) & (lax.div(lane, side) < side // 2)
    return jnp.where(half, jnp.ones((1, px), F32), flag)


def to_row(col):
    n = col.shape[0]
    eye = lax.broadcasted_iota(jnp.int32, (n, n), 0) == lax.broadcasted_iota(jnp.int32, (n, n), 1)
    return jnp.sum(jnp.where(eye, col, 0.0), axis=0, keepdims=True)


def to_col(row):
    n = row.shape[1]
    eye = lax.broadcasted_iota(jnp.int32, (n, n), 0) == lax.broadcasted_iota(jnp.int32, (n, n), 1)
    return jnp.sum(jnp.where(eye, row, 0.0), axis=1, keepdims=True)


def pack_cols(cols, n):
    lane = lax.broadcasted_iota(jnp.int32, (n, 128), 1)
    out = jnp.zeros((n, 128), F32)
    for k, col in enumerate(cols):
        out = jnp.where(lane == k, col, out)
    return out


def send(src, dst, ss, rs, device):
    return pltpu.make_async_remote_copy(
        src_ref=src, dst_ref=dst, send_sem=ss, recv_sem=rs, device_id=device, device_id_type=MESH
    )


def here():
    return lax.axis_index("dp"), lax.axis_index("chan")


def greet(plan):
    d, c = here()
    barrier = pltpu.get_barrier_semaphore()
    for j in range(1, plan.nd):
        pl.semaphore_signal(barrier, inc=1, device_id=(lax.rem(d + j, plan.nd), c), device_id_type=MESH)
    for j in range(1, plan.nc):
        pl.semaphore_signal(barrier, inc=1, device_id=(d, lax.rem(c + j, plan.nc)), device_id_type=MESH)
    pl.semaphore_wait(barrier, plan.nd - 1 + plan.nc - 1)


class LineGather:
    def __init__(self, plan, buf, ss, rs):
        self.p, self.buf, self.ss, self.rs = plan, buf, ss, rs
        d, self.c = here()
        self.z, self.y = lax.div(d, plan.ny), lax.rem(d, plan.ny)

    def copy(self, kind, zs, z_to, y_to):
        slot = zs * self.p.ny + self.y
        return send(
            self.buf.at[slot], self.buf.at[slot], self.ss.at[kind, zs], self.rs.at[slot], (z_to * self.p.ny + y_to, self.c)
        )

    def others(self, zs, do):
        for j in range(1, self.p.ny):
            do(self.copy(1 + j, zs, self.z, lax.rem(self.y + j, self.p.ny)))

    def up(self, zs):
        return self.copy(0, zs, lax.min(self.z + 1, self.p.nz - 1), self.y)

    def down(self, zs):
        return self.copy(1, zs, lax.max(self.z - 1, 0), self.y)

    def got(self, slot):
        partner = lax.rem(self.y + 1, self.p.ny)
        send(self.buf.at[slot], self.buf.at[slot], self.ss.at[0, 0], self.rs.at[slot], (self.z * self.p.ny + partner, self.c)).wait_recv()

    def start(self):
        pl.when(self.z < self.p.nz - 1)(lambda: self.up(self.z).start())
        pl.when(self.z > 0)(lambda: self.down(self.z).start())
        self.others(self.z, lambda cp: cp.start())

    def step(self, s):
        z, nz = self.z, self.p.nz

        @pl.when(z - s >= 0)
        def _():
            zs = z - s
            self.got(zs * self.p.ny + self.y)
            pl.when(z < nz - 1)(lambda: self.up(zs).start())
            self.others(zs, lambda cp: cp.start())

        @pl.when(z + s <= nz - 1)
        def _():
            zs = z + s
            self.got(zs * self.p.ny + self.y)
            pl.when(z > 0)(lambda: self.down(zs).start())
            self.others(zs, lambda cp: cp.start())

    def finish(self):
        z, nz = self.z, self.p.nz
        for zs in range(nz):
            for j in range(1, self.p.ny):
                self.got(zs * self.p.ny + lax.rem(self.y + j, self.p.ny))
        for zs in range(nz):
            self.others(zs, lambda cp: cp.wait_send())
            pl.when((zs <= z) & (z < nz - 1))(lambda: self.up(zs).wait_send())
            pl.when((zs >= z) & (z > 0))(lambda: self.down(zs).wait_send())


def gather_kernel(p, x_ref, cot_ref, k2_ref, par_ref, flag_ref, x_out, c_out, a2_out, par_out, flag_out,
                  xs, rx, ks, sx, rxs, sk, rk, sp, rp, sf, rf, s1, r1, s2, r2):
    d, c = here()
    rows = x_ref.shape[0]
    greet(p)
    owner = lax.div(d * p.db, p.cb)
    inner = pl.multiple_of(lax.rem(d * p.db, p.cb), 8)

    for j in range(p.nc):
        xs[j] = x_ref[:, j * p.cb : (j + 1) * p.cb]
    a2a = []
    for j in range(1, p.nc):
        to = lax.rem(c + j, p.nc)
        a2a.append(send(xs.at[to], rx.at[c], sx.at[j], rxs.at[c], (d, to)))
    for cp in a2a:
        cp.start()
    rx[c] = xs[c]

    par_out[c] = par_ref[...]
    flag_out[d] = flag_ref[...]
    small = []
    for j in range(1, p.nc):
        small.append(send(par_ref, par_out.at[c], sp.at[j], rp.at[c], (d, lax.rem(c + j, p.nc))))
    for j in range(1, p.nd):
        small.append(send(flag_ref, flag_out.at[d], sf.at[j], rf.at[d], (lax.rem(d + j, p.nd), c)))
    for cp in small:
        cp.start()

    c_out[d] = cot_ref[...].T
    cots = LineGather(p, c_out, s2, r2)

    for j in range(1, p.nc):
        a2a[j - 1].wait_send()
        other = lax.rem(c + j, p.nc)
        send(xs.at[other], rx.at[other], sx.at[j], rxs.at[other], (d, other)).wait_recv()
    x_out[d] = rx[...].reshape(p.nc * rows, p.cb).T
    ins = LineGather(p, x_out, s1, r1)
    ins.start()
    cots.start()

    @pl.when(c == owner)
    def _():
        for j in range(p.nc):
            ks[j] = k2_ref[:, pl.ds(inner, p.db), j * p.cb : (j + 1) * p.cb].reshape(9 * p.db, p.cb)
        a2_out[...] = ks[c]
        for j in range(1, p.nc):
            to = lax.rem(c + j, p.nc)
            send(ks.at[to], a2_out, sk.at[j], rk, (d, to)).start()

    for s in range(1, p.nz):
        ins.step(s)
    for s in range(1, p.nz):
        cots.step(s)
    ins.finish()
    cots.finish()

    @pl.when(c == owner)
    def _():
        for j in range(1, p.nc):
            to = lax.rem(c + j, p.nc)
            send(ks.at[to], a2_out, sk.at[j], rk, (d, to)).wait_send()

    @pl.when(c != owner)
    def _():
        send(ks.at[0], a2_out, sk.at[0], rk, (d, owner)).wait_recv()

    for cp in small:
        cp.wait_send()
    for j in range(1, p.nc):
        other = lax.rem(c + j, p.nc)
        send(par_ref, par_out.at[other], sp.at[0], rp.at[other], (d, other)).wait_recv()
    for j in range(1, p.nd):
        other = lax.rem(d + j, p.nd)
        send(flag_ref, flag_out.at[other], sf.at[0], rf.at[other], (other, c)).wait_recv()


def gather(p, x, cot, k2, par, flag):
    rows = x.shape[0]
    out = lambda *s: jax.ShapeDtypeStruct(s, F32)
    return pl.pallas_call(
        functools.partial(gather_kernel, p),
        out_shape=(
            out(p.nd, p.cb, p.px), out(p.nd, p.cb, p.px), out(9 * p.db, p.cb), out(p.nc, 8, p.cb), out(p.nd, 8, p.px),
        ),
        in_specs=[pl.BlockSpec(memory_space=VMEM)] * 5,
        out_specs=tuple([pl.BlockSpec(memory_space=VMEM)] * 5),
        scratch_shapes=[
            VMEM((p.nc, rows, p.cb), F32), VMEM((p.nc, rows, p.cb), F32), VMEM((p.nc, 9 * p.db, p.cb), F32),
            DMA((p.nc,)), DMA((p.nc,)), DMA((p.nc,)), DMA, DMA((p.nc,)), DMA((p.nc,)), DMA((p.nd,)), DMA((p.nd,)),
            DMA((1 + p.ny, p.nz)), DMA((p.nd,)), DMA((1 + p.ny, p.nz)), DMA((p.nd,)),
        ],
        compiler_params=pltpu.CompilerParams(collective_id=0, has_side_effects=True, vmem_limit_bytes=LIMIT),
    )(x, cot, k2, par, flag)


def masked_stats(ref, flag_ref, p, n):
    zero = jnp.zeros((n, 1), F32)

    def first(i, carry):
        total, pixels = carry
        val = valid_map(flag_ref[i, :1], p.side, p.px)
        return total + lanes_sum(ref[i] * val), pixels + lanes_sum(val)

    total, pixels = lax.fori_loop(0, p.nd, first, (zero, jnp.zeros((1, 1), F32)))
    center = total / pixels

    def second(i, carry):
        val = valid_map(flag_ref[i, :1], p.side, p.px)
        off = ref[i] - center
        return carry + lanes_sum(val * off * off)

    spread = lax.fori_loop(0, p.nd, second, zero) / pixels
    return center, lax.rsqrt(spread + epsilon), pixels


def project_kernel(p, take_stats, x_ref, c_ref, a1_ref, a2_ref, par_ref, flag_ref, sums_out, *rest):
    if take_stats:
        stat_out, rest = rest[0], rest[1:]
    a_cat, part, buf1, half, buf2, s1, r1, s2, r2, s3, r3 = rest
    d, c = here()
    k = lax.rem(c, 2)
    across = (d, c + 1 - 2 * k)
    far = (d, lax.rem(c + 2, 4))
    hb = p.db // 2
    mine = pl.multiple_of(k * hb, 8)
    greet(p)

    hi, lo = split(a1_ref[...])
    a_cat[0] = jnp.concatenate([hi, hi, lo], axis=1)
    for t in range(9):
        hi, lo = split(a2_ref[(8 - t) * p.db : (9 - t) * p.db])
        a_cat[1, t * p.db : (t + 1) * p.db] = jnp.concatenate([hi, hi, lo], axis=1)

    if take_stats:
        center, rscale, _ = masked_stats(x_ref, flag_ref, p, p.cb)
        stat_out[...] = pack_cols([center, rscale], p.cb)
        gain, shift = par_ref[:, 0:1], par_ref[:, 1:2]
    else:
        center, rscale, gain, shift = (par_ref[:, j : j + 1] for j in range(4))

    n = 2 * p.nd

    def produce(i):
        @pl.when(i < p.nd)
        def _():
            val = valid_map(flag_ref[i, :1], p.side, p.px)
            pre = (x_ref[i] - center) * rscale * gain + shift
            act = pre * sigmoid(pre) * val
            ah, al = split(act)
            prod = dot(a_cat[0], jnp.concatenate([ah, al, ah], axis=0))
            part[i] = gather_taps(prod, p.side, p.db) * val

        @pl.when(i >= p.nd)
        def _():
            img = lax.max(i - p.nd, 0)
            val = valid_map(flag_ref[img, :1], p.side, p.px)
            ah, al = split(c_ref[img] * val)
            prod = dot(a_cat[1], jnp.concatenate([ah, al, ah], axis=0))
            part[i] = gather_taps(prod, p.side, p.db) * val

        send(part.at[i], buf1.at[i], s1.at[i], r1.at[i], across).start()

    def reduce_chip(i):
        send(part.at[i], buf1.at[i], s1.at[i], r1.at[i], across).wait()
        half[i] = part[i, pl.ds(mine, hb)] + buf1[i, pl.ds(mine, hb)]
        send(half.at[i], buf2.at[i], s2.at[i], r2.at[i], far).start()

    def reduce_far(i):
        send(half.at[i], buf2.at[i], s2.at[i], r2.at[i], far).wait()
        rows = sums_out.at[i, pl.ds(mine, hb)]
        rows[...] = half[i] + buf2[i]
        send(rows, rows, s3.at[i], r3.at[i], across).start()

    def done(i):
        rows = sums_out.at[i, pl.ds(mine, hb)]
        cp = send(rows, sums_out.at[i, pl.ds(pl.multiple_of(hb - mine, 8), hb)], s3.at[i], r3.at[i], across)
        cp.wait()

    def body(i, _):
        pl.when(i < n)(lambda: produce(lax.min(i, n - 1)))
        pl.when((i >= 1) & (i < n + 1))(lambda: reduce_chip(lax.clamp(0, i - 1, n - 1)))
        pl.when((i >= 3) & (i < n + 3))(lambda: reduce_far(lax.clamp(0, i - 3, n - 1)))
        pl.when(i >= 4)(lambda: done(lax.clamp(0, i - 4, n - 1)))
        return 0

    lax.fori_loop(0, n + 4, body, 0)


def project(p, take_stats, collective, x, cot, a1, a2, par, flags):
    n = 2 * p.nd
    out = lambda *s: jax.ShapeDtypeStruct(s, F32)
    shapes = (out(n, p.db, p.px),) + ((out(p.cb, 128),) if take_stats else ())
    return pl.pallas_call(
        functools.partial(project_kernel, p, take_stats),
        out_shape=shapes,
        in_specs=[pl.BlockSpec(memory_space=VMEM)] * 6,
        out_specs=tuple([pl.BlockSpec(memory_space=VMEM)] * len(shapes)),
        scratch_shapes=[
            VMEM((2, 9 * p.db, 3 * p.cb), BF16),
            VMEM((n, p.db, p.px), F32), VMEM((n, p.db, p.px), F32),
            VMEM((n, p.db // 2, p.px), F32), VMEM((n, p.db // 2, p.px), F32),
        ] + [DMA((n,))] * 6,
        compiler_params=pltpu.CompilerParams(collective_id=collective, has_side_effects=True, vmem_limit_bytes=LIMIT),
    )(x, cot, a1, a2, par, flags)


def scatter_images(p, part, buf, ss, rs, order):
    d, c = here()
    return send(part.at[order], buf.at[d], ss.at[order], rs.at[d], (order, c))


def collect_images(p, part, buf, ss, rs):
    d, c = here()
    total = part[d]
    for j in range(1, p.nd):
        other = lax.rem(d + j, p.nd)
        send(part.at[other], buf.at[other], ss.at[other], rs.at[other], (other, c)).wait()
        total = total + buf[other]
    return total


def ascent_kernel(p, inner_ref, x_ref, c_ref, a1_ref, a2_ref, par1_ref, par2_ref, flag_ref,
                  out_ref, a1_out, a2_out, par1_out, par2_out, norm_out,
                  colh, coll, bm, part, buf, g1, g2, dpre_s, msg, rmsg, msg2, rmsg2, ss, rs, sm, rm, sm2, rm2):
    d, c = here()
    greet(p)
    cb, db, px, side = p.cb, p.db, p.px, p.side
    nd = p.nd
    center1, rs1, gain1, shift1 = (par1_ref[:, j : j + 1] for j in range(4))
    gain2, shift2 = par2_ref[:, 0:1], par2_ref[:, 1:2]
    center2, rs2, pixels = masked_stats(inner_ref.at[pl.ds(0, nd)], flag_ref, p, db)

    def val_of(i):
        return valid_map(flag_ref[i, :1], side, px)

    def dense(ref):
        hi, lo = split(ref[...].T)
        bm[0], bm[1] = hi, lo

    def set_cols(maps):
        for t, m in enumerate(maps):
            hi, lo = split(m)
            colh[t * db : (t + 1) * db] = hi
            coll[t * db : (t + 1) * db] = lo

    def im2col_dot():
        return dot(bm[0], colh[...]) + dot(bm[0], coll[...]) + dot(bm[1], colh[...])

    def wgrad(other):
        oh, ol = split(other)
        left = jnp.concatenate([colh[...], colh[...], coll[...]], axis=1)
        return dot_nt(left, jnp.concatenate([oh, ol, oh], axis=1))

    dense(a2_ref)
    g2[...] = jnp.zeros_like(g2)
    zero = jnp.zeros((db, 1), F32)

    def forward(j, carry):
        i = lax.rem(d + 1 + j, nd)
        val = val_of(i)
        scaled = (inner_ref[i] - center2) * rs2
        pre = scaled * gain2 + shift2
        sg = sigmoid(pre)
        act = pre * sg * val
        dpre = inner_ref[nd + i] * val * (sg * (1.0 + pre * (1.0 - sg)))
        dpre_s[i] = dpre
        set_cols(shifts(act, side))
        part[i] = im2col_dot()
        pl.when(i != d)(lambda: scatter_images(p, part, buf, ss, rs, i).start())
        g2[...] += wgrad(c_ref[i] * val)
        return carry[0] + lanes_sum(dpre), carry[1] + lanes_sum(dpre * scaled)

    sh2, gg2 = lax.fori_loop(0, nd, forward, (zero, zero))

    dense(a1_ref)
    g1[...] = jnp.zeros_like(g1)
    zero = jnp.zeros((cb, 1), F32)

    def backward(i, carry):
        val = val_of(i)
        scaled = (inner_ref[i] - center2) * rs2
        dinner = gain2 * rs2 * (dpre_s[i] - val * (sh2 + scaled * gg2) / pixels)
        set_cols(shifts(dinner, side, -1))
        scaled1 = (x_ref[i] - center1) * rs1
        pre1 = scaled1 * gain1 + shift1
        sg = sigmoid(pre1)
        g1[...] += wgrad(pre1 * sg * val)
        dpre1 = im2col_dot() * val * (sg * (1.0 + pre1 * (1.0 - sg)))
        return carry[0] + lanes_sum(dpre1), carry[1] + lanes_sum(dpre1 * scaled1)

    sh1, gg1 = lax.fori_loop(0, nd, backward, (zero, zero))

    sq = jnp.sum(g1[...] * g1[...] + g2[...] * g2[...], keepdims=True)
    small2 = jnp.sum(sh2 * sh2 + gg2 * gg2, keepdims=True)
    sq = sq + jnp.where(c == 0, small2, 0.0)
    row = lax.broadcasted_iota(jnp.int32, (8, cb), 0)
    msg[...] = jnp.where(row == 0, to_row(sh1), jnp.where(row == 1, to_row(gg1), sq))
    copies = [send(msg, rmsg.at[d], sm.at[j], rm.at[d], (lax.rem(d + j, nd), c)) for j in range(1, nd)]
    for cp in copies:
        cp.start()
    total = msg[...]
    for j in range(1, nd):
        other = lax.rem(d + j, nd)
        send(msg, rmsg.at[other], sm.at[0], rm.at[other], (other, c)).wait_recv()
    rmsg[d] = msg[...]
    total = rmsg[0]
    for j in range(1, nd):
        total = total + rmsg[j]
    sh1, gg1 = to_col(total[0:1]), to_col(total[1:2])
    sq = total[2:3, 0:1] + jnp.sum(sh1 * sh1 + gg1 * gg1, keepdims=True)
    msg2[...] = jnp.broadcast_to(sq, (8, 128))
    copies2 = [send(msg2, rmsg2.at[c], sm2.at[j], rm2.at[c], (d, lax.rem(c + j, p.nc))) for j in range(1, p.nc)]
    for cp in copies2:
        cp.start()
    for j in range(1, p.nc):
        other = lax.rem(c + j, p.nc)
        send(msg2, rmsg2.at[other], sm2.at[0], rm2.at[other], (d, other)).wait_recv()
    rmsg2[c] = msg2[...]
    sq = rmsg2[0]
    for j in range(1, p.nc):
        sq = sq + rmsg2[j]
    norm_out[...] = jnp.sqrt(sq)
    factor = (sam_radius * lax.rsqrt(sq + norm_floor))[0:1, 0:1]

    a1_out[...] = a1_ref[...] + factor * g1[...]
    a2_out[...] = a2_ref[...] + factor * g2[...]
    par1_out[...] = pack_cols([center1, rs1, gain1 + factor * gg1, shift1 + factor * sh1], cb)
    par2_out[...] = pack_cols([center2, rs2, gain2 + factor * gg2, shift2 + factor * sh2], db)

    total = collect_images(p, part, buf, ss, rs)
    val = val_of(d)
    out_ref[...] = ((x_ref[d] + total) * val).T
    for cp in copies + copies2:
        cp.wait_send()


def ascent(p, inner, x, cot, a1, a2, par1, par2, flags):
    out = lambda *s: jax.ShapeDtypeStruct(s, F32)
    nd, cb, db, px = p.nd, p.cb, p.db, p.px
    return pl.pallas_call(
        functools.partial(ascent_kernel, p),
        out_shape=(out(px, cb), out(9 * db, cb), out(9 * db, cb), out(cb, 128), out(db, 128), out(8, 128)),
        in_specs=[pl.BlockSpec(memory_space=VMEM)] * 8,
        out_specs=tuple([pl.BlockSpec(memory_space=VMEM)] * 6),
        scratch_shapes=[
            VMEM((9 * db, px), BF16), VMEM((9 * db, px), BF16), VMEM((2, cb, 9 * db), BF16),
            VMEM((nd, cb, px), F32), VMEM((nd, cb, px), F32), VMEM((9 * db, cb), F32), VMEM((9 * db, cb), F32),
            VMEM((nd, db, px), F32), VMEM((8, cb), F32), VMEM((nd, 8, cb), F32), VMEM((8, 128), F32), VMEM((p.nc, 8, 128), F32),
            DMA((nd,)), DMA((nd,)), DMA((nd,)), DMA((nd,)), DMA((p.nc,)), DMA((p.nc,)),
        ],
        compiler_params=pltpu.CompilerParams(collective_id=2, has_side_effects=True, vmem_limit_bytes=LIMIT),
    )(inner, x, cot, a1, a2, par1, par2, flags)


def perturbed_kernel(p, inner_ref, x_ref, c_ref, a1_ref, par1_ref, par2_ref, flag_ref,
                     in_out, g1_out, g2_out, vec_out,
                     colh, coll, bm, part, buf, dall, call, act2, lefth, right, xs, rx, msg, rmsg,
                     ss, rs, sg_, rg_, sc_, rc_, sb, rb, sx, rxs, sm, rm, dsem, stage):
    d, c = here()
    greet(p)
    cb, db, px, side, nd, nc = p.cb, p.db, p.px, p.side, p.nd, p.nc
    z, y = lax.div(d, p.ny), lax.rem(d, p.ny)
    k = lax.rem(c, 2)
    center1, rs1, gain1, shift1 = (par1_ref[:, j : j + 1] for j in range(4))
    center2, rs2, gain2, shift2 = (par2_ref[:, j : j + 1] for j in range(4))

    def val_of(i):
        return valid_map(flag_ref[i, :1], side, px)

    def masked(i, _):
        call[c, i] = c_ref[i] * val_of(i)
        return 0

    lax.fori_loop(0, nd, masked, 0)
    far, across = lax.rem(c + 2, 4), c + 1 - 2 * k
    cot_far = send(call.at[c], call.at[c], sc_.at[0], rc_.at[c], (d, far))
    cot_across = send(call.at[c], call.at[c], sc_.at[1], rc_.at[c], (d, across))
    cot_far.start()
    cot_across.start()

    zero = jnp.zeros((db, 1), F32)

    def inner_grad(i, carry):
        val = val_of(i)
        scaled = (inner_ref[i] - center2) * rs2
        pre = scaled * gain2 + shift2
        sg = sigmoid(pre)

        @pl.when(z == c)
        def _():
            act2[y, i] = pre * sg * val

        dpre = inner_ref[nd + i] * val * (sg * (1.0 + pre * (1.0 - sg)))
        dall[d, i] = gain2 * rs2 * dpre
        return carry[0] + lanes_sum(dpre), carry[1] + lanes_sum(dpre * scaled)

    sh2, gg2 = lax.fori_loop(0, nd, inner_grad, (zero, zero))
    grads = LineGather(p, dall, sg_, rg_)
    grads.start()

    def act_copy(kind, ys, z_to, y_to):
        return send(act2.at[ys], act2.at[ys], sb.at[kind], rb.at[ys], (z_to * p.ny + y_to, c))

    up = lambda: act_copy(0, y, lax.min(z + 1, p.nz - 1), y)
    down = lambda: act_copy(1, y, lax.max(z - 1, 0), y)
    side_copy = lambda: act_copy(2, y, z, 1 - y)

    def act_hand_on():
        pl.when((z >= c) & (z < p.nz - 1))(lambda: up().start())
        pl.when((z <= c) & (z > 0))(lambda: down().start())
        side_copy().start()

    pl.when(z == c)(act_hand_on)

    hi, lo = split(a1_ref[...].T)
    bm[0], bm[1] = hi, lo

    def backward(j, _):
        i = lax.rem(d + 1 + j, nd)
        for t, m in enumerate(shifts(dall[d, i], side, -1)):
            hi, lo = split(m)
            colh[t * db : (t + 1) * db] = hi
            coll[t * db : (t + 1) * db] = lo
        part[i] = dot(bm[0], colh[...]) + dot(bm[0], coll[...]) + dot(bm[1], colh[...])
        pl.when(i != d)(lambda: scatter_images(p, part, buf, ss, rs, i).start())
        return 0

    lax.fori_loop(0, nd, backward, 0)

    def norm_sums(i, carry):
        val = val_of(i)
        scaled = (x_ref[i] - center1) * rs1
        dpre = part[i] * val * slope(scaled * gain1 + shift1)
        return carry[0] + lanes_sum(dpre), carry[1] + lanes_sum(dpre * scaled)

    zero = jnp.zeros((cb, 1), F32)
    sh1, gg1 = lax.fori_loop(0, nd, norm_sums, (zero, zero))

    row = lax.broadcasted_iota(jnp.int32, (8, cb), 0)
    pad = jnp.zeros((1, cb - db), F32)
    wide = lambda col: jnp.concatenate([to_row(col), pad], axis=1)
    msg[...] = jnp.where(row == 0, to_row(sh1), jnp.where(row == 1, to_row(gg1), jnp.where(row == 2, wide(sh2), wide(gg2))))
    copies = [send(msg, rmsg.at[d], sm.at[j], rm.at[d], (lax.rem(d + j, nd), c)) for j in range(1, nd)]
    for cp in copies:
        cp.start()

    pl.when(z != c)(lambda: (act_copy(0, y, z, 1 - y).wait_recv(), act_hand_on()) and None)
    for s in range(1, p.nz):
        grads.step(s)

    send(call.at[far], call.at[far], sc_.at[0], rc_.at[far], (d, far)).wait_recv()
    cot_relay = send(call.at[far], call.at[far], sc_.at[2], rc_.at[far], (d, across))
    cot_relay.start()

    total = collect_images(p, part, buf, ss, rs)
    val = val_of(d)
    pre = (x_ref[d] - center1) * rs1 * gain1 + shift1
    grad = (gain1 * rs1 * (total * val * slope(pre)) + c_ref[d] * val).T
    rows = px // nc
    for j in range(nc):
        xs[j] = grad[j * rows : (j + 1) * rows]
    a2a = []
    for j in range(1, nc):
        to = lax.rem(c + j, nc)
        a2a.append(send(xs.at[to], rx.at[c], sx.at[j], rxs.at[c], (d, to)))
    for cp in a2a:
        cp.start()
    rx[c] = xs[c]

    for j in range(1, nd):
        other = lax.rem(d + j, nd)
        send(msg, rmsg.at[other], sm.at[0], rm.at[other], (other, c)).wait_recv()
    rmsg[d] = msg[...]
    total = rmsg[0]
    for j in range(1, nd):
        total = total + rmsg[j]
    per = cb // db
    both = jnp.concatenate([rmsg[per * c + j][:, :db] for j in range(per)], axis=1)
    vec_out[...] = jnp.where(row < 2, total, both)

    def kernel_grad(left_of, right_of, out_hbm):
        stage[...] = jnp.zeros_like(stage)

        def body(i, _):
            for t, m in enumerate(shifts(left_of(i), side)):
                hi, lo = split(m)
                lefth[t * cb : (t + 1) * cb] = jnp.concatenate([hi, hi, lo], axis=1)
            for q in range(p.ch // right_of(i, 0).shape[0]):
                r = right_of(i, q)
                n = r.shape[0]
                hi, lo = split(r)
                right[q * n : (q + 1) * n] = jnp.concatenate([hi, lo, hi], axis=1)
            stage[...] += dot_nt(lefth[...], right[...])
            return 0

        lax.fori_loop(0, nd, body, 0)
        cp = pltpu.make_async_copy(stage, out_hbm, dsem)
        cp.start()
        cp.wait()

    def act_one(i):
        pre = (x_ref[i] - center1) * rs1 * gain1 + shift1
        return pre * sigmoid(pre) * val_of(i)

    grads.finish()
    kernel_grad(act_one, lambda i, q: dall[q, i], g1_out)

    act_copy(2, 1 - y, z, 1 - y).wait_recv()
    side_copy().wait_send()
    pl.when((z >= c) & (z < p.nz - 1))(lambda: up().wait_send())
    pl.when((z <= c) & (z > 0))(lambda: down().wait_send())
    cot_far.wait_send()
    cot_across.wait_send()
    cot_relay.wait_send()
    send(call.at[across], call.at[across], sc_.at[0], rc_.at[across], (d, across)).wait_recv()
    last = 3 - c - far - across + 3
    send(call.at[last], call.at[last], sc_.at[0], rc_.at[last], (d, across)).wait_recv()
    kernel_grad(lambda i: jnp.concatenate([act2[0, i], act2[1, i]], axis=0), lambda i, q: call[q, i], g2_out)

    for j in range(1, nc):
        a2a[j - 1].wait_send()
        other = lax.rem(c + j, nc)
        send(xs.at[other], rx.at[other], sx.at[0], rxs.at[other], (d, other)).wait_recv()
    for j in range(nc):
        in_out[:, j * cb : (j + 1) * cb] = rx[j]
    for cp in copies:
        cp.wait_send()


def perturbed(p, inner, x, cot, a1, par1, par2, flags):
    out = lambda *s: jax.ShapeDtypeStruct(s, F32)
    nd, nc, cb, db, px = p.nd, p.nc, p.cb, p.db, p.px
    rows = px // nc
    return pl.pallas_call(
        functools.partial(perturbed_kernel, p),
        out_shape=(out(rows, p.ch), out(9 * cb, p.ch), out(9 * cb, p.ch), out(8, cb)),
        in_specs=[pl.BlockSpec(memory_space=VMEM)] * 7,
        out_specs=(pl.BlockSpec(memory_space=VMEM), pl.BlockSpec(memory_space=pl.ANY), pl.BlockSpec(memory_space=pl.ANY),
                   pl.BlockSpec(memory_space=VMEM)),
        scratch_shapes=[
            VMEM((9 * db, px), BF16), VMEM((9 * db, px), BF16), VMEM((2, cb, 9 * db), BF16),
            VMEM((nd, cb, px), F32), VMEM((nd, cb, px), F32), VMEM((nd, nd, db, px), F32), VMEM((nc, nd, cb, px), F32),
            VMEM((p.ny, nd, db, px), F32), VMEM((9 * cb, 3 * px), BF16), VMEM((p.ch, 3 * px), BF16),
            VMEM((nc, rows, cb), F32), VMEM((nc, rows, cb), F32), VMEM((8, cb), F32), VMEM((nd, 8, cb), F32),
            DMA((nd,)), DMA((nd,)), DMA((1 + p.ny, p.nz)), DMA((nd,)), DMA((3,)), DMA((nc,)), DMA((3,)), DMA((p.ny,)),
            DMA((nc,)), DMA((nc,)), DMA((nd,)), DMA((nd,)), DMA, VMEM((9 * cb, p.ch), F32),
        ],
        compiler_params=pltpu.CompilerParams(collective_id=4, has_side_effects=True, vmem_limit_bytes=LIMIT),
    )(inner, x, cot, a1, par1, par2, flags)


def fused_on_device(p, image_rows, groups, conv_first, conv_second, gain_first, shift_first, gain_second, shift_second, cotangent):
    d, c = lax.axis_index("dp"), lax.axis_index("chan")
    cb, db, px, nc = p.cb, p.db, p.px, p.nc
    x = image_rows.reshape(px // nc, p.ch)
    cot = cotangent.reshape(px, cb)
    pad = jnp.zeros((6, cb), F32)
    par = jnp.concatenate([gain_second[None], shift_second[None], pad])
    flag = jnp.broadcast_to(jnp.where(groups == 1, 1.0, 0.0).astype(F32)[:, None], (8, px))
    xs, cs, a2, pars, flags = gather(p, x, cot, conv_second.reshape(9, cb, p.ch), par, flag)
    a1 = lax.dynamic_slice_in_dim(conv_first, d * db, db, 3).reshape(9, cb, db).transpose(0, 2, 1).reshape(9 * db, cb)
    par1 = jnp.pad(jnp.stack([gain_first, shift_first], axis=1), ((0, 0), (0, 126)))
    sums, stat1 = project(p, True, 1, xs, cs, a1, a2, par1, flags)
    par1 = jnp.pad(jnp.concatenate([stat1[:, :2], par1[:, :2]], axis=1), ((0, 0), (0, 124)))
    both = lax.dynamic_slice_in_dim(pars.transpose(1, 0, 2).reshape(8, p.ch)[:2], d * db, db, 1)
    par2 = jnp.pad(both.T, ((0, 0), (0, 126)))
    block_out, a1_new, a2_new, par1, par2, norm = ascent(p, sums, xs, cs, a1, a2, par1, par2, flags)
    (sums,) = project(p, False, 3, xs, cs, a1_new, a2_new, par1, flags)
    input_grad, g1, g2, vec = perturbed(p, sums, xs, cs, a1_new, par1, par2, flags)
    return (
        block_out.reshape(cotangent.shape), input_grad.reshape(image_rows.shape),
        g1.reshape(conv_first.shape), g2.reshape(conv_second.shape), vec[1], vec[0], vec[3], vec[2], norm[0, 0],
    )


def valid_pixels(groups, extent_full):
    places = jnp.arange(extent_full, dtype=jnp.int32)
    extent = jnp.where(groups == 1, extent_full, extent_full // 2).astype(jnp.int32)
    inside = places[None, :] < extent[:, None]
    return (inside[:, :, None] & inside[:, None, :]).astype(jnp.float32)[..., None]


def convolve(values, kernel):
    return lax.conv_general_dilated(
        values,
        kernel,
        (1, 1),
        "SAME",
        dimension_numbers=("NHWC", "HWIO", "NHWC"),
        precision=lax.Precision.HIGHEST,
    )


def silu_slope(preact):
    sigmoid = jax.nn.sigmoid(preact)
    return sigmoid * (1.0 + preact * (1.0 - sigmoid))


def batch_moments(values, validity):
    summed, squares, pixels = lax.psum(
        (
            jnp.sum(values * validity, axis=(0, 1, 2)),
            jnp.sum(validity * values * values, axis=(0, 1, 2)),
            jnp.sum(validity),
        ),
        "dp",
    )
    center = summed / pixels
    spread = squares / pixels - center * center
    return (center, lax.rsqrt(spread + epsilon), pixels)


def project_over_chan(values, kernel):
    return lax.psum_scatter(convolve(values, kernel), "chan", scatter_dimension=3, tiled=True)


def conv_backward(upstream, values, kernel):
    columns = lax.all_gather(upstream, "chan", axis=3, tiled=True)
    offset = jnp.int32(0)
    inputs_grad = jnp.zeros_like(values)
    kernel_grad = jnp.zeros_like(kernel)
    breadth = columns.shape[3]
    kernel_part = lax.dynamic_slice_in_dim(kernel, offset, breadth, 3)
    primal, pull = jax.vjp(convolve, values, kernel_part)
    values_part, kernel_part_grad = pull(columns)
    kernel_grad = lax.dynamic_update_slice_in_dim(kernel_grad, kernel_part_grad, offset, 3)
    return (inputs_grad + values_part, kernel_grad)


def batch_sums(dpre, scaled):
    return lax.psum((jnp.sum(dpre, axis=(0, 1, 2)), jnp.sum(dpre * scaled, axis=(0, 1, 2))), "dp")


def plain_on_device(
    image_rows,
    groups,
    conv_first,
    conv_second,
    gain_first,
    shift_first,
    gain_second,
    shift_second,
    cotangent,
):
    inputs = lax.all_to_all(image_rows, "chan", split_axis=3, concat_axis=1, tiled=True)
    validity = valid_pixels(groups, inputs.shape[1])
    cot_valid = cotangent * validity
    center_one, rscale_one, pixels = batch_moments(inputs, validity)
    scaled_one = (inputs - center_one) * rscale_one
    pre_one = scaled_one * gain_first + shift_first
    act_one = jax.nn.silu(pre_one) * validity
    inner = project_over_chan(act_one, conv_first) * validity
    center_two, rscale_two, pixels_again = batch_moments(inner, validity)
    scaled_two = (inner - center_two) * rscale_two
    pre_two = scaled_two * gain_second + shift_second
    act_two = jax.nn.silu(pre_two) * validity
    block_out = inputs * validity + project_over_chan(act_two, conv_second) * validity
    dact_two, kernel_two_part = conv_backward(cot_valid, act_two, conv_second)
    dpre_two = dact_two * validity * silu_slope(pre_two)
    shift_two_grad, gain_two_grad = batch_sums(dpre_two, scaled_two)
    dinner = (
        gain_second
        * rscale_two
        * (dpre_two - validity * (shift_two_grad + scaled_two * gain_two_grad) / pixels)
    )
    dact_one, kernel_one_part = conv_backward(dinner, act_one, conv_first)
    dpre_one = dact_one * validity * silu_slope(pre_one)
    shift_one_grad, gain_one_grad = batch_sums(dpre_one, scaled_one)
    small_squares = (
        jnp.sum(gain_one_grad**2)
        + jnp.sum(shift_one_grad**2)
        + jnp.sum(gain_two_grad**2)
        + jnp.sum(shift_two_grad**2)
    )
    kernel_one_sum, kernel_two_sum = lax.psum((kernel_one_part, kernel_two_part), "dp")
    local_sq = jnp.sum(kernel_one_sum**2) + jnp.sum(kernel_two_sum**2) + small_squares
    squares = lax.psum(local_sq, "chan")
    factor = sam_radius * lax.rsqrt(squares + norm_floor)
    kernel_one = conv_first + factor * kernel_one_sum
    kernel_two = conv_second + factor * kernel_two_sum
    grad_norm = jnp.sqrt(squares)
    moved_gain_one = gain_first + factor * gain_one_grad
    moved_shift_one = shift_first + factor * shift_one_grad
    moved_gain_two = gain_second + factor * gain_two_grad
    moved_shift_two = shift_second + factor * shift_two_grad
    pre_one_new = scaled_one * moved_gain_one + moved_shift_one
    act_one_new = jax.nn.silu(pre_one_new) * validity
    inner_new = project_over_chan(act_one_new, kernel_one) * validity
    scaled_two_new = (inner_new - center_two) * rscale_two
    pre_two_new = scaled_two_new * moved_gain_two + moved_shift_two
    act_two_new = jax.nn.silu(pre_two_new) * validity
    dact_two_new, kernel_two_grad = conv_backward(cot_valid, act_two_new, kernel_two)
    dpre_two_new = dact_two_new * validity * silu_slope(pre_two_new)
    gain_two_new_grad = jnp.sum(dpre_two_new * scaled_two_new, axis=(0, 1, 2))
    shift_two_new_grad = jnp.sum(dpre_two_new, axis=(0, 1, 2))
    dinner_new = moved_gain_two * rscale_two * dpre_two_new
    dact_one_new, kernel_one_grad = conv_backward(dinner_new, act_one_new, kernel_one)
    dpre_one_new = dact_one_new * validity * silu_slope(pre_one_new)
    gain_one_new_grad = jnp.sum(dpre_one_new * scaled_one, axis=(0, 1, 2))
    shift_one_new_grad = jnp.sum(dpre_one_new, axis=(0, 1, 2))
    inputs_grad = moved_gain_one * rscale_one * dpre_one_new + cot_valid
    input_grad = lax.all_to_all(inputs_grad, "chan", split_axis=1, concat_axis=3, tiled=True)
    (
        kernel_one_grad,
        kernel_two_grad,
        gain_one_new_grad,
        shift_one_new_grad,
        gain_two_new_grad,
        shift_two_new_grad,
    ) = lax.psum(
        (
            kernel_one_grad,
            kernel_two_grad,
            gain_one_new_grad,
            shift_one_new_grad,
            gain_two_new_grad,
            shift_two_new_grad,
        ),
        "dp",
    )
    return (
        block_out,
        input_grad,
        kernel_one_grad,
        kernel_two_grad,
        gain_one_new_grad,
        shift_one_new_grad,
        gain_two_new_grad,
        shift_two_new_grad,
        grad_norm,
    )


def solution(mesh):
    nd, nc = mesh.shape["dp"], mesh.shape["chan"]

    def on_device(image_rows, *rest):
        images, side, channels = image_rows.shape[0], image_rows.shape[2], image_rows.shape[3]
        fits = images == 1 and nc == 4 and nd == 2 * nc and channels // nd % 16 == 0 and side * side % 128 == 0
        if not fits:
            return plain_on_device(image_rows, *rest)
        return fused_on_device(Plan(nd, nc, channels, side), image_rows, *rest)

    return jax.shard_map(
        on_device,
        mesh=mesh,
        in_specs=(
            P("dp", "chan", None, None),
            P("dp"),
            P(None, None, "chan", None),
            P(None, None, "chan", None),
            P("chan"),
            P("chan"),
            P("chan"),
            P("chan"),
            P("dp", None, None, "chan"),
        ),
        out_specs=(
            P("dp", None, None, "chan"),
            P("dp", "chan", None, None),
            P(None, None, "chan", None),
            P(None, None, "chan", None),
            P("chan"),
            P("chan"),
            P("chan"),
            P("chan"),
            P(),
        ),
        check_vma=False,
    )
```

```python
import functools
import types

import jax
import jax.numpy as jnp
from jax import lax
from jax.experimental import pallas as pl
from jax.experimental.pallas import tpu as pltpu
from jax.sharding import PartitionSpec as P

epsilon = 1e-05
sam_radius = 0.05
norm_floor = 1e-06
MESH = pl.DeviceIdType.MESH
F32, BF16 = jnp.float32, jnp.bfloat16
VMEM, SMEM = pltpu.VMEM, pltpu.SMEM
DMA = pltpu.SemaphoreType.DMA
LIMIT = 60 << 20


class Plan:
    def __init__(self, nd, nc, channels, side):
        self.nd, self.nc, self.ch, self.side = nd, nc, channels, side
        self.cb, self.db, self.px = channels // nc, channels // nd, side * side
        self.ny = 2
        self.nz = nd // 2


def split(v):
    hi = v.astype(BF16)
    return hi, (v - hi.astype(F32)).astype(BF16)


def dot(a, b):
    return lax.dot_general(a, b, (((1,), (0,)), ((), ())), preferred_element_type=F32)


def dot_nt(a, b):
    return lax.dot_general(a, b, (((1,), (1,)), ((), ())), preferred_element_type=F32)


def edge_masks(side, px):
    lane = lax.broadcasted_iota(jnp.int32, (1, px), 1)
    col = lax.rem(lane, side)
    row = lax.div(lane, side)
    one = jnp.ones((1, px), F32)
    zero = jnp.zeros((1, px), F32)
    rows = {-1: jnp.where(row >= 1, one, zero), 0: None, 1: jnp.where(row < side - 1, one, zero)}
    cols = {-1: jnp.where(col >= 1, one, zero), 0: None, 1: jnp.where(col < side - 1, one, zero)}
    return rows, cols


def moved(v, lanes, mask):
    if lanes:
        v = pltpu.roll(v, (-lanes) % v.shape[1], axis=1)
    return v if mask is None else v * mask


def shifts(v, side, sign=1):
    rows, cols = edge_masks(side, v.shape[1])
    by_col = {s: moved(v, s, cols[s]) for s in (-1, 0, 1)}
    return [moved(by_col[sign * s], sign * r * side, rows[sign * r]) for r in (-1, 0, 1) for s in (-1, 0, 1)]


def gather_taps(prod, side, n):
    rows, cols = edge_masks(side, prod.shape[1])
    total = None
    for j, s in enumerate((-1, 0, 1)):
        part = None
        for i, r in enumerate((-1, 0, 1)):
            t = 3 * i + j
            m = moved(prod[t * n : (t + 1) * n], r * side, rows[r])
            part = m if part is None else part + m
        m = moved(part, s, cols[s])
        total = m if total is None else total + m
    return total


def sigmoid(t):
    return 1.0 / (1.0 + jnp.exp(-t))


def silu_and_slope(pre):
    s = sigmoid(pre)
    return pre * s, s * (1.0 + pre * (1.0 - s))


def lanes_sum(v):
    return jnp.sum(v, axis=1, keepdims=True)


def valid_map(flag, side, px):
    lane = lax.broadcasted_iota(jnp.int32, (1, px), 1)
    half = (lax.rem(lane, side) < side // 2) & (lax.div(lane, side) < side // 2)
    return jnp.where(half, jnp.ones((1, px), F32), flag)


def diagonal(n):
    return lax.broadcasted_iota(jnp.int32, (n, n), 0) == lax.broadcasted_iota(jnp.int32, (n, n), 1)


def to_row(col):
    return jnp.sum(jnp.where(diagonal(col.shape[0]), col, 0.0), axis=0, keepdims=True)


def to_col(row):
    return jnp.sum(jnp.where(diagonal(row.shape[1]), row, 0.0), axis=1, keepdims=True)


def stacked(rows, n):
    at = lax.broadcasted_iota(jnp.int32, (8, n), 0)
    out = jnp.zeros((8, n), F32)
    for k, row in enumerate(rows):
        out = jnp.where(at == k, row, out)
    return out


def send(src, dst, ss, rs, device):
    return pltpu.make_async_remote_copy(
        src_ref=src, dst_ref=dst, send_sem=ss, recv_sem=rs, device_id=device, device_id_type=MESH
    )


def here():
    return lax.axis_index("dp"), lax.axis_index("chan")


def greet(p):
    d, c = here()
    barrier = pltpu.get_barrier_semaphore()
    for j in range(1, p.nd):
        pl.semaphore_signal(barrier, inc=1, device_id=(lax.rem(d + j, p.nd), c), device_id_type=MESH)
    for j in range(1, p.nc):
        pl.semaphore_signal(barrier, inc=1, device_id=(d, lax.rem(c + j, p.nc)), device_id_type=MESH)
    pl.semaphore_wait(barrier, p.nd - 1 + p.nc - 1)


class ToAll:
    def __init__(self, axis, n, tile, slots, ss, rs):
        d, c = here()
        self.n, self.tile, self.slots, self.ss, self.rs = n, tile, slots, ss, rs
        self.me = d if axis == "dp" else c
        self.device = (lambda o: (o, c)) if axis == "dp" else (lambda o: (d, o))

    def start(self):
        self.slots[self.me] = self.tile[...]
        for j in range(1, self.n):
            to = lax.rem(self.me + j, self.n)
            send(self.tile, self.slots.at[self.me], self.ss.at[j], self.rs.at[self.me], self.device(to)).start()

    def finish(self):
        for j in range(1, self.n):
            other = lax.rem(self.me + j, self.n)
            send(self.tile, self.slots.at[other], self.ss.at[j], self.rs.at[other], self.device(other)).wait()

    def total(self):
        total = self.slots[0]
        for j in range(1, self.n):
            total = total + self.slots[j]
        return total


class Line:
    def __init__(self, p, view, ss, rs):
        self.p, self.view, self.ss, self.rs = p, view, ss, rs
        d, self.c = here()
        self.z, self.y = lax.div(d, p.ny), lax.rem(d, p.ny)

    def copy(self, zs, sem, z_to, y_to):
        slot = zs * self.p.ny + self.y
        return send(self.view(slot), self.view(slot), self.ss.at[sem, zs], self.rs.at[slot], (z_to * self.p.ny + y_to, self.c))

    def up(self, zs):
        return self.copy(zs, 0, lax.min(self.z + 1, self.p.nz - 1), self.y)

    def down(self, zs):
        return self.copy(zs, 1, lax.max(self.z - 1, 0), self.y)

    def side(self, zs):
        return self.copy(zs, 2, self.z, 1 - self.y)

    def got(self, zs, y):
        slot = zs * self.p.ny + y
        send(self.view(slot), self.view(slot), self.ss.at[0, 0], self.rs.at[slot], (self.z * self.p.ny + 1 - self.y, self.c)).wait_recv()

    def hand_on(self, zs):
        pl.when((zs <= self.z) & (self.z < self.p.nz - 1))(lambda: self.up(zs).start())
        pl.when((zs >= self.z) & (self.z > 0))(lambda: self.down(zs).start())
        self.side(zs).start()

    def drain(self):
        for zs in range(self.p.nz):
            pl.when((zs <= self.z) & (self.z < self.p.nz - 1))(lambda: self.up(zs).wait_send())
            pl.when((zs >= self.z) & (self.z > 0))(lambda: self.down(zs).wait_send())
            self.side(zs).wait_send()


def nearest(z, k):
    t = lax.div(z, 2)
    low = z + t * (3 - 2 * z)
    first = 1 - lax.min(lax.div(k, 2), 1)
    place = k + low * first * (1 - 2 * k)
    return place * (1 - 2 * t) + 3 * t


class ChanSum:
    def __init__(self, p, r):
        self.p, self.r = p, r
        d, c = here()
        k = lax.rem(c, 2)
        self.hb = p.db // 2
        self.across, self.far = (d, c + 1 - 2 * k), (d, lax.rem(c + 2, 4))
        self.mine = pl.multiple_of(k * self.hb, 8)
        self.yours = pl.multiple_of((1 - k) * self.hb, 8)

    def first(self, i):
        r = self.r
        return send(r.part.at[i], r.near.at[i], r.cs1.at[i], r.cr1.at[i], self.across)

    def second(self, i):
        r = self.r
        return send(r.half.at[i], r.away.at[i], r.cs2.at[i], r.cr2.at[i], self.far)

    def third(self, i, rows):
        r = self.r
        mine = r.sums.at[i, pl.ds(self.mine, self.hb)]
        return send(mine, r.sums.at[i, pl.ds(rows, self.hb)], r.cs3.at[i], r.cr3.at[i], self.across)

    def chip(self, i):
        r = self.r
        self.first(i).wait()
        r.half[i] = r.part[i, pl.ds(self.mine, self.hb)] + r.near[i, pl.ds(self.mine, self.hb)]
        self.second(i).start()

    def cross(self, i):
        r = self.r
        self.second(i).wait()
        r.sums[i, pl.ds(self.mine, self.hb)] = r.half[i] + r.away[i]
        self.third(i, self.mine).start()

    def done(self, i):
        self.third(i, self.yours).wait()

    def advance(self, j, n, item):
        at = lambda m: item(lax.clamp(0, m, n - 1))
        pl.when((j >= 1) & (j < n + 1))(lambda: self.chip(at(j - 1)))
        pl.when((j >= 3) & (j < n + 3))(lambda: self.cross(at(j - 3)))
        pl.when((j >= 4) & (j < n + 4))(lambda: self.done(at(j - 4)))


class ImageSum:
    def __init__(self, p, part, near, acc, away, s1, r1, s2, r2):
        self.p, self.part, self.buf1, self.acc, self.buf2 = p, part, near, acc, away
        self.s1, self.r1, self.s2, self.r2 = s1, r1, s2, r2
        d, self.c = here()
        self.z, self.y = lax.div(d, p.ny), lax.rem(d, p.ny)

    def near(self, zs):
        side = 1 - self.y
        return send(self.part.at[zs * self.p.ny + side], self.buf1.at[zs], self.s1.at[zs], self.r1.at[zs],
                    (self.z * self.p.ny + side, self.c))

    def away(self, zs, slot):
        return send(self.acc.at[zs], self.buf2.at[slot], self.s2.at[zs], self.r2.at[slot], (zs * self.p.ny + self.y, self.c))

    def spread(self):
        for j in range(1, self.p.nz + 1):
            zs = lax.rem(self.z + j, self.p.nz)
            self.near(zs).wait()
            self.acc[zs] = self.part[zs * self.p.ny + self.y] + self.buf1[zs]
            if j < self.p.nz:
                self.away(zs, self.z).start()

    def total(self):
        total = self.acc[self.z]
        for j in range(1, self.p.nz):
            other = lax.rem(self.z + j, self.p.nz)
            self.away(other, other).wait()
            total = total + self.buf2[other]
        return total


def scratch_of(p):
    nd, nc, cb, db, px, nz, ny = p.nd, p.nc, p.cb, p.db, p.px, p.nz, p.ny
    rows = px // nc
    f = lambda *s: VMEM(s, F32)
    h = lambda *s: VMEM(s, BF16)
    return dict(
        k1w=f(9, cb, 256), k2w=f(9, db, p.ch), ks=f(nc, cb, 9 * db), b2=f(cb, 9 * db),
        a1=f(9 * db, cb), a2=f(9 * db, cb), g1=f(9 * db, cb), g2=f(9 * db, cb),
        a_cat=h(2, 9 * db, 3 * cb), bm=h(2, cb, 9 * db), b2m=h(2, cb, 9 * db), colh=h(9 * db, px), coll=h(9 * db, px),
        xs=f(nc, rows, cb), rx=f(nc, rows, cb), xin=f(nd, cb, px), act1=f(nd, cb, px), slope1=f(nd, cb, px),
        call=f(nc, nd, cb, px),
        part=f(2 * nd, db, px), near=f(2 * nd, db, px), half=f(2 * nd, db // 2, px), away=f(2 * nd, db // 2, px),
        sums=f(2 * nd, db, px), slope2=f(nd, db, px), dpre=f(nd, db, px),
        outp=f(nd, cb, px), outn=f(nz, cb, px), outc=f(nz, cb, px), outw=f(nz, cb, px),
        inp=f(nd, cb, px), inn=f(nz, cb, px), inc=f(nz, cb, px), inw=f(nz, cb, px),
        dall=f(nd, nd, db, px), act2=f(ny, nd, db, px), left=h(9 * cb, 6 * px), right=h(p.ch, 6 * px),
        stage=f(9 * cb, p.ch),
        par=f(8, cb), pars=f(nc, 8, cb), stat=f(8, cb), stats=f(nd, 8, cb), msg=f(8, cb), msgs=f(nd, 8, cb),
        sq=f(8, 128), sqs=f(nc, 8, 128), vec=f(8, cb), vecs=f(nd, 8, cb),
        k1_sem=DMA, k2_sem=DMA, g1_sem=DMA, g2_sem=DMA,
        xs_s=DMA((nc,)), xs_r=DMA((nc,)), ks_s=DMA((nc,)), ks_r=DMA,
        par_s=DMA((nc,)), par_r=DMA((nc,)), stat_s=DMA((nd,)), stat_r=DMA((nd,)), msg_s=DMA((nd,)), msg_r=DMA((nd,)),
        sq_s=DMA((nc,)), sq_r=DMA((nc,)), vec_s=DMA((nd,)), vec_r=DMA((nd,)),
        x_s=DMA((3, nz)), x_r=DMA((nd,)), c_s=DMA((3, nz)), c_r=DMA((nd,)), d_s=DMA((3, nz)), d_r=DMA((nd,)),
        cs1=DMA((2 * nd,)), cr1=DMA((2 * nd,)), cs2=DMA((2 * nd,)), cr2=DMA((2 * nd,)), cs3=DMA((2 * nd,)), cr3=DMA((2 * nd,)),
        o_s1=DMA((nz,)), o_r1=DMA((nz,)), o_s2=DMA((nz,)), o_r2=DMA((nz,)),
        i_s1=DMA((nz,)), i_r1=DMA((nz,)), i_s2=DMA((nz,)), i_r2=DMA((nz,)),
        call_s=DMA((3, nd)), call_r=DMA((nc, nd)), act_s=DMA((3, nd)), act_r=DMA((ny, nd)),
        far_s=DMA((nd,)), far_r=DMA((nd,)), core_s=DMA((2, nd)), core_r=DMA((2, nd)), in_s=DMA((nc,)), in_r=DMA((nc,)),
    )


ARGS = ("x", "cot", "k1", "k2", "gain1", "shift1", "gain2", "shift2", "groups")
OUTS = ("block_out", "input_grad", "g1_out", "g2_out", "gg1", "sh1", "gg2", "sh2", "norm")


def step_kernel(p, names, *refs):
    r = types.SimpleNamespace(**dict(zip(names, refs)))
    cb, db, px, side, nd, nc, nz, ny = p.cb, p.db, p.px, p.side, p.nd, p.nc, p.nz, p.ny
    d, c = here()
    z, y = lax.div(d, ny), lax.rem(d, ny)
    k = lax.rem(c, 2)
    far, across = lax.rem(c + 2, 4), c + 1 - 2 * k
    last = 6 - c - far - across
    rows = px // nc
    owner = lax.div(d * db, cb)
    image = lambda j: nearest(z, lax.div(j, 2)) * ny + y + lax.rem(j, 2) * (1 - 2 * y)

    base = lax.min(lax.div(d * db, 128), (p.ch - 256) // 128) * 128
    k1_copy = pltpu.make_async_copy(r.k1.at[:, :, pl.ds(pl.multiple_of(base, 128), 256)], r.k1w, r.k1_sem)
    k1_copy.start()
    k2_rows = pl.ds(pl.multiple_of(d * db - owner * cb, 8), db)
    k2_copy = pltpu.make_async_copy(r.k2.at[:, k2_rows], r.k2w, r.k2_sem)
    pl.when(c == owner)(lambda: k2_copy.start())
    greet(p)

    for j in range(nc):
        r.xs[j] = r.x[:, j * cb : (j + 1) * cb]
    a2a = lambda j: send(r.xs.at[lax.rem(c + j, nc)], r.rx.at[c], r.xs_s.at[j], r.xs_r.at[c], (d, lax.rem(c + j, nc)))
    for j in range(1, nc):
        a2a(j).start()
    r.rx[c] = r.xs[c]
    r.par[...] = stacked([r.gain2[...].reshape(1, cb), r.shift2[...].reshape(1, cb)], cb)
    params = ToAll("chan", nc, r.par, r.pars, r.par_s, r.par_r)
    params.start()
    flag = jnp.full((1, 1), jnp.where(r.groups[0] == 1, 1.0, 0.0), F32)
    mine = valid_map(flag, side, px)
    r.call[c, d] = r.cot[...].T * mine

    @pl.when(c == owner)
    def _():
        k2_copy.wait()
        for j in range(nc):
            r.ks[j] = r.k2w[:, :, j * cb : (j + 1) * cb].reshape(9 * db, cb).T

    for j in range(1, nc):
        a2a(j).wait_send()
        other = lax.rem(c + j, nc)
        send(r.xs.at[other], r.rx.at[other], r.xs_s.at[j], r.xs_r.at[other], (d, other)).wait_recv()
    r.xin[d] = r.rx[...].reshape(px, cb).T
    ins = Line(p, lambda s: r.xin.at[s], r.x_s, r.x_r)
    ins.hand_on(z)

    count = lanes_sum(mine)
    total = lanes_sum(r.xin[d] * mine)
    off = r.xin[d] - total / count
    r.stat[...] = stacked([to_row(total), to_row(lanes_sum(mine * off * off)), jnp.broadcast_to(flag, (1, cb))], cb)
    stats = ToAll("dp", nd, r.stat, r.stats, r.stat_s, r.stat_r)
    stats.start()

    piece = lambda j: send(r.ks.at[lax.rem(c + j, nc)], r.b2, r.ks_s.at[j], r.ks_r, (d, lax.rem(c + j, nc)))

    @pl.when(c == owner)
    def _():
        for j in range(1, nc):
            piece(j).start()

    k1_copy.wait()
    turn = lax.rem(256 - (d * db - base), 256)
    b1 = jnp.concatenate([pltpu.roll(r.k1w[t], turn, axis=1)[:, :db] for t in range(9)], axis=1)
    hi, lo = split(b1)
    r.bm[0], r.bm[1] = hi, lo
    r.a1[...] = b1.T
    hi, lo = split(r.a1[...])
    r.a_cat[0] = jnp.concatenate([hi, hi, lo], axis=1)

    stats.finish()

    def val_of(i):
        return valid_map(r.stats[i, 2:3, 0:1], side, px)

    counts = [jnp.sum(val_of(i), keepdims=True) for i in range(nd)]
    pixels = functools.reduce(jnp.add, counts)
    center = functools.reduce(jnp.add, [r.stats[i, 0:1] for i in range(nd)]) / pixels
    spread = [r.stats[i, 1:2] + counts[i] * (r.stats[i, 0:1] / counts[i] - center) ** 2 for i in range(nd)]
    center1, rs1 = to_col(center), to_col(lax.rsqrt(functools.reduce(jnp.add, spread) / pixels + epsilon))
    gain1, shift1 = to_col(r.gain1[...].reshape(1, cb)), to_col(r.shift1[...].reshape(1, cb))

    chan = ChanSum(p, r)

    def first_map(i, gain, shift):
        val = val_of(i)
        act, slope = silu_and_slope((r.xin[i] - center1) * rs1 * gain + shift)
        act = act * val
        r.act1[i], r.slope1[i] = act, slope * val
        ah, al = split(act)
        prod = dot(r.a_cat[0], jnp.concatenate([ah, al, ah], axis=0))
        r.part[i] = gather_taps(prod, side, db) * val
        chan.first(i).start()

    def second_back(i):
        ch, cl = split(r.call[c, i])
        prod = dot(r.a_cat[1], jnp.concatenate([ch, cl, ch], axis=0))
        r.part[nd + i] = gather_taps(prod, side, db) * val_of(i)
        chan.first(nd + i).start()

    def forward(kk, _):
        zs = nearest(z, kk)

        @pl.when(kk > 0)
        def _():
            ins.got(zs, y)
            ins.hand_on(zs)

        first_map(zs * ny + y, gain1, shift1)
        chan.advance(2 * kk, nd, image)
        ins.got(zs, 1 - y)
        first_map(zs * ny + 1 - y, gain1, shift1)
        chan.advance(2 * kk + 1, nd, image)
        return 0

    lax.fori_loop(0, nz, forward, 0)
    cots = Line(p, lambda s: r.call.at[c, s], r.c_s, r.c_r)
    cots.hand_on(z)

    @pl.when(c == owner)
    def _():
        r.b2[...] = r.ks[c]

    @pl.when(c != owner)
    def _():
        send(r.ks.at[0], r.b2, r.ks_s.at[0], r.ks_r, (d, owner)).wait_recv()

    def set_back(a2):
        for t in range(9):
            hi, lo = split(a2[(8 - t) * db : (9 - t) * db])
            r.a_cat[1, t * db : (t + 1) * db] = jnp.concatenate([hi, hi, lo], axis=1)

    r.a2[...] = r.b2[...].T
    set_back(r.a2)

    def flush(j, _):
        chan.advance(j, nd, image)
        return 0

    lax.fori_loop(nd, nd + 4, flush, 0)

    params.finish()
    both = [r.pars[owner, j : j + 1] for j in range(2)]
    low = lax.rem(d * db, cb) == 0
    gain2, shift2 = (to_col(jnp.where(low, v[:, :db], v[:, cb - db :])) for v in both)

    def add_up(i, carry):
        return carry + lanes_sum(r.sums[i] * val_of(i))

    center2 = lax.fori_loop(0, nd, add_up, jnp.zeros((db, 1), F32)) / pixels

    def add_squares(i, carry):
        off = r.sums[i] - center2
        return carry + lanes_sum(val_of(i) * off * off)

    rs2 = lax.rsqrt(lax.fori_loop(0, nd, add_squares, jnp.zeros((db, 1), F32)) / pixels + epsilon)

    outs = ImageSum(p, r.outp, r.outn, r.outc, r.outw, r.o_s1, r.o_r1, r.o_s2, r.o_r2)
    b2h, b2l = split(r.b2[...])

    def set_cols(maps):
        for t, m in enumerate(maps):
            hi, lo = split(m)
            r.colh[t * db : (t + 1) * db] = hi
            r.coll[t * db : (t + 1) * db] = lo

    def im2col_dot(which):
        return dot(which[0], r.colh[...]) + dot(which[0], r.coll[...]) + dot(which[1], r.colh[...])

    def wgrad(other):
        oh, ol = split(other)
        left = jnp.concatenate([r.colh[...], r.colh[...], r.coll[...]], axis=1)
        return dot_nt(left, jnp.concatenate([oh, ol, oh], axis=1))

    call_copy = lambda which, sem, i, to: send(
        r.call.at[which, i], r.call.at[which, i], r.call_s.at[sem, i], r.call_r.at[which, i], (d, to)
    )
    r.g2[...] = jnp.zeros_like(r.g2)

    def second_map(i):
        val = val_of(i)
        act, slope = silu_and_slope((r.sums[i] - center2) * rs2 * gain2 + shift2)
        r.slope2[i] = slope * val
        set_cols(shifts(act * val, side))
        r.outp[i] = im2col_dot((r.b2m[0], r.b2m[1]))
        r.g2[...] += wgrad(r.call[c, i])

    def back_item(j):
        return nd + image(j)

    def cotangent(kk, _):
        zs = nearest(z, kk)

        @pl.when(kk > 0)
        def _():
            cots.got(zs, y)
            cots.hand_on(zs)

        i = zs * ny + y
        second_back(i)
        call_copy(c, 0, i, far).start()
        call_copy(c, 1, i, across).start()
        chan.advance(2 * kk, nd, back_item)
        second_map(i)
        cots.got(zs, 1 - y)
        i = zs * ny + 1 - y
        second_back(i)
        call_copy(c, 0, i, far).start()
        call_copy(c, 1, i, across).start()
        chan.advance(2 * kk + 1, nd, back_item)
        second_map(i)
        outs.near(zs).start()
        return 0

    r.b2m[0], r.b2m[1] = b2h, b2l
    lax.fori_loop(0, nz, cotangent, 0)

    def flush_back(j, _):
        chan.advance(j, nd, back_item)
        return 0

    lax.fori_loop(nd, nd + 4, flush_back, 0)
    outs.spread()

    def inner_sums(i, carry):
        dpre = r.sums[nd + i] * r.slope2[i]
        r.dpre[i] = dpre
        scaled = (r.sums[i] - center2) * rs2
        return carry[0] + lanes_sum(dpre), carry[1] + lanes_sum(dpre * scaled)

    zero = jnp.zeros((db, 1), F32)
    sh2, gg2 = lax.fori_loop(0, nd, inner_sums, (zero, zero))
    r.g1[...] = jnp.zeros_like(r.g1)

    def backward(i, carry):
        scaled = (r.sums[i] - center2) * rs2
        dinner = gain2 * rs2 * (r.dpre[i] - val_of(i) * (sh2 + scaled * gg2) / pixels)
        set_cols(shifts(dinner, side, -1))
        r.g1[...] += wgrad(r.act1[i])
        dpre1 = im2col_dot((r.bm[0], r.bm[1])) * r.slope1[i]
        scaled1 = (r.xin[i] - center1) * rs1
        return carry[0] + lanes_sum(dpre1), carry[1] + lanes_sum(dpre1 * scaled1)

    zero = jnp.zeros((cb, 1), F32)
    sh1, gg1 = lax.fori_loop(0, nd, backward, (zero, zero))

    square = jnp.sum(r.g1[...] * r.g1[...] + r.g2[...] * r.g2[...], keepdims=True)
    square = square + jnp.where(c == 0, jnp.sum(sh2 * sh2 + gg2 * gg2, keepdims=True), 0.0)
    r.msg[...] = stacked([to_row(sh1), to_row(gg1), jnp.broadcast_to(square, (1, cb))], cb)
    over_dp = ToAll("dp", nd, r.msg, r.msgs, r.msg_s, r.msg_r)
    over_dp.start()
    r.block_out[...] = ((r.xin[d] + outs.total()) * mine).T
    over_dp.finish()
    total = over_dp.total()
    sh1, gg1 = to_col(total[0:1]), to_col(total[1:2])
    square = total[2:3, 0:1] + jnp.sum(sh1 * sh1 + gg1 * gg1, keepdims=True)
    r.sq[...] = jnp.broadcast_to(square, (8, 128))
    over_chan = ToAll("chan", nc, r.sq, r.sqs, r.sq_s, r.sq_r)
    over_chan.start()
    over_chan.finish()
    square = over_chan.total()[0:1, 0:1]
    r.norm[0, 0] = jnp.sum(jnp.sqrt(square))
    factor = sam_radius * lax.rsqrt(square + norm_floor)

    gain1, shift1 = gain1 + factor * gg1, shift1 + factor * sh1
    gain2, shift2 = gain2 + factor * gg2, shift2 + factor * sh2
    r.a1[...] += factor * r.g1[...]
    hi, lo = split(r.a1[...])
    r.a_cat[0] = jnp.concatenate([hi, hi, lo], axis=1)
    r.a2[...] += factor * r.g2[...]
    set_back(r.a2)

    act_copy = lambda sem, ys, i, z_to, y_to: send(
        r.act2.at[ys, i], r.act2.at[ys, i], r.act_s.at[sem, i], r.act_r.at[ys, i], (z_to * ny + y_to, c)
    )
    act_up = lambda i: act_copy(0, y, i, lax.min(z + 1, nz - 1), y)
    act_down = lambda i: act_copy(1, y, i, lax.max(z - 1, 0), y)
    act_side = lambda i: act_copy(2, y, i, z, 1 - y)

    def act_hand_on(i):
        pl.when((z >= c) & (z < nz - 1))(lambda: act_up(i).start())
        pl.when((z <= c) & (z > 0))(lambda: act_down(i).start())
        act_side(i).start()

    def second_act(i):
        val = val_of(i)
        act, slope = silu_and_slope((r.sums[i] - center2) * rs2 * gain2 + shift2)
        r.slope2[i] = slope * val

        @pl.when(z == c)
        def _():
            r.act2[y, i] = act * val
            act_hand_on(i)

    both_item = lambda j: j

    def project(j, _):
        pl.when(j < nd)(lambda: first_map(lax.min(j, nd - 1), gain1, shift1))
        pl.when((j >= nd) & (j < 2 * nd))(lambda: second_back(lax.clamp(0, j - nd, nd - 1)))
        chan.advance(j, 2 * nd, both_item)
        pl.when((j >= 4) & (j < nd + 4))(lambda: second_act(lax.clamp(0, j - 4, nd - 1)))
        return 0

    lax.fori_loop(0, 2 * nd + 4, project, 0)

    def inner_grad(i, carry):
        dpre = r.sums[nd + i] * r.slope2[i]
        r.dall[d, i] = gain2 * rs2 * dpre
        scaled = (r.sums[i] - center2) * rs2
        return carry[0] + lanes_sum(dpre), carry[1] + lanes_sum(dpre * scaled)

    zero = jnp.zeros((db, 1), F32)
    sh2, gg2 = lax.fori_loop(0, nd, inner_grad, (zero, zero))

    pair = lambda s, q: r.dall.at[s, pl.ds(2 * q, 2)]
    grads = Line(p, lambda s: pair(s, c), r.d_s, r.d_r)
    grads.hand_on(z)
    to_far = lambda s, q: send(pair(s, q), pair(s, q), r.far_s.at[s], r.far_r.at[s], (d, far))
    to_core = lambda lane, s, q: send(pair(s, q), pair(s, q), r.core_s.at[lane, s], r.core_r.at[lane, s], (d, across))

    def over_chan_too(s):
        to_far(s, c).start()
        to_core(0, s, c).start()

    hi, lo = split(r.a1[...].T)
    r.bm[0], r.bm[1] = hi, lo
    ins_grad = ImageSum(p, r.inp, r.inn, r.inc, r.inw, r.i_s1, r.i_r1, r.i_s2, r.i_r2)

    def input_grad(i):
        set_cols(shifts(r.dall[d, i], side, -1))
        r.inp[i] = im2col_dot((r.bm[0], r.bm[1]))

    def to_partner(kk, _):
        zs = nearest(z, kk)
        input_grad(zs * ny + 1 - y)
        ins_grad.near(zs).start()

        @pl.when(z != c)
        def _():
            for j in range(2):
                i = 2 * kk + j
                act_copy(0, y, i, z, 1 - y).wait_recv()
                act_hand_on(i)

        return 0

    lax.fori_loop(0, nz, to_partner, 0)

    def at_home(kk, _):
        zs = nearest(z, kk)
        input_grad(zs * ny + y)

        @pl.when(kk > 0)
        def _():
            grads.got(zs, y)
            grads.hand_on(zs)
            over_chan_too(zs * ny + y)

        return 0

    lax.fori_loop(0, nz, at_home, 0)
    ins_grad.spread()

    def norm_sums(i, carry):
        dpre = r.inp[i] * r.slope1[i]
        scaled = (r.xin[i] - center1) * rs1
        return carry[0] + lanes_sum(dpre), carry[1] + lanes_sum(dpre * scaled)

    zero = jnp.zeros((cb, 1), F32)
    sh1, gg1 = lax.fori_loop(0, nd, norm_sums, (zero, zero))
    pad = jnp.zeros((1, cb - db), F32)
    wide = lambda col: jnp.concatenate([to_row(col), pad], axis=1)
    r.vec[...] = stacked([to_row(sh1), to_row(gg1), wide(sh2), wide(gg2)], cb)
    vectors = ToAll("dp", nd, r.vec, r.vecs, r.vec_s, r.vec_r)
    vectors.start()

    def relay_call(i, _):
        call_copy(far, 0, i, far).wait_recv()
        call_copy(far, 2, i, across).start()
        return 0

    lax.fori_loop(0, nd, relay_call, 0)

    def call_here(i, _):
        call_copy(across, 0, i, across).wait_recv()
        call_copy(last, 0, i, across).wait_recv()
        return 0

    lax.fori_loop(0, nd, call_here, 0)

    def kernel_grad(images, left_of, rights_of):
        for j, i in enumerate(images):
            lanes = slice(3 * j * px, 3 * (j + 1) * px)
            for t, m in enumerate(shifts(left_of(i), side)):
                hi, lo = split(m)
                r.left[t * cb : (t + 1) * cb, lanes] = jnp.concatenate([hi, hi, lo], axis=1)
            at = 0
            for v in rights_of(i):
                n = v.shape[0]
                hi, lo = split(v)
                r.right[at : at + n, lanes] = jnp.concatenate([hi, lo, hi], axis=1)
                at += n
        r.stage[...] += dot_nt(r.left[...], r.right[...])

    r.stage[...] = jnp.zeros_like(r.stage)

    def second_kernel(q, _):
        for j in range(2):
            act_copy(0, 1 - y, 2 * q + j, z, 1 - y).wait_recv()
        kernel_grad(
            [2 * q, 2 * q + 1],
            lambda i: jnp.concatenate([r.act2[0, i], r.act2[1, i]], axis=0),
            lambda i: [r.call[j, i] for j in range(nc)],
        )
        zs = nearest(z, q)
        grads.got(zs, 1 - y)
        over_chan_too(zs * ny + 1 - y)
        return 0

    lax.fori_loop(0, nz, second_kernel, 0)
    g2_copy = pltpu.make_async_copy(r.stage, r.g2_out, r.g2_sem)
    g2_copy.start()

    for j in range(1, nd):
        s = lax.rem(d + j, nd)
        to_far(s, far).wait_recv()
        to_core(1, s, far).start()

    grad = (gain1 * rs1 * (ins_grad.total() * r.slope1[d]) + r.call[c, d]).T
    for j in range(nc):
        r.xs[j] = grad[j * rows : (j + 1) * rows]
    back = lambda j: send(r.xs.at[lax.rem(c + j, nc)], r.rx.at[c], r.in_s.at[j], r.in_r.at[c], (d, lax.rem(c + j, nc)))
    for j in range(1, nc):
        back(j).start()
    r.rx[c] = r.xs[c]

    g2_copy.wait()
    r.stage[...] = jnp.zeros_like(r.stage)

    def first_kernel(q):
        kernel_grad([2 * q, 2 * q + 1], lambda i: r.act1[i], lambda i: [r.dall[s, i] for s in range(nd)])

    first_kernel(c)
    for j in range(1, nd):
        to_core(0, lax.rem(d + j, nd), across).wait_recv()
    first_kernel(across)
    first_kernel(far)
    for j in range(1, nd):
        to_core(1, lax.rem(d + j, nd), last).wait_recv()
    first_kernel(last)
    g1_copy = pltpu.make_async_copy(r.stage, r.g1_out, r.g1_sem)
    g1_copy.start()

    vectors.finish()
    total = vectors.total()
    per = cb // db
    rows_of = lambda j: jnp.concatenate([r.vecs[per * c + q, j : j + 1, :db] for q in range(per)], axis=1)
    r.sh1[...], r.gg1[...] = total[0:1].reshape(cb), total[1:2].reshape(cb)
    r.sh2[...], r.gg2[...] = rows_of(2).reshape(cb), rows_of(3).reshape(cb)
    for j in range(1, nc):
        back(j).wait_send()
        other = lax.rem(c + j, nc)
        send(r.xs.at[other], r.rx.at[other], r.in_s.at[0], r.in_r.at[other], (d, other)).wait_recv()
    for j in range(nc):
        r.input_grad[:, j * cb : (j + 1) * cb] = r.rx[j]

    for line in (ins, cots, grads):
        line.drain()

    @pl.when(c == owner)
    def _():
        for j in range(1, nc):
            piece(j).wait_send()

    def sent(i, _):
        call_copy(c, 0, i, far).wait_send()
        call_copy(c, 1, i, across).wait_send()
        call_copy(far, 2, i, across).wait_send()
        pl.when((z >= c) & (z < nz - 1))(lambda: act_up(i).wait_send())
        pl.when((z <= c) & (z > 0))(lambda: act_down(i).wait_send())
        act_side(i).wait_send()
        return 0

    lax.fori_loop(0, nd, sent, 0)
    for j in range(1, nd):
        s = lax.rem(d + j, nd)
        to_far(s, c).wait_send()
        to_core(0, s, c).wait_send()
        to_core(1, s, far).wait_send()
    g1_copy.wait()


def fused_on_device(p, image_rows, groups, conv_first, conv_second, gain_first, shift_first, gain_second, shift_second, cotangent):
    cb, px = p.cb, p.px
    rows = px // p.nc
    scratch = scratch_of(p)
    out = lambda *s: jax.ShapeDtypeStruct(s, F32)
    any_, vmem, smem = (pl.BlockSpec(memory_space=m) for m in (pl.ANY, VMEM, SMEM))
    block_out, input_grad, g1, g2, gg1, sh1, gg2, sh2, norm = pl.pallas_call(
        functools.partial(step_kernel, p, ARGS + OUTS + tuple(scratch)),
        out_shape=(out(px, cb), out(rows, p.ch), out(9 * cb, p.ch), out(9 * cb, p.ch), out(cb), out(cb), out(cb), out(cb), out(1, 1)),
        in_specs=[vmem, vmem, any_, any_, vmem, vmem, vmem, vmem, smem],
        out_specs=(vmem, vmem, any_, any_, vmem, vmem, vmem, vmem, smem),
        scratch_shapes=list(scratch.values()),
        compiler_params=pltpu.CompilerParams(collective_id=0, has_side_effects=True, vmem_limit_bytes=LIMIT),
    )(
        image_rows.reshape(rows, p.ch), cotangent.reshape(px, cb), conv_first.reshape(9, cb, p.ch),
        conv_second.reshape(9, cb, p.ch), gain_first, shift_first, gain_second, shift_second, groups,
    )
    return (
        block_out.reshape(cotangent.shape), input_grad.reshape(image_rows.shape),
        g1.reshape(conv_first.shape), g2.reshape(conv_second.shape), gg1, sh1, gg2, sh2, norm[0, 0],
    )


def valid_pixels(groups, extent_full):
    places = jnp.arange(extent_full, dtype=jnp.int32)
    extent = jnp.where(groups == 1, extent_full, extent_full // 2).astype(jnp.int32)
    inside = places[None, :] < extent[:, None]
    return (inside[:, :, None] & inside[:, None, :]).astype(jnp.float32)[..., None]


def convolve(values, kernel):
    return lax.conv_general_dilated(
        values,
        kernel,
        (1, 1),
        "SAME",
        dimension_numbers=("NHWC", "HWIO", "NHWC"),
        precision=lax.Precision.HIGHEST,
    )


def silu_slope(preact):
    sigmoid = jax.nn.sigmoid(preact)
    return sigmoid * (1.0 + preact * (1.0 - sigmoid))


def batch_moments(values, validity):
    summed, squares, pixels = lax.psum(
        (
            jnp.sum(values * validity, axis=(0, 1, 2)),
            jnp.sum(validity * values * values, axis=(0, 1, 2)),
            jnp.sum(validity),
        ),
        "dp",
    )
    center = summed / pixels
    spread = squares / pixels - center * center
    return (center, lax.rsqrt(spread + epsilon), pixels)


def project_over_chan(values, kernel):
    return lax.psum_scatter(convolve(values, kernel), "chan", scatter_dimension=3, tiled=True)


def conv_backward(upstream, values, kernel):
    columns = lax.all_gather(upstream, "chan", axis=3, tiled=True)
    offset = jnp.int32(0)
    inputs_grad = jnp.zeros_like(values)
    kernel_grad = jnp.zeros_like(kernel)
    breadth = columns.shape[3]
    kernel_part = lax.dynamic_slice_in_dim(kernel, offset, breadth, 3)
    primal, pull = jax.vjp(convolve, values, kernel_part)
    values_part, kernel_part_grad = pull(columns)
    kernel_grad = lax.dynamic_update_slice_in_dim(kernel_grad, kernel_part_grad, offset, 3)
    return (inputs_grad + values_part, kernel_grad)


def batch_sums(dpre, scaled):
    return lax.psum((jnp.sum(dpre, axis=(0, 1, 2)), jnp.sum(dpre * scaled, axis=(0, 1, 2))), "dp")


def plain_on_device(
    image_rows,
    groups,
    conv_first,
    conv_second,
    gain_first,
    shift_first,
    gain_second,
    shift_second,
    cotangent,
):
    inputs = lax.all_to_all(image_rows, "chan", split_axis=3, concat_axis=1, tiled=True)
    validity = valid_pixels(groups, inputs.shape[1])
    cot_valid = cotangent * validity
    center_one, rscale_one, pixels = batch_moments(inputs, validity)
    scaled_one = (inputs - center_one) * rscale_one
    pre_one = scaled_one * gain_first + shift_first
    act_one = jax.nn.silu(pre_one) * validity
    inner = project_over_chan(act_one, conv_first) * validity
    center_two, rscale_two, pixels_again = batch_moments(inner, validity)
    scaled_two = (inner - center_two) * rscale_two
    pre_two = scaled_two * gain_second + shift_second
    act_two = jax.nn.silu(pre_two) * validity
    block_out = inputs * validity + project_over_chan(act_two, conv_second) * validity
    dact_two, kernel_two_part = conv_backward(cot_valid, act_two, conv_second)
    dpre_two = dact_two * validity * silu_slope(pre_two)
    shift_two_grad, gain_two_grad = batch_sums(dpre_two, scaled_two)
    dinner = (
        gain_second
        * rscale_two
        * (dpre_two - validity * (shift_two_grad + scaled_two * gain_two_grad) / pixels)
    )
    dact_one, kernel_one_part = conv_backward(dinner, act_one, conv_first)
    dpre_one = dact_one * validity * silu_slope(pre_one)
    shift_one_grad, gain_one_grad = batch_sums(dpre_one, scaled_one)
    small_squares = (
        jnp.sum(gain_one_grad**2)
        + jnp.sum(shift_one_grad**2)
        + jnp.sum(gain_two_grad**2)
        + jnp.sum(shift_two_grad**2)
    )
    kernel_one_sum, kernel_two_sum = lax.psum((kernel_one_part, kernel_two_part), "dp")
    local_sq = jnp.sum(kernel_one_sum**2) + jnp.sum(kernel_two_sum**2) + small_squares
    squares = lax.psum(local_sq, "chan")
    factor = sam_radius * lax.rsqrt(squares + norm_floor)
    kernel_one = conv_first + factor * kernel_one_sum
    kernel_two = conv_second + factor * kernel_two_sum
    grad_norm = jnp.sqrt(squares)
    moved_gain_one = gain_first + factor * gain_one_grad
    moved_shift_one = shift_first + factor * shift_one_grad
    moved_gain_two = gain_second + factor * gain_two_grad
    moved_shift_two = shift_second + factor * shift_two_grad
    pre_one_new = scaled_one * moved_gain_one + moved_shift_one
    act_one_new = jax.nn.silu(pre_one_new) * validity
    inner_new = project_over_chan(act_one_new, kernel_one) * validity
    scaled_two_new = (inner_new - center_two) * rscale_two
    pre_two_new = scaled_two_new * moved_gain_two + moved_shift_two
    act_two_new = jax.nn.silu(pre_two_new) * validity
    dact_two_new, kernel_two_grad = conv_backward(cot_valid, act_two_new, kernel_two)
    dpre_two_new = dact_two_new * validity * silu_slope(pre_two_new)
    gain_two_new_grad = jnp.sum(dpre_two_new * scaled_two_new, axis=(0, 1, 2))
    shift_two_new_grad = jnp.sum(dpre_two_new, axis=(0, 1, 2))
    dinner_new = moved_gain_two * rscale_two * dpre_two_new
    dact_one_new, kernel_one_grad = conv_backward(dinner_new, act_one_new, kernel_one)
    dpre_one_new = dact_one_new * validity * silu_slope(pre_one_new)
    gain_one_new_grad = jnp.sum(dpre_one_new * scaled_one, axis=(0, 1, 2))
    shift_one_new_grad = jnp.sum(dpre_one_new, axis=(0, 1, 2))
    inputs_grad = moved_gain_one * rscale_one * dpre_one_new + cot_valid
    input_grad = lax.all_to_all(inputs_grad, "chan", split_axis=1, concat_axis=3, tiled=True)
    (
        kernel_one_grad,
        kernel_two_grad,
        gain_one_new_grad,
        shift_one_new_grad,
        gain_two_new_grad,
        shift_two_new_grad,
    ) = lax.psum(
        (
            kernel_one_grad,
            kernel_two_grad,
            gain_one_new_grad,
            shift_one_new_grad,
            gain_two_new_grad,
            shift_two_new_grad,
        ),
        "dp",
    )
    return (
        block_out,
        input_grad,
        kernel_one_grad,
        kernel_two_grad,
        gain_one_new_grad,
        shift_one_new_grad,
        gain_two_new_grad,
        shift_two_new_grad,
        grad_norm,
    )


def solution(mesh):
    nd, nc = mesh.shape["dp"], mesh.shape["chan"]

    def on_device(image_rows, *rest):
        images, side, channels = image_rows.shape[0], image_rows.shape[2], image_rows.shape[3]
        fits = images == 1 and nc == 4 and nd == 2 * nc and channels // nd % 16 == 0 and side * side == 256
        if not fits:
            return plain_on_device(image_rows, *rest)
        return fused_on_device(Plan(nd, nc, channels, side), image_rows, *rest)

    return jax.shard_map(
        on_device,
        mesh=mesh,
        in_specs=(
            P("dp", "chan", None, None),
            P("dp"),
            P(None, None, "chan", None),
            P(None, None, "chan", None),
            P("chan"),
            P("chan"),
            P("chan"),
            P("chan"),
            P("dp", None, None, "chan"),
        ),
        out_specs=(
            P("dp", None, None, "chan"),
            P("dp", "chan", None, None),
            P(None, None, "chan", None),
            P(None, None, "chan", None),
            P("chan"),
            P("chan"),
            P("chan"),
            P("chan"),
            P(),
        ),
        check_vma=False,
    )
```

```python
import functools
import types

import jax
import jax.numpy as jnp
from jax import lax
from jax.experimental import pallas as pl
from jax.experimental.pallas import tpu as pltpu
from jax.sharding import PartitionSpec as P

epsilon = 1e-05
sam_radius = 0.05
norm_floor = 1e-06
MESH = pl.DeviceIdType.MESH
F32, BF16 = jnp.float32, jnp.bfloat16
VMEM, SMEM = pltpu.VMEM, pltpu.SMEM
DMA = pltpu.SemaphoreType.DMA
LIMIT = 60 << 20


class Plan:
    def __init__(self, nd, nc, channels, side):
        self.nd, self.nc, self.ch, self.side = nd, nc, channels, side
        self.cb, self.db, self.px = channels // nc, channels // nd, side * side
        self.ny = 2
        self.nz = nd // 2


def split(v):
    hi = v.astype(BF16)
    return hi, (v - hi.astype(F32)).astype(BF16)


def dot(a, b):
    return lax.dot_general(a, b, (((1,), (0,)), ((), ())), preferred_element_type=F32)


def dot_nt(a, b):
    return lax.dot_general(a, b, (((1,), (1,)), ((), ())), preferred_element_type=F32)


def edge_masks(side, px):
    lane = lax.broadcasted_iota(jnp.int32, (1, px), 1)
    col = lax.rem(lane, side)
    row = lax.div(lane, side)
    one = jnp.ones((1, px), F32)
    zero = jnp.zeros((1, px), F32)
    rows = {-1: jnp.where(row >= 1, one, zero), 0: None, 1: jnp.where(row < side - 1, one, zero)}
    cols = {-1: jnp.where(col >= 1, one, zero), 0: None, 1: jnp.where(col < side - 1, one, zero)}
    return rows, cols


def moved(v, lanes, mask):
    if lanes:
        v = pltpu.roll(v, (-lanes) % v.shape[1], axis=1)
    return v if mask is None else v * mask


def shifts(v, side, sign=1):
    rows, cols = edge_masks(side, v.shape[1])
    by_col = {s: moved(v, s, cols[s]) for s in (-1, 0, 1)}
    return [moved(by_col[sign * s], sign * r * side, rows[sign * r]) for r in (-1, 0, 1) for s in (-1, 0, 1)]


def gather_taps(prod, side, n):
    rows, cols = edge_masks(side, prod.shape[1])
    total = None
    for j, s in enumerate((-1, 0, 1)):
        part = None
        for i, r in enumerate((-1, 0, 1)):
            t = 3 * i + j
            m = moved(prod[t * n : (t + 1) * n], r * side, rows[r])
            part = m if part is None else part + m
        m = moved(part, s, cols[s])
        total = m if total is None else total + m
    return total


def sigmoid(t):
    return 1.0 / (1.0 + jnp.exp(-t))


def silu_and_slope(pre):
    s = sigmoid(pre)
    return pre * s, s * (1.0 + pre * (1.0 - s))


def lanes_sum(v):
    return jnp.sum(v, axis=1, keepdims=True)


def valid_map(flag, side, px):
    lane = lax.broadcasted_iota(jnp.int32, (1, px), 1)
    half = (lax.rem(lane, side) < side // 2) & (lax.div(lane, side) < side // 2)
    return jnp.where(half, jnp.ones((1, px), F32), flag)


def diagonal(n):
    return lax.broadcasted_iota(jnp.int32, (n, n), 0) == lax.broadcasted_iota(jnp.int32, (n, n), 1)


def to_row(col):
    return jnp.sum(jnp.where(diagonal(col.shape[0]), col, 0.0), axis=0, keepdims=True)


def to_col(row):
    return jnp.sum(jnp.where(diagonal(row.shape[1]), row, 0.0), axis=1, keepdims=True)


def stacked(rows, n):
    at = lax.broadcasted_iota(jnp.int32, (8, n), 0)
    out = jnp.zeros((8, n), F32)
    for k, row in enumerate(rows):
        out = jnp.where(at == k, row, out)
    return out


def send(src, dst, ss, rs, device):
    return pltpu.make_async_remote_copy(
        src_ref=src, dst_ref=dst, send_sem=ss, recv_sem=rs, device_id=device, device_id_type=MESH
    )


def here():
    return lax.axis_index("dp"), lax.axis_index("chan")


def greet(p):
    d, c = here()
    barrier = pltpu.get_barrier_semaphore()
    for j in range(1, p.nd):
        pl.semaphore_signal(barrier, inc=1, device_id=(lax.rem(d + j, p.nd), c), device_id_type=MESH)
    for j in range(1, p.nc):
        pl.semaphore_signal(barrier, inc=1, device_id=(d, lax.rem(c + j, p.nc)), device_id_type=MESH)
    pl.semaphore_wait(barrier, p.nd - 1 + p.nc - 1)


class ToAll:
    def __init__(self, axis, n, tile, slots, ss, rs):
        d, c = here()
        self.n, self.tile, self.slots, self.ss, self.rs = n, tile, slots, ss, rs
        self.me = d if axis == "dp" else c
        self.device = (lambda o: (o, c)) if axis == "dp" else (lambda o: (d, o))

    def start(self):
        self.slots[self.me] = self.tile[...]
        for j in range(1, self.n):
            to = lax.rem(self.me + j, self.n)
            send(self.tile, self.slots.at[self.me], self.ss.at[j], self.rs.at[self.me], self.device(to)).start()

    def finish(self):
        for j in range(1, self.n):
            other = lax.rem(self.me + j, self.n)
            send(self.tile, self.slots.at[other], self.ss.at[j], self.rs.at[other], self.device(other)).wait()

    def total(self):
        total = self.slots[0]
        for j in range(1, self.n):
            total = total + self.slots[j]
        return total


class Line:
    def __init__(self, p, view, ss, rs, sides=True):
        self.p, self.view, self.ss, self.rs, self.sides = p, view, ss, rs, sides
        d, self.c = here()
        self.z, self.y = lax.div(d, p.ny), lax.rem(d, p.ny)

    def copy(self, zs, sem, z_to, y_to):
        slot = zs * self.p.ny + self.y
        return send(self.view(slot), self.view(slot), self.ss.at[sem, zs], self.rs.at[slot], (z_to * self.p.ny + y_to, self.c))

    def up(self, zs):
        return self.copy(zs, 0, lax.min(self.z + 1, self.p.nz - 1), self.y)

    def down(self, zs):
        return self.copy(zs, 1, lax.max(self.z - 1, 0), self.y)

    def side(self, zs):
        return self.copy(zs, 2, self.z, 1 - self.y)

    def got(self, zs, y):
        slot = zs * self.p.ny + y
        send(self.view(slot), self.view(slot), self.ss.at[0, 0], self.rs.at[slot], (self.z * self.p.ny + 1 - self.y, self.c)).wait_recv()

    def hand_on(self, zs):
        pl.when((zs <= self.z) & (self.z < self.p.nz - 1))(lambda: self.up(zs).start())
        pl.when((zs >= self.z) & (self.z > 0))(lambda: self.down(zs).start())
        if self.sides:
            self.side(zs).start()

    def drain(self):
        for zs in range(self.p.nz):
            pl.when((zs <= self.z) & (self.z < self.p.nz - 1))(lambda: self.up(zs).wait_send())
            pl.when((zs >= self.z) & (self.z > 0))(lambda: self.down(zs).wait_send())
            if self.sides:
                self.side(zs).wait_send()


def nearest(z, k):
    t = lax.div(z, 2)
    low = z + t * (3 - 2 * z)
    first = 1 - lax.min(lax.div(k, 2), 1)
    place = k + low * first * (1 - 2 * k)
    return place * (1 - 2 * t) + 3 * t


class ChanSum:
    def __init__(self, p, r):
        self.p, self.r = p, r
        d, c = here()
        k = lax.rem(c, 2)
        self.hb = p.db // 2
        self.across, self.far = (d, c + 1 - 2 * k), (d, lax.rem(c + 2, 4))
        self.mine = pl.multiple_of(k * self.hb, 8)
        self.yours = pl.multiple_of((1 - k) * self.hb, 8)

    def first(self, i):
        r = self.r
        return send(r.part.at[i, pl.ds(self.yours, self.hb)], r.near.at[i], r.cs1.at[i], r.cr1.at[i], self.across)

    def second(self, i):
        r = self.r
        return send(r.half.at[i], r.away.at[i], r.cs2.at[i], r.cr2.at[i], self.far)

    def third(self, i, rows):
        r = self.r
        mine = r.sums.at[i, pl.ds(self.mine, self.hb)]
        return send(mine, r.sums.at[i, pl.ds(rows, self.hb)], r.cs3.at[i], r.cr3.at[i], self.across)

    def chip(self, i):
        r = self.r
        self.first(i).wait()
        r.half[i] = r.part[i, pl.ds(self.mine, self.hb)] + r.near[i]
        self.second(i).start()

    def cross(self, i):
        r = self.r
        self.second(i).wait()
        r.sums[i, pl.ds(self.mine, self.hb)] = r.half[i] + r.away[i]
        self.third(i, self.mine).start()

    def done(self, i):
        self.third(i, self.yours).wait()

    def advance(self, j, n, item):
        at = lambda m: item(lax.clamp(0, m, n - 1))
        pl.when((j >= 1) & (j < n + 1))(lambda: self.chip(at(j - 1)))
        pl.when((j >= 3) & (j < n + 3))(lambda: self.cross(at(j - 3)))
        pl.when((j >= 4) & (j < n + 4))(lambda: self.done(at(j - 4)))


class ImageSum:
    def __init__(self, p, part, near, acc, away, s1, r1, s2, r2):
        self.p, self.part, self.buf1, self.acc, self.buf2 = p, part, near, acc, away
        self.s1, self.r1, self.s2, self.r2 = s1, r1, s2, r2
        d, self.c = here()
        self.z, self.y = lax.div(d, p.ny), lax.rem(d, p.ny)

    def near(self, zs):
        side = 1 - self.y
        return send(self.part.at[zs * self.p.ny + side], self.buf1.at[zs], self.s1.at[zs], self.r1.at[zs],
                    (self.z * self.p.ny + side, self.c))

    def away(self, zs, slot):
        return send(self.acc.at[zs], self.buf2.at[slot], self.s2.at[zs], self.r2.at[slot], (zs * self.p.ny + self.y, self.c))

    def spread(self, zs):
        self.near(zs).wait()
        self.acc[zs] = self.part[zs * self.p.ny + self.y] + self.buf1[zs]
        pl.when(zs != self.z)(lambda: self.away(zs, self.z).start())

    def total(self):
        total = self.acc[self.z]
        for j in range(1, self.p.nz):
            other = lax.rem(self.z + j, self.p.nz)
            self.away(other, other).wait()
            total = total + self.buf2[other]
        return total


def scratch_of(p):
    nd, nc, cb, db, px, nz, ny = p.nd, p.nc, p.cb, p.db, p.px, p.nz, p.ny
    rows = px // nc
    f = lambda *s: VMEM(s, F32)
    h = lambda *s: VMEM(s, BF16)
    return dict(
        k1w=f(9, cb, 256), k2w=f(9, db, p.ch), ks=f(nc, cb, 9 * db), b2=f(cb, 9 * db),
        a1=f(9 * db, cb), a2=f(9 * db, cb), g1=f(9 * db, cb), g2=f(9 * db, cb),
        a_cat=h(2, 9 * db, 3 * cb), bm=h(2, cb, 9 * db), b2m=h(2, cb, 9 * db), colh=h(9 * db, px), coll=h(9 * db, px),
        xs=f(nc, rows, cb), rx=f(nc, rows, cb), xin=f(nd, cb, px), act1=f(nd, cb, px), slope1=f(nd, cb, px),
        call=f(nc, nd, cb, px),
        part=f(3 * nd, db, px), near=f(3 * nd, db // 2, px), half=f(3 * nd, db // 2, px), away=f(3 * nd, db // 2, px),
        sums=f(3 * nd, db, px), slope2=f(nd, db, px), dpre=f(nd, db, px), add1=f(2, cb, px), add2=f(2, db, px),
        outp=f(nd, cb, px), outn=f(nz, cb, px), outc=f(nz, cb, px), outw=f(nz, cb, px),
        inp=f(nd, cb, px), inn=f(nz, cb, px), inc=f(nz, cb, px), inw=f(nz, cb, px),
        dall=f(nd, nd, db, px), act2=f(ny, nd, db, px), own2=f(nd, db, px), left=h(9 * cb, 6 * px), right=h(p.ch, 6 * px),
        stage=f(9 * cb, p.ch),
        par=f(8, cb), pars=f(nc, 8, cb), stat=f(8, cb), stats=f(nd, 8, cb), msg=f(8, cb), msgs=f(nd, 8, cb),
        sq=f(8, 128), sqs=f(nc, 8, 128), vec=f(8, cb), vecs=f(nd, 8, cb),
        k1_sem=DMA, k2_sem=DMA, g1_sem=DMA, g2_sem=DMA,
        xs_s=DMA((nc,)), xs_r=DMA((nc,)), ks_s=DMA((nc,)), ks_r=DMA,
        par_s=DMA((nc,)), par_r=DMA((nc,)), stat_s=DMA((nd,)), stat_r=DMA((nd,)), msg_s=DMA((nd,)), msg_r=DMA((nd,)),
        sq_s=DMA((nc,)), sq_r=DMA((nc,)), vec_s=DMA((nd,)), vec_r=DMA((nd,)),
        x_s=DMA((3, nz)), x_r=DMA((nd,)), c_s=DMA((3, nz)), c_r=DMA((nd,)), d_s=DMA((3, nz)), d_r=DMA((nd,)),
        cs1=DMA((3 * nd,)), cr1=DMA((3 * nd,)), cs2=DMA((3 * nd,)), cr2=DMA((3 * nd,)), cs3=DMA((3 * nd,)), cr3=DMA((3 * nd,)),
        o_s1=DMA((nz,)), o_r1=DMA((nz,)), o_s2=DMA((nz,)), o_r2=DMA((nz,)),
        i_s1=DMA((nz,)), i_r1=DMA((nz,)), i_s2=DMA((nz,)), i_r2=DMA((nz,)),
        call_s=DMA((2, nd)), call_r=DMA((2, nd)), own_s=DMA, f_s=DMA((3, nz)), f_r=DMA((nd,)), act_s=DMA((3, nd)), act_r=DMA((ny, nd)),
        far_s=DMA((nd,)), far_r=DMA((nd,)), core_s=DMA((2, nd)), core_r=DMA((2, nd)), in_s=DMA((nc,)), in_r=DMA((nc,)),
    )


ARGS = ("x", "cot", "k1", "k2", "gain1", "shift1", "gain2", "shift2", "groups")
OUTS = ("block_out", "input_grad", "g1_out", "g2_out", "small")


def step_kernel(p, names, *refs):
    r = types.SimpleNamespace(**dict(zip(names, refs)))
    cb, db, px, side, nd, nc, nz, ny = p.cb, p.db, p.px, p.side, p.nd, p.nc, p.nz, p.ny
    d, c = here()
    z, y = lax.div(d, ny), lax.rem(d, ny)
    k = lax.rem(c, 2)
    far, across = lax.rem(c + 2, 4), c + 1 - 2 * k
    last = 6 - c - far - across
    rows = px // nc
    owner = lax.div(d * db, cb)
    image = lambda j: nearest(z, lax.div(j, 2)) * ny + y + lax.rem(j, 2) * (1 - 2 * y)

    base = lax.min(lax.div(d * db, 128), (p.ch - 256) // 128) * 128
    k1_copy = pltpu.make_async_copy(r.k1.at[:, :, pl.ds(pl.multiple_of(base, 128), 256)], r.k1w, r.k1_sem)
    k1_copy.start()
    k2_rows = pl.ds(pl.multiple_of(d * db - owner * cb, 8), db)
    k2_copy = pltpu.make_async_copy(r.k2.at[:, k2_rows], r.k2w, r.k2_sem)
    pl.when(c == owner)(lambda: k2_copy.start())
    greet(p)

    for j in range(nc):
        r.xs[j] = r.x[:, j * cb : (j + 1) * cb]
    a2a = lambda j: send(r.xs.at[lax.rem(c + j, nc)], r.rx.at[c], r.xs_s.at[j], r.xs_r.at[c], (d, lax.rem(c + j, nc)))
    for j in range(1, nc):
        a2a(j).start()
    r.rx[c] = r.xs[c]
    r.par[...] = stacked([r.gain2[...].reshape(1, cb), r.shift2[...].reshape(1, cb)], cb)
    params = ToAll("chan", nc, r.par, r.pars, r.par_s, r.par_r)
    params.start()
    flag = jnp.full((1, 1), jnp.where(r.groups[0] == 1, 1.0, 0.0), F32)
    mine = valid_map(flag, side, px)
    r.call[c, d] = r.cot[...].T * mine

    @pl.when(c == owner)
    def _():
        k2_copy.wait()
        for j in range(nc):
            r.ks[j] = r.k2w[:, :, j * cb : (j + 1) * cb].reshape(9 * db, cb).T

    for j in range(1, nc):
        a2a(j).wait_send()
        other = lax.rem(c + j, nc)
        send(r.xs.at[other], r.rx.at[other], r.xs_s.at[j], r.xs_r.at[other], (d, other)).wait_recv()
    r.xin[d] = r.rx[...].reshape(px, cb).T
    ins = Line(p, lambda s: r.xin.at[s], r.x_s, r.x_r)
    ins.hand_on(z)

    count = lanes_sum(mine)
    total = lanes_sum(r.xin[d] * mine)
    off = r.xin[d] - total / count
    r.stat[...] = stacked([to_row(total), to_row(lanes_sum(mine * off * off)), jnp.broadcast_to(flag, (1, cb))], cb)
    stats = ToAll("dp", nd, r.stat, r.stats, r.stat_s, r.stat_r)
    stats.start()

    piece = lambda j: send(r.ks.at[lax.rem(c + j, nc)], r.b2, r.ks_s.at[j], r.ks_r, (d, lax.rem(c + j, nc)))

    @pl.when(c == owner)
    def _():
        for j in range(1, nc):
            piece(j).start()

    k1_copy.wait()
    turn = lax.rem(256 - (d * db - base), 256)
    b1 = jnp.concatenate([pltpu.roll(r.k1w[t], turn, axis=1)[:, :db] for t in range(9)], axis=1)
    hi, lo = split(b1)
    r.bm[0], r.bm[1] = hi, lo
    r.a1[...] = b1.T
    hi, lo = split(r.a1[...])
    r.a_cat[0] = jnp.concatenate([hi, hi, lo], axis=1)

    stats.finish()

    def val_of(i):
        return valid_map(r.stats[i, 2:3, 0:1], side, px)

    counts = [jnp.sum(val_of(i), keepdims=True) for i in range(nd)]
    pixels = functools.reduce(jnp.add, counts)
    center = functools.reduce(jnp.add, [r.stats[i, 0:1] for i in range(nd)]) / pixels
    spread = [r.stats[i, 1:2] + counts[i] * (r.stats[i, 0:1] / counts[i] - center) ** 2 for i in range(nd)]
    center1, rs1 = to_col(center), to_col(lax.rsqrt(functools.reduce(jnp.add, spread) / pixels + epsilon))
    gain1, shift1 = to_col(r.gain1[...].reshape(1, cb)), to_col(r.shift1[...].reshape(1, cb))

    chan = ChanSum(p, r)

    def first_map(i, gain, shift):
        val = val_of(i)
        act, slope = silu_and_slope((r.xin[i] - center1) * rs1 * gain + shift)
        act = act * val
        r.act1[i], r.slope1[i] = act, slope * val
        ah, al = split(act)
        prod = dot(r.a_cat[0], jnp.concatenate([ah, al, ah], axis=0))
        r.part[i] = gather_taps(prod, side, db) * val
        chan.first(i).start()

    def second_back(i, first):
        ch, cl = split(r.call[c, i])
        prod = dot(r.a_cat[1], jnp.concatenate([ch, cl, ch], axis=0))
        r.part[first + i] = gather_taps(prod, side, db) * val_of(i)
        chan.first(first + i).start()

    def meet(line, step, then=None):
        def one(zs):
            line.got(zs, y)
            line.hand_on(zs)
            if then is not None:
                then(zs)

        pl.when(z >= step)(lambda: one(lax.max(z - step, 0)))
        pl.when(z + step < nz)(lambda: one(lax.min(z + step, nz - 1)))

    cots = Line(p, lambda s: r.call.at[c, s], r.c_s, r.c_r)

    def forward(kk, _):
        zs = nearest(z, kk)
        first_map(zs * ny + y, gain1, shift1)
        chan.advance(2 * kk, nd, image)
        meet(ins, kk + 1)
        pl.when(kk == nz - 2)(lambda: cots.hand_on(z))
        ins.got(zs, 1 - y)
        first_map(zs * ny + 1 - y, gain1, shift1)
        chan.advance(2 * kk + 1, nd, image)
        return 0

    lax.fori_loop(0, nz, forward, 0)

    own_cot = lambda q: send(r.call.at[q, d], r.call.at[q, d], r.own_s, r.f_r.at[d], (d, far))
    own_cot(c).start()
    fars = Line(p, lambda s: r.call.at[far, s], r.f_s, r.f_r, False)
    far_side = lambda zs: fars.side(zs)
    call_copy = lambda lane, q, i: send(
        r.call.at[q, i], r.call.at[q, i], r.call_s.at[lane, i], r.call_r.at[lane, i], (d, across)
    )

    meet(cots, 1)

    @pl.when(c == owner)
    def _():
        r.b2[...] = r.ks[c]

    @pl.when(c != owner)
    def _():
        send(r.ks.at[0], r.b2, r.ks_s.at[0], r.ks_r, (d, owner)).wait_recv()

    def set_back(a2):
        for t in range(9):
            hi, lo = split(a2[(8 - t) * db : (9 - t) * db])
            r.a_cat[1, t * db : (t + 1) * db] = jnp.concatenate([hi, hi, lo], axis=1)

    chan.advance(nd, nd, image)
    r.a2[...] = r.b2[...].T
    chan.advance(nd + 1, nd, image)
    set_back(r.a2)
    chan.advance(nd + 2, nd, image)
    b2h, b2l = split(r.b2[...])
    r.b2m[0], r.b2m[1] = b2h, b2l
    chan.advance(nd + 3, nd, image)

    meet(cots, 2)

    params.finish()
    both = [r.pars[owner, j : j + 1] for j in range(2)]
    low = lax.rem(d * db, cb) == 0
    gain2, shift2 = (to_col(jnp.where(low, v[:, :db], v[:, cb - db :])) for v in both)

    def add_up(i, carry):
        return carry + lanes_sum(r.sums[i] * val_of(i))

    center2 = lax.fori_loop(0, nd, add_up, jnp.zeros((db, 1), F32)) / pixels

    def add_squares(i, carry):
        off = r.sums[i] - center2
        return carry + lanes_sum(val_of(i) * off * off)

    rs2 = lax.rsqrt(lax.fori_loop(0, nd, add_squares, jnp.zeros((db, 1), F32)) / pixels + epsilon)

    outs = ImageSum(p, r.outp, r.outn, r.outc, r.outw, r.o_s1, r.o_r1, r.o_s2, r.o_r2)

    def set_cols(maps):
        for t, m in enumerate(maps):
            hi, lo = split(m)
            r.colh[t * db : (t + 1) * db] = hi
            r.coll[t * db : (t + 1) * db] = lo

    def im2col_dot(which):
        return dot(which[0], r.colh[...]) + dot(which[0], r.coll[...]) + dot(which[1], r.colh[...])

    def wgrad(other):
        oh, ol = split(other)
        left = jnp.concatenate([r.colh[...], r.colh[...], r.coll[...]], axis=1)
        return dot_nt(left, jnp.concatenate([oh, ol, oh], axis=1))

    r.g2[...] = jnp.zeros_like(r.g2)

    def second_map(i):
        val = val_of(i)
        act, slope = silu_and_slope((r.sums[i] - center2) * rs2 * gain2 + shift2)
        r.slope2[i] = slope * val
        set_cols(shifts(act * val, side))
        r.outp[i] = im2col_dot((r.b2m[0], r.b2m[1]))
        r.g2[...] += wgrad(r.call[c, i])

    def back_item(j):
        return nd + image(j)

    def cotangent(kk, _):
        zs = nearest(z, kk)
        second_back(zs * ny + y, nd)
        chan.advance(2 * kk, nd, back_item)

        @pl.when(kk > 0)
        def _():
            before = nearest(z, lax.max(kk - 1, 0))
            second_map(before * ny + 1 - y)
            outs.near(before).start()

        pl.when(kk == 0)(lambda: meet(cots, 3))

        @pl.when(kk == nz - 2)
        def _():
            own_cot(far).wait_recv()
            fars.hand_on(z)

        cots.got(zs, 1 - y)
        second_back(zs * ny + 1 - y, nd)
        chan.advance(2 * kk + 1, nd, back_item)
        second_map(zs * ny + y)
        return 0

    lax.fori_loop(0, nz, cotangent, 0)
    chan.advance(nd, nd, back_item)
    furthest = nearest(z, nz - 1)
    second_map(furthest * ny + 1 - y)
    outs.near(furthest).start()
    chan.advance(nd + 1, nd, back_item)
    set_back(r.g2)
    chan.advance(nd + 2, nd, back_item)
    chan.advance(nd + 3, nd, back_item)

    def inner_sums(i, carry):
        dpre = r.sums[nd + i] * r.slope2[i]
        r.dpre[i] = dpre
        scaled = (r.sums[i] - center2) * rs2
        return carry[0] + lanes_sum(dpre), carry[1] + lanes_sum(dpre * scaled)

    zero = jnp.zeros((db, 1), F32)
    sh2, gg2 = lax.fori_loop(0, nd, inner_sums, (zero, zero))
    r.g1[...] = jnp.zeros_like(r.g1)

    change_item = lambda j: 2 * nd + j

    def backward(i, carry):
        call_copy(0, c, i).start()

        pl.when(i == 0)(lambda: far_side(z).start())
        pl.when(i >= nz)(lambda: outs.spread(nearest(z, lax.max(nd - 1 - i, 0))))
        scaled = (r.sums[i] - center2) * rs2
        dinner = gain2 * rs2 * (r.dpre[i] - val_of(i) * (sh2 + scaled * gg2) / pixels)
        set_cols(shifts(dinner, side, -1))
        r.g1[...] += wgrad(r.act1[i])
        dpre1 = im2col_dot((r.bm[0], r.bm[1])) * r.slope1[i]
        scaled1 = (r.xin[i] - center1) * rs1
        pl.when(i == 2)(lambda: meet(fars, 1, lambda zs: far_side(zs).start()))
        pl.when(i == 6)(lambda: meet(fars, 2, lambda zs: far_side(zs).start()))
        return carry[0] + lanes_sum(dpre1), carry[1] + lanes_sum(dpre1 * scaled1)

    zero = jnp.zeros((cb, 1), F32)
    sh1, gg1 = lax.fori_loop(0, nd, backward, (zero, zero))

    square = jnp.sum(r.g1[...] * r.g1[...] + r.g2[...] * r.g2[...], keepdims=True)
    square = square + jnp.where(c == 0, jnp.sum(sh2 * sh2 + gg2 * gg2, keepdims=True), 0.0)
    r.msg[...] = stacked([to_row(sh1), to_row(gg1), jnp.broadcast_to(square, (1, cb))], cb)
    over_dp = ToAll("dp", nd, r.msg, r.msgs, r.msg_s, r.msg_r)
    over_dp.start()

    def change(j, _):
        second_back(j, 2 * nd)
        chan.advance(j, nd, change_item)
        return 0

    lax.fori_loop(0, nd // 2, change, 0)
    over_dp.finish()
    total = over_dp.total()
    sh1, gg1 = to_col(total[0:1]), to_col(total[1:2])
    square = total[2:3, 0:1] + jnp.sum(sh1 * sh1 + gg1 * gg1, keepdims=True)
    r.sq[...] = jnp.broadcast_to(square, (8, 128))
    over_chan = ToAll("chan", nc, r.sq, r.sqs, r.sq_s, r.sq_r)
    over_chan.start()
    lax.fori_loop(nd // 2, nd, change, 0)
    over_chan.finish()
    square = over_chan.total()[0:1, 0:1]
    norm = jnp.sqrt(square)
    factor = sam_radius * lax.rsqrt(square + norm_floor)

    gain1, shift1 = gain1 + factor * gg1, shift1 + factor * sh1
    gain2, shift2 = gain2 + factor * gg2, shift2 + factor * sh2
    r.a1[...] += factor * r.g1[...]
    hi, lo = split(r.a1[...])
    r.a_cat[0] = jnp.concatenate([hi, hi, lo], axis=1)

    act_copy = lambda sem, ys, i, z_to, y_to: send(
        r.act2.at[ys, i], r.act2.at[ys, i], r.act_s.at[sem, i], r.act_r.at[ys, i], (z_to * ny + y_to, c)
    )
    act_up = lambda i: act_copy(0, y, i, lax.min(z + 1, nz - 1), y)
    act_down = lambda i: act_copy(1, y, i, lax.max(z - 1, 0), y)
    act_side = lambda i: act_copy(2, y, i, z, 1 - y)

    def act_hand_on(i):
        pl.when((z >= c) & (z < nz - 1))(lambda: act_up(i).start())
        pl.when((z <= c) & (z > 0))(lambda: act_down(i).start())
        act_side(i).start()

    def second_act(i):
        val = val_of(i)
        act, slope = silu_and_slope((r.sums[i] - center2) * rs2 * gain2 + shift2)
        r.slope2[i] = slope * val
        r.own2[i] = act * val

    def far_to_core(j):
        zs = nearest(z, lax.div(j, 2))
        pl.when(lax.rem(j, 2) == 1)(lambda: fars.got(zs, 1 - y))
        call_copy(1, far, image(j)).start()

    away = lax.max(z - c, c - z)

    def act_step(t):
        for i in range(nd):

            @pl.when((away > 0) & (t == lax.div(16 + 8 * away + 5 * i, 4)))
            def _():
                act_copy(0, y, i, z, 1 - y).wait_recv()
                act_hand_on(i)

    pair = lambda s, q: r.dall.at[s, pl.ds(2 * q, 2)]
    grads = Line(p, lambda s: pair(s, c), r.d_s, r.d_r)
    to_far = lambda s, q: send(pair(s, q), pair(s, q), r.far_s.at[s], r.far_r.at[s], (d, far))
    to_core = lambda lane, s, q: send(pair(s, q), pair(s, q), r.core_s.at[lane, s], r.core_r.at[lane, s], (d, across))

    def over_chan_too(s):
        to_far(s, c).start()
        to_core(0, s, c).start()

    def meet_sides(step):
        def one(zs):
            grads.got(zs, 1 - y)
            over_chan_too(zs * ny + 1 - y)

        pl.when(z >= step)(lambda: one(lax.max(z - step, 0)))
        if step > 0:
            pl.when(z + step < nz)(lambda: one(lax.min(z + step, nz - 1)))

    hi, lo = split(r.a1[...].T)
    r.bm[0], r.bm[1] = hi, lo
    ins_grad = ImageSum(p, r.inp, r.inn, r.inc, r.inw, r.i_s1, r.i_r1, r.i_s2, r.i_r2)
    r.add1[...] = jnp.zeros_like(r.add1)
    r.add2[...] = jnp.zeros_like(r.add2)

    def inner_grad(i):
        second_act(i)
        dpre = (r.sums[nd + i] + factor * r.sums[2 * nd + i]) * r.slope2[i]
        dinner = gain2 * rs2 * dpre
        r.dall[d, i] = dinner
        r.add2[0] += dpre
        r.add2[1] += dpre * ((r.sums[i] - center2) * rs2)
        set_cols(shifts(dinner, side, -1))
        dact1 = im2col_dot((r.bm[0], r.bm[1]))
        r.inp[i] = dact1
        dpre1 = dact1 * r.slope1[i]
        r.add1[0] += dpre1
        r.add1[1] += dpre1 * ((r.xin[i] - center1) * rs1)

        @pl.when(z == c)
        def _():
            r.act2[y, i] = r.own2[i]
            act_hand_on(i)


    same = lambda j: j

    def start(j, _):
        pl.when(j == 2)(lambda: meet(fars, 3, lambda zs: far_side(zs).start()))
        first_map(j, gain1, shift1)
        chan.advance(nd + j, nd, change_item)
        chan.advance(j, nd, same)
        return 0

    def steady(j, _):
        first_map(j, gain1, shift1)
        chan.advance(j, nd, same)
        inner_grad(j - 4)
        far_to_core(j - 4)
        act_step(j)
        return 0

    def end(j, _):
        chan.advance(j, nd, same)
        inner_grad(j - 4)
        ins_grad.near(j - nd).start()
        far_to_core(j - 4)
        act_step(j)
        return 0

    lax.fori_loop(0, 4, start, 0)
    lax.fori_loop(4, nd, steady, 0)
    lax.fori_loop(nd, nd + 4, end, 0)
    grads.hand_on(z)
    sh1, gg1 = lanes_sum(r.add1[0]), lanes_sum(r.add1[1])
    sh2, gg2 = lanes_sum(r.add2[0]), lanes_sum(r.add2[1])

    pad = jnp.zeros((1, cb - db), F32)
    wide = lambda col: jnp.concatenate([to_row(col), pad], axis=1)
    r.vec[...] = stacked([to_row(sh1), to_row(gg1), wide(sh2), wide(gg2)], cb)
    vectors = ToAll("dp", nd, r.vec, r.vecs, r.vec_s, r.vec_r)
    vectors.start()

    def kernel_grad(images, left_of, rights_of, between=None):
        for j, i in enumerate(images):
            lanes = slice(3 * j * px, 3 * (j + 1) * px)
            for t, m in enumerate(shifts(left_of(i), side)):
                hi, lo = split(m)
                r.left[t * cb : (t + 1) * cb, lanes] = jnp.concatenate([hi, hi, lo], axis=1)
            at = 0
            for v in rights_of(i):
                n = v.shape[0]
                hi, lo = split(v)
                r.right[at : at + n, lanes] = jnp.concatenate([hi, lo, hi], axis=1)
                at += n

        def add(m, _):
            third = pl.ds(pl.multiple_of(m * 3 * cb, 16), 3 * cb)
            r.stage[third] += dot_nt(r.left[third], r.right[...])
            if between is not None:
                between(m)
            return 0

        lax.fori_loop(0, 3, add, 0)

    r.stage[...] = jnp.zeros_like(r.stage)

    def second_kernel(q, _):
        zs = nearest(z, q)
        for j in range(2):
            act_copy(0, 1 - y, 2 * q + j, z, 1 - y).wait_recv()
            call_copy(0, across, 2 * q + j).wait_recv()
            call_copy(1, last, 2 * q + j).wait_recv()

        def between(m):
            act_step(nd + 4 + 3 * q + m)

            for o in range(nz):
                pl.when(3 * q + m == 2 * o + 5)(lambda: ins_grad.spread(o))
            for step in range(1, nz):
                pl.when((q == step) & (m == 0))(lambda: meet(grads, step, lambda zs: over_chan_too(zs * ny + y)))
                pl.when((q == step) & (m == 2))(lambda: meet_sides(step - 1))

        kernel_grad(
            [2 * q, 2 * q + 1],
            lambda i: jnp.concatenate([r.act2[0, i], r.act2[1, i]], axis=0),
            lambda i: [r.call[j, i] for j in range(nc)],
            between,
        )
        return 0

    lax.fori_loop(0, nz, second_kernel, 0)
    g2_copy = pltpu.make_async_copy(r.stage, r.g2_out, r.g2_sem)
    g2_copy.start()

    r.block_out[...] = ((r.xin[d] + outs.total()) * mine).T
    meet_sides(nz - 1)
    back = lambda j: send(r.xs.at[lax.rem(c + j, nc)], r.rx.at[c], r.in_s.at[j], r.in_r.at[c], (d, lax.rem(c + j, nc)))

    def input_rows():
        grad = (gain1 * rs1 * (ins_grad.total() * r.slope1[d]) + r.call[c, d]).T
        for j in range(nc):
            r.xs[j] = grad[j * rows : (j + 1) * rows]
        for j in range(1, nc):
            back(j).start()
        r.rx[c] = r.xs[c]

    g2_copy.wait()
    r.stage[...] = jnp.zeros_like(r.stage)

    def first_kernel(j, _):
        @pl.when(j == 1)
        def _():
            for o in range(1, nd):
                to_core(0, lax.rem(d + o, nd), across).wait_recv()

        @pl.when(j == 2)
        def _():
            for o in range(1, nd):
                s = lax.rem(d + o, nd)
                to_far(s, far).wait_recv()
                to_core(1, s, far).start()

        @pl.when(j == 3)
        def _():
            for o in range(1, nd):
                to_core(1, lax.rem(d + o, nd), last).wait_recv()

        q = jnp.where(j == 0, c, jnp.where(j == 1, across, jnp.where(j == 2, far, last)))

        def between(m):
            pl.when((j == 2) & (m == 1))(input_rows)

        kernel_grad([2 * q, 2 * q + 1], lambda i: r.act1[i], lambda i: [r.dall[s, i] for s in range(nd)], between)
        return 0

    lax.fori_loop(0, nc, first_kernel, 0)
    g1_copy = pltpu.make_async_copy(r.stage, r.g1_out, r.g1_sem)
    g1_copy.start()

    vectors.finish()
    total = vectors.total()
    per = cb // db
    rows_of = lambda j: jnp.concatenate([r.vecs[per * c + q, j : j + 1, :db] for q in range(per)], axis=1)
    r.small[...] = stacked([total[0:1], total[1:2], rows_of(2), rows_of(3), jnp.broadcast_to(norm, (1, cb))], cb)
    for j in range(1, nc):
        back(j).wait_send()
        other = lax.rem(c + j, nc)
        send(r.xs.at[other], r.rx.at[other], r.in_s.at[0], r.in_r.at[other], (d, other)).wait_recv()
    for j in range(nc):
        r.input_grad[:, j * cb : (j + 1) * cb] = r.rx[j]

    own_cot(c).wait_send()
    for line in (ins, cots, fars, grads):
        line.drain()
    for zs in range(nz):
        far_side(zs).wait_send()

    @pl.when(c == owner)
    def _():
        for j in range(1, nc):
            piece(j).wait_send()

    def sent(i, _):
        call_copy(0, c, i).wait_send()
        call_copy(1, far, i).wait_send()
        pl.when((z >= c) & (z < nz - 1))(lambda: act_up(i).wait_send())
        pl.when((z <= c) & (z > 0))(lambda: act_down(i).wait_send())
        act_side(i).wait_send()
        return 0

    lax.fori_loop(0, nd, sent, 0)
    for j in range(1, nd):
        s = lax.rem(d + j, nd)
        to_far(s, c).wait_send()
        to_core(0, s, c).wait_send()
        to_core(1, s, far).wait_send()
    g1_copy.wait()


def close_kernel(pieces, small, block_in, rows_in, first_in, second_in, block_out, rows_out, first_out, second_out,
                 gg1, sh1, gg2, sh2, norm, first, second, vec, sems, side_sems):
    cut = first_in.shape[0] // pieces
    legs = []
    for j in range(pieces):
        part = pl.ds(j * cut, cut)
        for k, (src, mid, dst) in enumerate(((second_in, second, second_out), (first_in, first, first_out))):
            legs.append((
                pltpu.make_async_copy(src.at[part], mid.at[part], sems.at[0, k, j]),
                pltpu.make_async_copy(mid.at[part], dst.at[part], sems.at[1, k, j]),
            ))
    sides = [pltpu.make_async_copy(a, b, side_sems.at[j])
             for j, (a, b) in enumerate(((small, vec), (block_in, block_out), (rows_in, rows_out)))]
    for cp in sides:
        cp.start()
    for come, _ in legs:
        come.start()
    sides[0].wait()
    for j, ref in enumerate((sh1, gg1, sh2, gg2)):
        ref[...] = vec[j : j + 1].reshape(vec.shape[1])
    norm[0] = jnp.sum(vec[4:5, 0:1])
    for come, go in legs:
        come.wait()
        go.start()
    for _, go in legs:
        go.wait()
    for cp in sides[1:]:
        cp.wait()


def fused_on_device(p, image_rows, groups, conv_first, conv_second, gain_first, shift_first, gain_second, shift_second, cotangent):
    cb, px = p.cb, p.px
    rows = px // p.nc
    scratch = scratch_of(p)
    out = lambda *s: jax.ShapeDtypeStruct(s, F32)
    any_, vmem, smem = (pl.BlockSpec(memory_space=m) for m in (pl.ANY, VMEM, SMEM))
    large = (out(px, cb), out(rows, p.ch), out(9 * cb, p.ch), out(9 * cb, p.ch))
    block_out, input_grad, g1, g2, small = pl.pallas_call(
        functools.partial(step_kernel, p, ARGS + OUTS + tuple(scratch)),
        out_shape=large + (out(8, cb),),
        in_specs=[vmem, vmem, any_, any_, vmem, vmem, vmem, vmem, smem],
        out_specs=(vmem, vmem, any_, any_, vmem),
        scratch_shapes=list(scratch.values()),
        compiler_params=pltpu.CompilerParams(collective_id=0, has_side_effects=True, vmem_limit_bytes=LIMIT),
    )(
        image_rows.reshape(rows, p.ch), cotangent.reshape(px, cb), conv_first.reshape(9, cb, p.ch),
        conv_second.reshape(9, cb, p.ch), gain_first, shift_first, gain_second, shift_second, groups,
    )
    pieces = 6
    block_out, input_grad, g1, g2, gg1, sh1, gg2, sh2, norm = pl.pallas_call(
        functools.partial(close_kernel, pieces),
        out_shape=large + (out(cb),) * 4 + (out(1),),
        in_specs=[any_] * 5,
        out_specs=(vmem, vmem, any_, any_) + (vmem,) * 4 + (smem,),
        scratch_shapes=[VMEM((9 * cb, p.ch), F32), VMEM((9 * cb, p.ch), F32), VMEM((8, cb), F32), DMA((2, 2, pieces)), DMA((3,))],
        compiler_params=pltpu.CompilerParams(vmem_limit_bytes=LIMIT),
    )(small, block_out, input_grad, g1, g2)
    return (
        block_out.reshape(cotangent.shape), input_grad.reshape(image_rows.shape),
        g1.reshape(conv_first.shape), g2.reshape(conv_second.shape), gg1, sh1, gg2, sh2, norm.reshape(()),
    )


def valid_pixels(groups, extent_full):
    places = jnp.arange(extent_full, dtype=jnp.int32)
    extent = jnp.where(groups == 1, extent_full, extent_full // 2).astype(jnp.int32)
    inside = places[None, :] < extent[:, None]
    return (inside[:, :, None] & inside[:, None, :]).astype(jnp.float32)[..., None]


def convolve(values, kernel):
    return lax.conv_general_dilated(
        values,
        kernel,
        (1, 1),
        "SAME",
        dimension_numbers=("NHWC", "HWIO", "NHWC"),
        precision=lax.Precision.HIGHEST,
    )


def silu_slope(preact):
    sigmoid = jax.nn.sigmoid(preact)
    return sigmoid * (1.0 + preact * (1.0 - sigmoid))


def batch_moments(values, validity):
    summed, squares, pixels = lax.psum(
        (
            jnp.sum(values * validity, axis=(0, 1, 2)),
            jnp.sum(validity * values * values, axis=(0, 1, 2)),
            jnp.sum(validity),
        ),
        "dp",
    )
    center = summed / pixels
    spread = squares / pixels - center * center
    return (center, lax.rsqrt(spread + epsilon), pixels)


def project_over_chan(values, kernel):
    return lax.psum_scatter(convolve(values, kernel), "chan", scatter_dimension=3, tiled=True)


def conv_backward(upstream, values, kernel):
    columns = lax.all_gather(upstream, "chan", axis=3, tiled=True)
    offset = jnp.int32(0)
    inputs_grad = jnp.zeros_like(values)
    kernel_grad = jnp.zeros_like(kernel)
    breadth = columns.shape[3]
    kernel_part = lax.dynamic_slice_in_dim(kernel, offset, breadth, 3)
    primal, pull = jax.vjp(convolve, values, kernel_part)
    values_part, kernel_part_grad = pull(columns)
    kernel_grad = lax.dynamic_update_slice_in_dim(kernel_grad, kernel_part_grad, offset, 3)
    return (inputs_grad + values_part, kernel_grad)


def batch_sums(dpre, scaled):
    return lax.psum((jnp.sum(dpre, axis=(0, 1, 2)), jnp.sum(dpre * scaled, axis=(0, 1, 2))), "dp")


def plain_on_device(
    image_rows,
    groups,
    conv_first,
    conv_second,
    gain_first,
    shift_first,
    gain_second,
    shift_second,
    cotangent,
):
    inputs = lax.all_to_all(image_rows, "chan", split_axis=3, concat_axis=1, tiled=True)
    validity = valid_pixels(groups, inputs.shape[1])
    cot_valid = cotangent * validity
    center_one, rscale_one, pixels = batch_moments(inputs, validity)
    scaled_one = (inputs - center_one) * rscale_one
    pre_one = scaled_one * gain_first + shift_first
    act_one = jax.nn.silu(pre_one) * validity
    inner = project_over_chan(act_one, conv_first) * validity
    center_two, rscale_two, pixels_again = batch_moments(inner, validity)
    scaled_two = (inner - center_two) * rscale_two
    pre_two = scaled_two * gain_second + shift_second
    act_two = jax.nn.silu(pre_two) * validity
    block_out = inputs * validity + project_over_chan(act_two, conv_second) * validity
    dact_two, kernel_two_part = conv_backward(cot_valid, act_two, conv_second)
    dpre_two = dact_two * validity * silu_slope(pre_two)
    shift_two_grad, gain_two_grad = batch_sums(dpre_two, scaled_two)
    dinner = (
        gain_second
        * rscale_two
        * (dpre_two - validity * (shift_two_grad + scaled_two * gain_two_grad) / pixels)
    )
    dact_one, kernel_one_part = conv_backward(dinner, act_one, conv_first)
    dpre_one = dact_one * validity * silu_slope(pre_one)
    shift_one_grad, gain_one_grad = batch_sums(dpre_one, scaled_one)
    small_squares = (
        jnp.sum(gain_one_grad**2)
        + jnp.sum(shift_one_grad**2)
        + jnp.sum(gain_two_grad**2)
        + jnp.sum(shift_two_grad**2)
    )
    kernel_one_sum, kernel_two_sum = lax.psum((kernel_one_part, kernel_two_part), "dp")
    local_sq = jnp.sum(kernel_one_sum**2) + jnp.sum(kernel_two_sum**2) + small_squares
    squares = lax.psum(local_sq, "chan")
    factor = sam_radius * lax.rsqrt(squares + norm_floor)
    kernel_one = conv_first + factor * kernel_one_sum
    kernel_two = conv_second + factor * kernel_two_sum
    grad_norm = jnp.sqrt(squares)
    moved_gain_one = gain_first + factor * gain_one_grad
    moved_shift_one = shift_first + factor * shift_one_grad
    moved_gain_two = gain_second + factor * gain_two_grad
    moved_shift_two = shift_second + factor * shift_two_grad
    pre_one_new = scaled_one * moved_gain_one + moved_shift_one
    act_one_new = jax.nn.silu(pre_one_new) * validity
    inner_new = project_over_chan(act_one_new, kernel_one) * validity
    scaled_two_new = (inner_new - center_two) * rscale_two
    pre_two_new = scaled_two_new * moved_gain_two + moved_shift_two
    act_two_new = jax.nn.silu(pre_two_new) * validity
    dact_two_new, kernel_two_grad = conv_backward(cot_valid, act_two_new, kernel_two)
    dpre_two_new = dact_two_new * validity * silu_slope(pre_two_new)
    gain_two_new_grad = jnp.sum(dpre_two_new * scaled_two_new, axis=(0, 1, 2))
    shift_two_new_grad = jnp.sum(dpre_two_new, axis=(0, 1, 2))
    dinner_new = moved_gain_two * rscale_two * dpre_two_new
    dact_one_new, kernel_one_grad = conv_backward(dinner_new, act_one_new, kernel_one)
    dpre_one_new = dact_one_new * validity * silu_slope(pre_one_new)
    gain_one_new_grad = jnp.sum(dpre_one_new * scaled_one, axis=(0, 1, 2))
    shift_one_new_grad = jnp.sum(dpre_one_new, axis=(0, 1, 2))
    inputs_grad = moved_gain_one * rscale_one * dpre_one_new + cot_valid
    input_grad = lax.all_to_all(inputs_grad, "chan", split_axis=1, concat_axis=3, tiled=True)
    (
        kernel_one_grad,
        kernel_two_grad,
        gain_one_new_grad,
        shift_one_new_grad,
        gain_two_new_grad,
        shift_two_new_grad,
    ) = lax.psum(
        (
            kernel_one_grad,
            kernel_two_grad,
            gain_one_new_grad,
            shift_one_new_grad,
            gain_two_new_grad,
            shift_two_new_grad,
        ),
        "dp",
    )
    return (
        block_out,
        input_grad,
        kernel_one_grad,
        kernel_two_grad,
        gain_one_new_grad,
        shift_one_new_grad,
        gain_two_new_grad,
        shift_two_new_grad,
        grad_norm,
    )


def solution(mesh):
    nd, nc = mesh.shape["dp"], mesh.shape["chan"]

    def on_device(image_rows, *rest):
        images, side, channels = image_rows.shape[0], image_rows.shape[2], image_rows.shape[3]
        fits = images == 1 and nc == 4 and nd == 2 * nc and channels // nd % 16 == 0 and side * side == 256
        if not fits:
            return plain_on_device(image_rows, *rest)
        return fused_on_device(Plan(nd, nc, channels, side), image_rows, *rest)

    return jax.shard_map(
        on_device,
        mesh=mesh,
        in_specs=(
            P("dp", "chan", None, None),
            P("dp"),
            P(None, None, "chan", None),
            P(None, None, "chan", None),
            P("chan"),
            P("chan"),
            P("chan"),
            P("chan"),
            P("dp", None, None, "chan"),
        ),
        out_specs=(
            P("dp", None, None, "chan"),
            P("dp", "chan", None, None),
            P(None, None, "chan", None),
            P(None, None, "chan", None),
            P("chan"),
            P("chan"),
            P("chan"),
            P("chan"),
            P(),
        ),
        check_vma=False,
    )
```

```python
import functools
import types

import jax
import jax.numpy as jnp
from jax import lax
from jax.experimental import pallas as pl
from jax.experimental.pallas import tpu as pltpu
from jax.sharding import PartitionSpec as P

epsilon = 1e-05
sam_radius = 0.05
norm_floor = 1e-06
MESH = pl.DeviceIdType.MESH
F32, BF16 = jnp.float32, jnp.bfloat16
VMEM, SMEM = pltpu.VMEM, pltpu.SMEM
DMA = pltpu.SemaphoreType.DMA
LIMIT = 60 << 20


class Plan:
    def __init__(self, nd, nc, channels, side):
        self.nd, self.nc, self.ch, self.side = nd, nc, channels, side
        self.cb, self.db, self.px = channels // nc, channels // nd, side * side
        self.ny = 2
        self.nz = nd // 2


def split(v):
    hi = v.astype(BF16)
    return hi, (v - hi.astype(F32)).astype(BF16)


def dot(a, b):
    return lax.dot_general(a, b, (((1,), (0,)), ((), ())), preferred_element_type=F32)


def dot_nt(a, b):
    return lax.dot_general(a, b, (((1,), (1,)), ((), ())), preferred_element_type=F32)


def edge_masks(side, px):
    lane = lax.broadcasted_iota(jnp.int32, (1, px), 1)
    col = lax.rem(lane, side)
    row = lax.div(lane, side)
    one = jnp.ones((1, px), F32)
    zero = jnp.zeros((1, px), F32)
    rows = {-1: jnp.where(row >= 1, one, zero), 0: None, 1: jnp.where(row < side - 1, one, zero)}
    cols = {-1: jnp.where(col >= 1, one, zero), 0: None, 1: jnp.where(col < side - 1, one, zero)}
    return rows, cols


def moved(v, lanes, mask):
    if lanes:
        v = pltpu.roll(v, (-lanes) % v.shape[1], axis=1)
    return v if mask is None else v * mask


def shifts(v, side, sign=1):
    rows, cols = edge_masks(side, v.shape[1])
    by_col = {s: moved(v, s, cols[s]) for s in (-1, 0, 1)}
    return [moved(by_col[sign * s], sign * r * side, rows[sign * r]) for r in (-1, 0, 1) for s in (-1, 0, 1)]


def gather_taps(prod, side, n):
    rows, cols = edge_masks(side, prod.shape[1])
    total = None
    for j, s in enumerate((-1, 0, 1)):
        part = None
        for i, r in enumerate((-1, 0, 1)):
            t = 3 * i + j
            m = moved(prod[t * n : (t + 1) * n], r * side, rows[r])
            part = m if part is None else part + m
        m = moved(part, s, cols[s])
        total = m if total is None else total + m
    return total


def sigmoid(t):
    return 1.0 / (1.0 + jnp.exp(-t))


def silu_and_slope(pre):
    s = sigmoid(pre)
    return pre * s, s * (1.0 + pre * (1.0 - s))


def lanes_sum(v):
    return jnp.sum(v, axis=1, keepdims=True)


def valid_map(flag, side, px):
    lane = lax.broadcasted_iota(jnp.int32, (1, px), 1)
    half = (lax.rem(lane, side) < side // 2) & (lax.div(lane, side) < side // 2)
    return jnp.where(half, jnp.ones((1, px), F32), flag)


def diagonal(n):
    return lax.broadcasted_iota(jnp.int32, (n, n), 0) == lax.broadcasted_iota(jnp.int32, (n, n), 1)


def to_row(col):
    return jnp.sum(jnp.where(diagonal(col.shape[0]), col, 0.0), axis=0, keepdims=True)


def to_col(row):
    return jnp.sum(jnp.where(diagonal(row.shape[1]), row, 0.0), axis=1, keepdims=True)


def stacked(rows, n):
    at = lax.broadcasted_iota(jnp.int32, (8, n), 0)
    out = jnp.zeros((8, n), F32)
    for k, row in enumerate(rows):
        out = jnp.where(at == k, row, out)
    return out


def send(src, dst, ss, rs, device):
    return pltpu.make_async_remote_copy(
        src_ref=src, dst_ref=dst, send_sem=ss, recv_sem=rs, device_id=device, device_id_type=MESH
    )


def here():
    return lax.axis_index("dp"), lax.axis_index("chan")


def greet(p):
    d, c = here()
    barrier = pltpu.get_barrier_semaphore()
    for j in range(1, p.nd):
        pl.semaphore_signal(barrier, inc=1, device_id=(lax.rem(d + j, p.nd), c), device_id_type=MESH)
    for j in range(1, p.nc):
        pl.semaphore_signal(barrier, inc=1, device_id=(d, lax.rem(c + j, p.nc)), device_id_type=MESH)
    pl.semaphore_wait(barrier, p.nd - 1 + p.nc - 1)


class ToAll:
    def __init__(self, axis, n, tile, slots, ss, rs):
        d, c = here()
        self.n, self.tile, self.slots, self.ss, self.rs = n, tile, slots, ss, rs
        self.me = d if axis == "dp" else c
        self.device = (lambda o: (o, c)) if axis == "dp" else (lambda o: (d, o))

    def start(self):
        self.slots[self.me] = self.tile[...]
        for j in range(1, self.n):
            to = lax.rem(self.me + j, self.n)
            send(self.tile, self.slots.at[self.me], self.ss.at[j], self.rs.at[self.me], self.device(to)).start()

    def finish(self):
        for j in range(1, self.n):
            other = lax.rem(self.me + j, self.n)
            send(self.tile, self.slots.at[other], self.ss.at[j], self.rs.at[other], self.device(other)).wait()

    def total(self):
        total = self.slots[0]
        for j in range(1, self.n):
            total = total + self.slots[j]
        return total


class Line:
    def __init__(self, p, view, ss, rs, sides=True):
        self.p, self.view, self.ss, self.rs, self.sides = p, view, ss, rs, sides
        d, self.c = here()
        self.z, self.y = lax.div(d, p.ny), lax.rem(d, p.ny)

    def copy(self, zs, sem, z_to, y_to):
        slot = zs * self.p.ny + self.y
        return send(self.view(slot), self.view(slot), self.ss.at[sem, zs], self.rs.at[slot], (z_to * self.p.ny + y_to, self.c))

    def up(self, zs):
        return self.copy(zs, 0, lax.min(self.z + 1, self.p.nz - 1), self.y)

    def down(self, zs):
        return self.copy(zs, 1, lax.max(self.z - 1, 0), self.y)

    def side(self, zs):
        return self.copy(zs, 2, self.z, 1 - self.y)

    def got(self, zs, y):
        slot = zs * self.p.ny + y
        send(self.view(slot), self.view(slot), self.ss.at[0, 0], self.rs.at[slot], (self.z * self.p.ny + 1 - self.y, self.c)).wait_recv()

    def hand_on(self, zs):
        pl.when((zs <= self.z) & (self.z < self.p.nz - 1))(lambda: self.up(zs).start())
        pl.when((zs >= self.z) & (self.z > 0))(lambda: self.down(zs).start())
        if self.sides:
            self.side(zs).start()

    def drain(self):
        for zs in range(self.p.nz):
            pl.when((zs <= self.z) & (self.z < self.p.nz - 1))(lambda: self.up(zs).wait_send())
            pl.when((zs >= self.z) & (self.z > 0))(lambda: self.down(zs).wait_send())
            if self.sides:
                self.side(zs).wait_send()


def nearest(z, k):
    t = lax.div(z, 2)
    low = z + t * (3 - 2 * z)
    first = 1 - lax.min(lax.div(k, 2), 1)
    place = k + low * first * (1 - 2 * k)
    return place * (1 - 2 * t) + 3 * t


class ChanSum:
    def __init__(self, p, r):
        self.p, self.r = p, r
        d, c = here()
        k = lax.rem(c, 2)
        self.hb = p.db // 2
        self.across, self.far = (d, c + 1 - 2 * k), (d, lax.rem(c + 2, 4))
        self.mine = pl.multiple_of(k * self.hb, 8)
        self.yours = pl.multiple_of((1 - k) * self.hb, 8)

    def first(self, i):
        r = self.r
        return send(r.part.at[i, pl.ds(self.yours, self.hb)], r.near.at[i], r.cs1.at[i], r.cr1.at[i], self.across)

    def second(self, i):
        r = self.r
        return send(r.half.at[i], r.away.at[i], r.cs2.at[i], r.cr2.at[i], self.far)

    def third(self, i, rows):
        r = self.r
        mine = r.sums.at[i, pl.ds(self.mine, self.hb)]
        return send(mine, r.sums.at[i, pl.ds(rows, self.hb)], r.cs3.at[i], r.cr3.at[i], self.across)

    def chip(self, i):
        r = self.r
        self.first(i).wait()
        r.half[i] = r.part[i, pl.ds(self.mine, self.hb)] + r.near[i]
        self.second(i).start()

    def cross(self, i):
        r = self.r
        self.second(i).wait()
        r.sums[i, pl.ds(self.mine, self.hb)] = r.half[i] + r.away[i]
        self.third(i, self.mine).start()

    def done(self, i):
        self.third(i, self.yours).wait()

    def advance(self, j, n, item):
        at = lambda m: item(lax.clamp(0, m, n - 1))
        pl.when((j >= 1) & (j < n + 1))(lambda: self.chip(at(j - 1)))
        pl.when((j >= 3) & (j < n + 3))(lambda: self.cross(at(j - 3)))
        pl.when((j >= 4) & (j < n + 4))(lambda: self.done(at(j - 4)))


class ImageSum:
    def __init__(self, p, part, near, acc, away, s1, r1, s2, r2):
        self.p, self.part, self.buf1, self.acc, self.buf2 = p, part, near, acc, away
        self.s1, self.r1, self.s2, self.r2 = s1, r1, s2, r2
        d, self.c = here()
        self.z, self.y = lax.div(d, p.ny), lax.rem(d, p.ny)

    def near(self, zs):
        side = 1 - self.y
        return send(self.part.at[zs * self.p.ny + side], self.buf1.at[zs], self.s1.at[zs], self.r1.at[zs],
                    (self.z * self.p.ny + side, self.c))

    def away(self, zs, slot):
        return send(self.acc.at[zs], self.buf2.at[slot], self.s2.at[zs], self.r2.at[slot], (zs * self.p.ny + self.y, self.c))

    def spread(self, zs):
        self.near(zs).wait()
        self.acc[zs] = self.part[zs * self.p.ny + self.y] + self.buf1[zs]
        pl.when(zs != self.z)(lambda: self.away(zs, self.z).start())

    def total(self):
        total = self.acc[self.z]
        for j in range(1, self.p.nz):
            other = lax.rem(self.z + j, self.p.nz)
            self.away(other, other).wait()
            total = total + self.buf2[other]
        return total


def scratch_of(p):
    nd, nc, cb, db, px, nz, ny = p.nd, p.nc, p.cb, p.db, p.px, p.nz, p.ny
    rows = px // nc
    f = lambda *s: VMEM(s, F32)
    h = lambda *s: VMEM(s, BF16)
    return dict(
        k1w=f(9, cb, 256), k2w=f(9, db, p.ch), ks=f(nc, cb, 9 * db), b2=f(cb, 9 * db),
        a1=f(9 * db, cb), a2=f(9 * db, cb), g1=f(9 * db, cb), g2=f(9 * db, cb),
        a_cat=h(2, 9 * db, 3 * cb), bm=h(2, cb, 9 * db), b2m=h(2, cb, 9 * db), colh=h(2, 9 * db, px), coll=h(2, 9 * db, px),
        xs=f(nc, rows, cb), rx=f(nc, rows, cb), xin=f(nd, cb, px), act1=f(nd, cb, px), slope1=f(nd, cb, px),
        call=f(nc, nd, cb, px),
        part=f(3 * nd, db, px), near=f(3 * nd, db // 2, px), half=f(3 * nd, db // 2, px), away=f(3 * nd, db // 2, px),
        sums=f(3 * nd, db, px), slope2=f(nd, db, px), dpre=f(nd, db, px), add1=f(2, cb, px), add2=f(2, db, px),
        outp=f(nd, cb, px), outn=f(nz, cb, px), outc=f(nz, cb, px), outw=f(nz, cb, px),
        inp=f(nd, cb, px), inn=f(nz, cb, px), inc=f(nz, cb, px), inw=f(nz, cb, px),
        dall=f(nd, nd, db, px), act2=f(ny, nd, db, px), own2=f(nd, db, px), left=h(9 * cb, 6 * px), right=h(p.ch, 6 * px),
        stage=f(9 * cb, p.ch),
        par=f(8, cb), pars=f(nc, 8, cb), stat=f(8, cb), stats=f(nd, 8, cb), msg=f(8, cb), msgs=f(nd, 8, cb),
        sq=f(8, 128), sqs=f(nc, 8, 128), vec=f(8, cb), vecs=f(nd, 8, cb),
        k1_sem=DMA, k2_sem=DMA, g1_sem=DMA, g2_sem=DMA,
        xs_s=DMA((nc,)), xs_r=DMA((nc,)), ks_s=DMA((nc,)), ks_r=DMA,
        par_s=DMA((nc,)), par_r=DMA((nc,)), stat_s=DMA((nd,)), stat_r=DMA((nd,)), msg_s=DMA((nd,)), msg_r=DMA((nd,)),
        sq_s=DMA((nc,)), sq_r=DMA((nc,)), vec_s=DMA((nd,)), vec_r=DMA((nd,)),
        x_s=DMA((3, nz)), x_r=DMA((nd,)), c_s=DMA((3, nz)), c_r=DMA((nd,)), d_s=DMA((3, nz)), d_r=DMA((nd,)),
        cs1=DMA((3 * nd,)), cr1=DMA((3 * nd,)), cs2=DMA((3 * nd,)), cr2=DMA((3 * nd,)), cs3=DMA((3 * nd,)), cr3=DMA((3 * nd,)),
        o_s1=DMA((nz,)), o_r1=DMA((nz,)), o_s2=DMA((nz,)), o_r2=DMA((nz,)),
        i_s1=DMA((nz,)), i_r1=DMA((nz,)), i_s2=DMA((nz,)), i_r2=DMA((nz,)),
        call_s=DMA((2, nd)), call_r=DMA((2, nd)), own_s=DMA, f_s=DMA((3, nz)), f_r=DMA((nd,)), col_s=DMA((nz,)), act_s=DMA((3, nd)), act_r=DMA((ny, nd)),
        far_s=DMA((nd,)), far_r=DMA((nd,)), core_s=DMA((2, nd)), core_r=DMA((2, nd)), in_s=DMA((nc,)), in_r=DMA((nc,)),
    )


FARS = (3, 6, 12)
OUTS_AT = (9, 10, 11, 13)
ACT = (44, 8, 4)
LINE_AT = (5, 9, 12)
SIDE_AT = (6, 11, 14, 17)
NEAR_AT = 14
SUMS_AT = (18, 20, 22, 24)
ROWS_AT = 28

ARGS = ("x", "cot", "k1", "k2", "gain1", "shift1", "gain2", "shift2", "groups")
OUTS = ("block_out", "input_grad", "g1_out", "g2_out", "small")


def step_kernel(p, names, *refs):
    r = types.SimpleNamespace(**dict(zip(names, refs)))
    cb, db, px, side, nd, nc, nz, ny = p.cb, p.db, p.px, p.side, p.nd, p.nc, p.nz, p.ny
    d, c = here()
    z, y = lax.div(d, ny), lax.rem(d, ny)
    k = lax.rem(c, 2)
    far, across = lax.rem(c + 2, 4), c + 1 - 2 * k
    last = 6 - c - far - across
    rows = px // nc
    owner = (1 - lax.div(z, 2)) * (2 - 2 * lax.rem(z, 2)) + lax.div(z, 2) * (1 + 2 * lax.rem(z, 2))
    origin = lambda c: (1 - c // 2) * (1 + c % 2) + c // 2 * 3 * (c % 2)
    start_z = (1 - lax.div(c, 2)) * (1 + k) + lax.div(c, 2) * 3 * k
    first = owner * cb + y * db
    slots = [origin(q) * ny + j for q in range(nc) for j in range(ny)]
    image = lambda j: nearest(z, lax.div(j, 2)) * ny + y + lax.rem(j, 2) * (1 - 2 * y)

    base = lax.min(lax.div(first, 128), (p.ch - 256) // 128) * 128
    k1_copy = pltpu.make_async_copy(r.k1.at[:, :, pl.ds(pl.multiple_of(base, 128), 256)], r.k1w, r.k1_sem)
    k1_copy.start()
    k2_rows = pl.ds(pl.multiple_of(y * db, 8), db)
    k2_copy = pltpu.make_async_copy(r.k2.at[:, k2_rows], r.k2w, r.k2_sem)
    pl.when(c == owner)(lambda: k2_copy.start())
    greet(p)

    for j in range(nc):
        r.xs[j] = r.x[:, j * cb : (j + 1) * cb]
    a2a = lambda j: send(r.xs.at[lax.rem(c + j, nc)], r.rx.at[c], r.xs_s.at[j], r.xs_r.at[c], (d, lax.rem(c + j, nc)))
    for j in range(1, nc):
        a2a(j).start()
    r.rx[c] = r.xs[c]
    r.par[...] = stacked([r.gain2[...].reshape(1, cb), r.shift2[...].reshape(1, cb)], cb)
    params = ToAll("chan", nc, r.par, r.pars, r.par_s, r.par_r)
    params.start()
    flag = jnp.full((1, 1), jnp.where(r.groups[0] == 1, 1.0, 0.0), F32)
    mine = valid_map(flag, side, px)
    r.call[c, d] = r.cot[...].T * mine

    def meet(line, step, then=None):
        def one(zs):
            line.got(zs, y)
            line.hand_on(zs)
            if then is not None:
                then(zs)

        pl.when(z >= step)(lambda: one(lax.max(z - step, 0)))
        pl.when(z + step < nz)(lambda: one(lax.min(z + step, nz - 1)))

    cots = Line(p, lambda s: r.call.at[c, s], r.c_s, r.c_r)
    cots.hand_on(z)
    own_cot = lambda q: send(r.call.at[q, d], r.call.at[q, d], r.own_s, r.f_r.at[d], (d, far))
    fars = Line(p, lambda s: r.call.at[far, s], r.f_s, r.f_r, False)
    column = lambda q, zs: send(
        r.call.at[q, zs * ny + 1 - y], r.call.at[q, zs * ny + 1 - y], r.col_s.at[zs], r.f_r.at[zs * ny + 1 - y], (d, far)
    )
    call_copy = lambda lane, q, i: send(
        r.call.at[q, i], r.call.at[q, i], r.call_s.at[lane, i], r.call_r.at[lane, i], (d, across)
    )

    @pl.when(c == owner)
    def _():
        k2_copy.wait()
        for j in range(nc):
            r.ks[j] = r.k2w[:, :, j * cb : (j + 1) * cb].reshape(9 * db, cb).T

    for j in range(1, nc):
        a2a(j).wait_send()
        other = lax.rem(c + j, nc)
        send(r.xs.at[other], r.rx.at[other], r.xs_s.at[j], r.xs_r.at[other], (d, other)).wait_recv()
    r.xin[d] = r.rx[...].reshape(px, cb).T
    ins = Line(p, lambda s: r.xin.at[s], r.x_s, r.x_r)
    ins.hand_on(z)

    count = lanes_sum(mine)
    total = lanes_sum(r.xin[d] * mine)
    off = r.xin[d] - total / count
    r.stat[...] = stacked([to_row(total), to_row(lanes_sum(mine * off * off)), jnp.broadcast_to(flag, (1, cb))], cb)
    stats = ToAll("dp", nd, r.stat, r.stats, r.stat_s, r.stat_r)
    stats.start()

    piece = lambda j: send(r.ks.at[lax.rem(c + j, nc)], r.b2, r.ks_s.at[j], r.ks_r, (d, lax.rem(c + j, nc)))

    @pl.when(c == owner)
    def _():
        for j in range(1, nc):
            piece(j).start()

    k1_copy.wait()
    turn = lax.rem(256 - (first - base), 256)
    b1 = jnp.concatenate([pltpu.roll(r.k1w[t], turn, axis=1)[:, :db] for t in range(9)], axis=1)
    hi, lo = split(b1)
    r.bm[0], r.bm[1] = hi, lo
    r.a1[...] = b1.T
    hi, lo = split(r.a1[...])
    r.a_cat[0] = jnp.concatenate([hi, hi, lo], axis=1)

    meet(cots, 1)
    own_cot(c).start()
    stats.finish()

    def val_of(i):
        return valid_map(r.stats[i, 2:3, 0:1], side, px)

    counts = [jnp.sum(val_of(i), keepdims=True) for i in range(nd)]
    pixels = functools.reduce(jnp.add, counts)
    center = functools.reduce(jnp.add, [r.stats[i, 0:1] for i in range(nd)]) / pixels
    spread = [r.stats[i, 1:2] + counts[i] * (r.stats[i, 0:1] / counts[i] - center) ** 2 for i in range(nd)]
    center1, rs1 = to_col(center), to_col(lax.rsqrt(functools.reduce(jnp.add, spread) / pixels + epsilon))
    gain1, shift1 = to_col(r.gain1[...].reshape(1, cb)), to_col(r.shift1[...].reshape(1, cb))

    chan = ChanSum(p, r)

    def first_map(i, gain, shift):
        val = val_of(i)
        act, slope = silu_and_slope((r.xin[i] - center1) * rs1 * gain + shift)
        act = act * val
        r.act1[i], r.slope1[i] = act, slope * val
        ah, al = split(act)
        prod = dot(r.a_cat[0], jnp.concatenate([ah, al, ah], axis=0))
        r.part[i] = gather_taps(prod, side, db) * val
        chan.first(i).start()

    def second_back(i, first):
        ch, cl = split(r.call[c, i])
        prod = dot(r.a_cat[1], jnp.concatenate([ch, cl, ch], axis=0))
        r.part[first + i] = gather_taps(prod, side, db) * val_of(i)
        chan.first(first + i).start()

    def back_item(j):
        return nd + image(j)

    def set_back(a2):
        for t in range(9):
            hi, lo = split(a2[(8 - t) * db : (9 - t) * db])
            r.a_cat[1, t * db : (t + 1) * db] = jnp.concatenate([hi, hi, lo], axis=1)

    def second_block():
        @pl.when(c == owner)
        def _():
            r.b2[...] = r.ks[c]

        @pl.when(c != owner)
        def _():
            send(r.ks.at[0], r.b2, r.ks_s.at[0], r.ks_r, (d, owner)).wait_recv()

        r.a2[...] = r.b2[...].T
        set_back(r.a2)
        b2h, b2l = split(r.b2[...])
        r.b2m[0], r.b2m[1] = b2h, b2l

    def forward(kk, _):
        zs = nearest(z, kk)
        first_map(zs * ny + y, gain1, shift1)
        chan.advance(2 * kk, nd, image)
        meet(ins, kk + 1)
        pl.when(kk == 0)(lambda: meet(cots, 2))
        pl.when(kk == 1)(lambda: meet(cots, 3))
        pl.when(kk == 1)(second_block)
        ins.got(zs, 1 - y)
        first_map(zs * ny + 1 - y, gain1, shift1)
        chan.advance(2 * kk + 1, nd, image)

        @pl.when(kk > 0)
        def _():
            before = nearest(z, lax.max(kk - 1, 0))
            second_back(before * ny + y, nd)
            chan.advance(2 * kk - 2, nd, back_item)
            cots.got(before, 1 - y)
            second_back(before * ny + 1 - y, nd)
            chan.advance(2 * kk - 1, nd, back_item)

        return 0

    lax.fori_loop(0, nz, forward, 0)
    furthest = nearest(z, nz - 1)
    chan.advance(nd, nd, image)
    second_back(furthest * ny + y, nd)
    chan.advance(nd - 2, nd, back_item)
    chan.advance(nd + 1, nd, image)
    cots.got(furthest, 1 - y)
    second_back(furthest * ny + 1 - y, nd)
    chan.advance(nd - 1, nd, back_item)
    chan.advance(nd + 2, nd, image)
    chan.advance(nd, nd, back_item)
    chan.advance(nd + 3, nd, image)

    params.finish()
    both = [r.pars[owner, j : j + 1] for j in range(2)]
    gain2, shift2 = (to_col(jnp.where(y == 0, v[:, :db], v[:, cb - db :])) for v in both)

    def add_up(i, carry):
        return carry + lanes_sum(r.sums[i] * val_of(i))

    chan.advance(nd + 1, nd, back_item)
    center2 = lax.fori_loop(0, nd, add_up, jnp.zeros((db, 1), F32)) / pixels

    def add_squares(i, carry):
        off = r.sums[i] - center2
        return carry + lanes_sum(val_of(i) * off * off)

    chan.advance(nd + 2, nd, back_item)
    rs2 = lax.rsqrt(lax.fori_loop(0, nd, add_squares, jnp.zeros((db, 1), F32)) / pixels + epsilon)

    chan.advance(nd + 3, nd, back_item)
    own_cot(far).wait_recv()
    fars.hand_on(z)
    for zs in range(nz):
        column(c, zs).start()

    def inner_sums(i, carry):
        val = val_of(i)
        scaled = (r.sums[i] - center2) * rs2
        act, slope = silu_and_slope(scaled * gain2 + shift2)
        r.own2[i] = act * val
        dpre = r.sums[nd + i] * (slope * val)
        r.dpre[i] = dpre
        return carry[0] + lanes_sum(dpre), carry[1] + lanes_sum(dpre * scaled)

    zero = jnp.zeros((db, 1), F32)
    sh2, gg2 = lax.fori_loop(0, nd, inner_sums, (zero, zero))

    outs = ImageSum(p, r.outp, r.outn, r.outc, r.outw, r.o_s1, r.o_r1, r.o_s2, r.o_r2)

    def set_cols(w, maps):
        for t, m in enumerate(maps):
            hi, lo = split(m)
            r.colh[w, t * db : (t + 1) * db] = hi
            r.coll[w, t * db : (t + 1) * db] = lo

    def im2col_dot(w, which):
        return dot(which[0], r.colh[w]) + dot(which[0], r.coll[w]) + dot(which[1], r.colh[w])

    def wgrad(w, other):
        oh, ol = split(other)
        left = jnp.concatenate([r.colh[w], r.colh[w], r.coll[w]], axis=1)
        return dot_nt(left, jnp.concatenate([oh, ol, oh], axis=1))

    r.g1[...] = jnp.zeros_like(r.g1)
    r.g2[...] = jnp.zeros_like(r.g2)
    change_item = lambda j: 2 * nd + j

    def settle(t):
        for step in range(1, nz):
            pl.when(t == FARS[step - 1])(lambda: meet(fars, step))
        for zs in range(nz):
            pl.when(t == OUTS_AT[zs])(lambda: outs.spread(zs))

    def gradients(i, carry):
        scaled = (r.sums[i] - center2) * rs2
        dinner = gain2 * rs2 * (r.dpre[i] - val_of(i) * (sh2 + scaled * gg2) / pixels)
        set_cols(0, shifts(r.own2[i], side))
        set_cols(1, shifts(dinner, side, -1))
        r.outp[i] = im2col_dot(0, (r.b2m[0], r.b2m[1]))
        r.g2[...] += wgrad(0, r.call[c, i])
        r.g1[...] += wgrad(1, r.act1[i])
        dpre1 = im2col_dot(1, (r.bm[0], r.bm[1])) * r.slope1[i]
        scaled1 = (r.xin[i] - center1) * rs1
        pl.when(lax.rem(i, 2) == 1 - y)(lambda: outs.near(lax.div(i, 2)).start())
        call_copy(0, c, i).start()
        settle(i)
        return carry[0] + lanes_sum(dpre1), carry[1] + lanes_sum(dpre1 * scaled1)

    zero = jnp.zeros((cb, 1), F32)
    sh1, gg1 = lax.fori_loop(0, nd, gradients, (zero, zero))
    set_back(r.g2)

    square = jnp.sum(r.g1[...] * r.g1[...] + r.g2[...] * r.g2[...], keepdims=True)
    square = square + jnp.where(c == 0, jnp.sum(sh2 * sh2 + gg2 * gg2, keepdims=True), 0.0)
    r.msg[...] = stacked([to_row(sh1), to_row(gg1), jnp.broadcast_to(square, (1, cb))], cb)
    over_dp = ToAll("dp", nd, r.msg, r.msgs, r.msg_s, r.msg_r)
    over_dp.start()

    def change(j, _):
        second_back(j, 2 * nd)
        chan.advance(j, nd, change_item)
        return 0

    lax.fori_loop(0, nd // 2, change, 0)
    over_dp.finish()
    total = over_dp.total()
    sh1, gg1 = to_col(total[0:1]), to_col(total[1:2])
    square = total[2:3, 0:1] + jnp.sum(sh1 * sh1 + gg1 * gg1, keepdims=True)
    r.sq[...] = jnp.broadcast_to(square, (8, 128))
    over_chan = ToAll("chan", nc, r.sq, r.sqs, r.sq_s, r.sq_r)
    over_chan.start()
    lax.fori_loop(nd // 2, nd, change, 0)
    over_chan.finish()
    square = over_chan.total()[0:1, 0:1]
    norm = jnp.sqrt(square)
    factor = sam_radius * lax.rsqrt(square + norm_floor)

    gain1, shift1 = gain1 + factor * gg1, shift1 + factor * sh1
    gain2, shift2 = gain2 + factor * gg2, shift2 + factor * sh2
    r.a1[...] += factor * r.g1[...]
    hi, lo = split(r.a1[...])
    r.a_cat[0] = jnp.concatenate([hi, hi, lo], axis=1)

    act_copy = lambda sem, ys, i, z_to, y_to: send(
        r.act2.at[ys, i], r.act2.at[ys, i], r.act_s.at[sem, i], r.act_r.at[ys, i], (z_to * ny + y_to, c)
    )
    act_up = lambda i: act_copy(0, y, i, lax.min(z + 1, nz - 1), y)
    act_down = lambda i: act_copy(1, y, i, lax.max(z - 1, 0), y)
    act_side = lambda i: act_copy(2, y, i, z, 1 - y)

    def act_hand_on(i):
        pl.when((z >= start_z) & (z < nz - 1))(lambda: act_up(i).start())
        pl.when((z <= start_z) & (z > 0))(lambda: act_down(i).start())
        act_side(i).start()

    def second_act(i):
        val = val_of(i)
        act, slope = silu_and_slope((r.sums[i] - center2) * rs2 * gain2 + shift2)
        r.slope2[i] = slope * val
        r.own2[i] = act * val

    def far_to_core(j):
        zs = nearest(z, lax.div(j, 2))
        pl.when(lax.rem(j, 2) == 1)(lambda: column(far, zs).wait_recv())
        call_copy(1, far, image(j)).start()

    away = lax.max(z - start_z, start_z - z)

    def act_step(t):
        for i in range(nd):

            @pl.when((away > 0) & (t == lax.div(ACT[0] + ACT[1] * away + ACT[2] * i, 4)))
            def _():
                act_copy(0, y, i, z, 1 - y).wait_recv()
                act_hand_on(i)

    pair = lambda s, q: r.dall.at[s, pl.ds(2 * q, 2)]
    grads = Line(p, lambda s: pair(s, c), r.d_s, r.d_r)
    to_far = lambda s, q: send(pair(s, q), pair(s, q), r.far_s.at[s], r.far_r.at[s], (d, far))
    to_core = lambda lane, s, q: send(pair(s, q), pair(s, q), r.core_s.at[lane, s], r.core_r.at[lane, s], (d, across))

    def over_chan_too(s):
        to_far(s, c).start()
        to_core(0, s, c).start()

    def meet_sides(step):
        def one(zs):
            grads.got(zs, 1 - y)
            over_chan_too(zs * ny + 1 - y)

        pl.when(z >= step)(lambda: one(lax.max(z - step, 0)))
        if step > 0:
            pl.when(z + step < nz)(lambda: one(lax.min(z + step, nz - 1)))

    hi, lo = split(r.a1[...].T)
    r.bm[0], r.bm[1] = hi, lo
    ins_grad = ImageSum(p, r.inp, r.inn, r.inc, r.inw, r.i_s1, r.i_r1, r.i_s2, r.i_r2)
    r.add1[...] = jnp.zeros_like(r.add1)
    r.add2[...] = jnp.zeros_like(r.add2)

    def inner_grad(i):
        second_act(i)
        dpre = (r.sums[nd + i] + factor * r.sums[2 * nd + i]) * r.slope2[i]
        r.dall[d, i] = gain2 * rs2 * dpre
        r.add2[0] += dpre
        r.add2[1] += dpre * ((r.sums[i] - center2) * rs2)

        @pl.when(z == start_z)
        def _():
            r.act2[y, i] = r.own2[i]
            act_hand_on(i)

    def rows_grad(i):
        set_cols(1, shifts(r.dall[d, i], side, -1))
        dact1 = im2col_dot(1, (r.bm[0], r.bm[1]))
        r.inp[i] = dact1
        dpre1 = dact1 * r.slope1[i]
        r.add1[0] += dpre1
        r.add1[1] += dpre1 * ((r.xin[i] - center1) * rs1)

    same = lambda j: j

    def start(j, _):
        settle(nd + j)
        first_map(j, gain1, shift1)
        chan.advance(nd + j, nd, change_item)
        chan.advance(j, nd, same)
        return 0

    def steady(j, _):
        first_map(j, gain1, shift1)
        chan.advance(j, nd, same)
        settle(nd + j)
        inner_grad(j - 4)
        far_to_core(j - 4)
        act_step(j)
        return 0

    def end(j, _):
        chan.advance(j, nd, same)
        settle(nd + j)
        inner_grad(j - 4)
        far_to_core(j - 4)
        act_step(j)
        return 0

    lax.fori_loop(0, 4, start, 0)
    lax.fori_loop(4, nd, steady, 0)
    lax.fori_loop(nd, nd + 4, end, 0)
    grads.hand_on(z)
    back = lambda j: send(r.xs.at[lax.rem(c + j, nc)], r.rx.at[c], r.in_s.at[j], r.in_r.at[c], (d, lax.rem(c + j, nc)))

    def input_rows():
        grad = (gain1 * rs1 * (ins_grad.total() * r.slope1[d]) + r.call[c, d]).T
        for j in range(nc):
            r.xs[j] = grad[j * rows : (j + 1) * rows]
        for j in range(1, nc):
            back(j).start()
        r.rx[c] = r.xs[c]

    def gather_grads(u):
        for step in range(1, nz):
            pl.when(u == LINE_AT[step - 1])(lambda: meet(grads, step, lambda zs: over_chan_too(zs * ny + y)))
        for step in range(nz):
            pl.when(u == SIDE_AT[step])(lambda: meet_sides(step))

        @pl.when(u == NEAR_AT)
        def _():
            for o in range(nz):
                ins_grad.near(nearest(z, nz - 1 - o)).start()

        for o in range(nz):
            pl.when(u == SUMS_AT[o])(lambda: ins_grad.spread(nearest(z, nz - 1 - o)))
        pl.when(u == ROWS_AT)(input_rows)

    def all_rows(i, _):
        rows_grad(i)
        act_step(nd + 4 + i)
        gather_grads(i)
        return 0

    lax.fori_loop(0, nd, all_rows, 0)
    sh1, gg1 = lanes_sum(r.add1[0]), lanes_sum(r.add1[1])
    sh2, gg2 = lanes_sum(r.add2[0]), lanes_sum(r.add2[1])

    pad = jnp.zeros((1, cb - db), F32)
    wide = lambda col: jnp.concatenate([to_row(col), pad], axis=1)
    r.vec[...] = stacked([to_row(sh1), to_row(gg1), wide(sh2), wide(gg2)], cb)
    vectors = ToAll("dp", nd, r.vec, r.vecs, r.vec_s, r.vec_r)
    vectors.start()

    def kernel_grad(images, left_of, rights_of, between=None):
        for j, i in enumerate(images):
            lanes = slice(3 * j * px, 3 * (j + 1) * px)
            for t, m in enumerate(shifts(left_of(i), side)):
                hi, lo = split(m)
                r.left[t * cb : (t + 1) * cb, lanes] = jnp.concatenate([hi, hi, lo], axis=1)
            at = 0
            for v in rights_of(i):
                n = v.shape[0]
                hi, lo = split(v)
                r.right[at : at + n, lanes] = jnp.concatenate([hi, lo, hi], axis=1)
                at += n

        def add(m, _):
            third = pl.ds(pl.multiple_of(m * 3 * cb, 16), 3 * cb)
            r.stage[third] += dot_nt(r.left[third], r.right[...])
            if between is not None:
                between(m)
            return 0

        lax.fori_loop(0, 3, add, 0)

    r.stage[...] = jnp.zeros_like(r.stage)

    def second_kernel(q, _):
        zs = nearest(z, q)
        for j in range(2):
            act_copy(0, 1 - y, 2 * q + j, z, 1 - y).wait_recv()
            call_copy(0, across, 2 * q + j).wait_recv()
            call_copy(1, last, 2 * q + j).wait_recv()

        def between(m):
            u = nd + 3 * q + m
            act_step(nd + 4 + u)
            gather_grads(u)

        kernel_grad(
            [2 * q, 2 * q + 1],
            lambda i: jnp.concatenate([r.act2[0, i], r.act2[1, i]], axis=0),
            lambda i: [r.call[j, i] for j in range(nc)],
            between,
        )
        return 0

    lax.fori_loop(0, nz, second_kernel, 0)
    g2_copy = pltpu.make_async_copy(r.stage, r.g2_out, r.g2_sem)
    g2_copy.start()

    r.block_out[...] = ((r.xin[d] + outs.total()) * mine).T
    gather_grads(20)
    g2_copy.wait()
    r.stage[...] = jnp.zeros_like(r.stage)

    def first_kernel(j, _):
        @pl.when(j == 1)
        def _():
            for o in range(1, nd):
                to_core(0, lax.rem(d + o, nd), across).wait_recv()

        @pl.when(j == 2)
        def _():
            for o in range(1, nd):
                s = lax.rem(d + o, nd)
                to_far(s, far).wait_recv()
                to_core(1, s, far).start()

        @pl.when(j == 3)
        def _():
            for o in range(1, nd):
                to_core(1, lax.rem(d + o, nd), last).wait_recv()

        q = jnp.where(j == 0, c, jnp.where(j == 1, across, jnp.where(j == 2, far, last)))

        def between(m):
            gather_grads(21 + 3 * j + m)

        kernel_grad([2 * q, 2 * q + 1], lambda i: r.act1[i], lambda i: [r.dall[s, i] for s in slots], between)
        return 0

    lax.fori_loop(0, nc, first_kernel, 0)
    gather_grads(33)
    g1_copy = pltpu.make_async_copy(r.stage, r.g1_out, r.g1_sem)
    g1_copy.start()

    vectors.finish()
    total = vectors.total()
    rows_of = lambda j: jnp.concatenate([r.vecs[start_z * ny + q, j : j + 1, :db] for q in range(ny)], axis=1)
    r.small[...] = stacked([total[0:1], total[1:2], rows_of(2), rows_of(3), jnp.broadcast_to(norm, (1, cb))], cb)
    for j in range(1, nc):
        back(j).wait_send()
        other = lax.rem(c + j, nc)
        send(r.xs.at[other], r.rx.at[other], r.in_s.at[0], r.in_r.at[other], (d, other)).wait_recv()
    for j in range(nc):
        r.input_grad[:, j * cb : (j + 1) * cb] = r.rx[j]

    own_cot(c).wait_send()
    for line in (ins, cots, fars, grads):
        line.drain()
    for zs in range(nz):
        column(c, zs).wait_send()

    @pl.when(c == owner)
    def _():
        for j in range(1, nc):
            piece(j).wait_send()

    def sent(i, _):
        call_copy(0, c, i).wait_send()
        call_copy(1, far, i).wait_send()
        pl.when((z >= start_z) & (z < nz - 1))(lambda: act_up(i).wait_send())
        pl.when((z <= start_z) & (z > 0))(lambda: act_down(i).wait_send())
        act_side(i).wait_send()
        return 0

    lax.fori_loop(0, nd, sent, 0)
    for j in range(1, nd):
        s = lax.rem(d + j, nd)
        to_far(s, c).wait_send()
        to_core(0, s, c).wait_send()
        to_core(1, s, far).wait_send()
    g1_copy.wait()


def close_kernel(pieces, small, block_in, rows_in, first_in, second_in, block_out, rows_out, first_out, second_out,
                 gg1, sh1, gg2, sh2, norm, first, second, vec, sems, side_sems):
    cut = first_in.shape[0] // pieces
    legs = []
    for j in range(pieces):
        part = pl.ds(j * cut, cut)
        for k, (src, mid, dst) in enumerate(((second_in, second, second_out), (first_in, first, first_out))):
            legs.append((
                pltpu.make_async_copy(src.at[part], mid.at[part], sems.at[0, k, j]),
                pltpu.make_async_copy(mid.at[part], dst.at[part], sems.at[1, k, j]),
            ))
    sides = [pltpu.make_async_copy(a, b, side_sems.at[j])
             for j, (a, b) in enumerate(((small, vec), (block_in, block_out), (rows_in, rows_out)))]
    for cp in sides:
        cp.start()
    for come, _ in legs:
        come.start()
    sides[0].wait()
    for j, ref in enumerate((sh1, gg1, sh2, gg2)):
        ref[...] = vec[j : j + 1].reshape(vec.shape[1])
    norm[0] = jnp.sum(vec[4:5, 0:1])
    for come, go in legs:
        come.wait()
        go.start()
    for _, go in legs:
        go.wait()
    for cp in sides[1:]:
        cp.wait()


def fused_on_device(p, image_rows, groups, conv_first, conv_second, gain_first, shift_first, gain_second, shift_second, cotangent):
    cb, px = p.cb, p.px
    rows = px // p.nc
    scratch = scratch_of(p)
    out = lambda *s: jax.ShapeDtypeStruct(s, F32)
    any_, vmem, smem = (pl.BlockSpec(memory_space=m) for m in (pl.ANY, VMEM, SMEM))
    large = (out(px, cb), out(rows, p.ch), out(9 * cb, p.ch), out(9 * cb, p.ch))
    block_out, input_grad, g1, g2, small = pl.pallas_call(
        functools.partial(step_kernel, p, ARGS + OUTS + tuple(scratch)),
        out_shape=large + (out(8, cb),),
        in_specs=[vmem, vmem, any_, any_, vmem, vmem, vmem, vmem, smem],
        out_specs=(vmem, vmem, any_, any_, vmem),
        scratch_shapes=list(scratch.values()),
        compiler_params=pltpu.CompilerParams(collective_id=0, has_side_effects=True, vmem_limit_bytes=LIMIT),
    )(
        image_rows.reshape(rows, p.ch), cotangent.reshape(px, cb), conv_first.reshape(9, cb, p.ch),
        conv_second.reshape(9, cb, p.ch), gain_first, shift_first, gain_second, shift_second, groups,
    )
    pieces = 6
    block_out, input_grad, g1, g2, gg1, sh1, gg2, sh2, norm = pl.pallas_call(
        functools.partial(close_kernel, pieces),
        out_shape=large + (out(cb),) * 4 + (out(1),),
        in_specs=[any_] * 5,
        out_specs=(vmem, vmem, any_, any_) + (vmem,) * 4 + (smem,),
        scratch_shapes=[VMEM((9 * cb, p.ch), F32), VMEM((9 * cb, p.ch), F32), VMEM((8, cb), F32), DMA((2, 2, pieces)), DMA((3,))],
        compiler_params=pltpu.CompilerParams(vmem_limit_bytes=LIMIT),
    )(small, block_out, input_grad, g1, g2)
    return (
        block_out.reshape(cotangent.shape), input_grad.reshape(image_rows.shape),
        g1.reshape(conv_first.shape), g2.reshape(conv_second.shape), gg1, sh1, gg2, sh2, norm.reshape(()),
    )


def valid_pixels(groups, extent_full):
    places = jnp.arange(extent_full, dtype=jnp.int32)
    extent = jnp.where(groups == 1, extent_full, extent_full // 2).astype(jnp.int32)
    inside = places[None, :] < extent[:, None]
    return (inside[:, :, None] & inside[:, None, :]).astype(jnp.float32)[..., None]


def convolve(values, kernel):
    return lax.conv_general_dilated(
        values,
        kernel,
        (1, 1),
        "SAME",
        dimension_numbers=("NHWC", "HWIO", "NHWC"),
        precision=lax.Precision.HIGHEST,
    )


def silu_slope(preact):
    sigmoid = jax.nn.sigmoid(preact)
    return sigmoid * (1.0 + preact * (1.0 - sigmoid))


def batch_moments(values, validity):
    summed, squares, pixels = lax.psum(
        (
            jnp.sum(values * validity, axis=(0, 1, 2)),
            jnp.sum(validity * values * values, axis=(0, 1, 2)),
            jnp.sum(validity),
        ),
        "dp",
    )
    center = summed / pixels
    spread = squares / pixels - center * center
    return (center, lax.rsqrt(spread + epsilon), pixels)


def project_over_chan(values, kernel):
    return lax.psum_scatter(convolve(values, kernel), "chan", scatter_dimension=3, tiled=True)


def conv_backward(upstream, values, kernel):
    columns = lax.all_gather(upstream, "chan", axis=3, tiled=True)
    offset = jnp.int32(0)
    inputs_grad = jnp.zeros_like(values)
    kernel_grad = jnp.zeros_like(kernel)
    breadth = columns.shape[3]
    kernel_part = lax.dynamic_slice_in_dim(kernel, offset, breadth, 3)
    primal, pull = jax.vjp(convolve, values, kernel_part)
    values_part, kernel_part_grad = pull(columns)
    kernel_grad = lax.dynamic_update_slice_in_dim(kernel_grad, kernel_part_grad, offset, 3)
    return (inputs_grad + values_part, kernel_grad)


def batch_sums(dpre, scaled):
    return lax.psum((jnp.sum(dpre, axis=(0, 1, 2)), jnp.sum(dpre * scaled, axis=(0, 1, 2))), "dp")


def plain_on_device(
    image_rows,
    groups,
    conv_first,
    conv_second,
    gain_first,
    shift_first,
    gain_second,
    shift_second,
    cotangent,
):
    inputs = lax.all_to_all(image_rows, "chan", split_axis=3, concat_axis=1, tiled=True)
    validity = valid_pixels(groups, inputs.shape[1])
    cot_valid = cotangent * validity
    center_one, rscale_one, pixels = batch_moments(inputs, validity)
    scaled_one = (inputs - center_one) * rscale_one
    pre_one = scaled_one * gain_first + shift_first
    act_one = jax.nn.silu(pre_one) * validity
    inner = project_over_chan(act_one, conv_first) * validity
    center_two, rscale_two, pixels_again = batch_moments(inner, validity)
    scaled_two = (inner - center_two) * rscale_two
    pre_two = scaled_two * gain_second + shift_second
    act_two = jax.nn.silu(pre_two) * validity
    block_out = inputs * validity + project_over_chan(act_two, conv_second) * validity
    dact_two, kernel_two_part = conv_backward(cot_valid, act_two, conv_second)
    dpre_two = dact_two * validity * silu_slope(pre_two)
    shift_two_grad, gain_two_grad = batch_sums(dpre_two, scaled_two)
    dinner = (
        gain_second
        * rscale_two
        * (dpre_two - validity * (shift_two_grad + scaled_two * gain_two_grad) / pixels)
    )
    dact_one, kernel_one_part = conv_backward(dinner, act_one, conv_first)
    dpre_one = dact_one * validity * silu_slope(pre_one)
    shift_one_grad, gain_one_grad = batch_sums(dpre_one, scaled_one)
    small_squares = (
        jnp.sum(gain_one_grad**2)
        + jnp.sum(shift_one_grad**2)
        + jnp.sum(gain_two_grad**2)
        + jnp.sum(shift_two_grad**2)
    )
    kernel_one_sum, kernel_two_sum = lax.psum((kernel_one_part, kernel_two_part), "dp")
    local_sq = jnp.sum(kernel_one_sum**2) + jnp.sum(kernel_two_sum**2) + small_squares
    squares = lax.psum(local_sq, "chan")
    factor = sam_radius * lax.rsqrt(squares + norm_floor)
    kernel_one = conv_first + factor * kernel_one_sum
    kernel_two = conv_second + factor * kernel_two_sum
    grad_norm = jnp.sqrt(squares)
    moved_gain_one = gain_first + factor * gain_one_grad
    moved_shift_one = shift_first + factor * shift_one_grad
    moved_gain_two = gain_second + factor * gain_two_grad
    moved_shift_two = shift_second + factor * shift_two_grad
    pre_one_new = scaled_one * moved_gain_one + moved_shift_one
    act_one_new = jax.nn.silu(pre_one_new) * validity
    inner_new = project_over_chan(act_one_new, kernel_one) * validity
    scaled_two_new = (inner_new - center_two) * rscale_two
    pre_two_new = scaled_two_new * moved_gain_two + moved_shift_two
    act_two_new = jax.nn.silu(pre_two_new) * validity
    dact_two_new, kernel_two_grad = conv_backward(cot_valid, act_two_new, kernel_two)
    dpre_two_new = dact_two_new * validity * silu_slope(pre_two_new)
    gain_two_new_grad = jnp.sum(dpre_two_new * scaled_two_new, axis=(0, 1, 2))
    shift_two_new_grad = jnp.sum(dpre_two_new, axis=(0, 1, 2))
    dinner_new = moved_gain_two * rscale_two * dpre_two_new
    dact_one_new, kernel_one_grad = conv_backward(dinner_new, act_one_new, kernel_one)
    dpre_one_new = dact_one_new * validity * silu_slope(pre_one_new)
    gain_one_new_grad = jnp.sum(dpre_one_new * scaled_one, axis=(0, 1, 2))
    shift_one_new_grad = jnp.sum(dpre_one_new, axis=(0, 1, 2))
    inputs_grad = moved_gain_one * rscale_one * dpre_one_new + cot_valid
    input_grad = lax.all_to_all(inputs_grad, "chan", split_axis=1, concat_axis=3, tiled=True)
    (
        kernel_one_grad,
        kernel_two_grad,
        gain_one_new_grad,
        shift_one_new_grad,
        gain_two_new_grad,
        shift_two_new_grad,
    ) = lax.psum(
        (
            kernel_one_grad,
            kernel_two_grad,
            gain_one_new_grad,
            shift_one_new_grad,
            gain_two_new_grad,
            shift_two_new_grad,
        ),
        "dp",
    )
    return (
        block_out,
        input_grad,
        kernel_one_grad,
        kernel_two_grad,
        gain_one_new_grad,
        shift_one_new_grad,
        gain_two_new_grad,
        shift_two_new_grad,
        grad_norm,
    )


def solution(mesh):
    nd, nc = mesh.shape["dp"], mesh.shape["chan"]

    def on_device(image_rows, *rest):
        images, side, channels = image_rows.shape[0], image_rows.shape[2], image_rows.shape[3]
        fits = images == 1 and nc == 4 and nd == 2 * nc and channels // nd % 16 == 0 and side * side == 256
        if not fits:
            return plain_on_device(image_rows, *rest)
        return fused_on_device(Plan(nd, nc, channels, side), image_rows, *rest)

    return jax.shard_map(
        on_device,
        mesh=mesh,
        in_specs=(
            P("dp", "chan", None, None),
            P("dp"),
            P(None, None, "chan", None),
            P(None, None, "chan", None),
            P("chan"),
            P("chan"),
            P("chan"),
            P("chan"),
            P("dp", None, None, "chan"),
        ),
        out_specs=(
            P("dp", None, None, "chan"),
            P("dp", "chan", None, None),
            P(None, None, "chan", None),
            P(None, None, "chan", None),
            P("chan"),
            P("chan"),
            P("chan"),
            P("chan"),
            P(),
        ),
        check_vma=False,
    )
```

```python
import functools
import types

import jax
import jax.numpy as jnp
from jax import lax
from jax.experimental import pallas as pl
from jax.experimental.pallas import tpu as pltpu
from jax.sharding import PartitionSpec as P

epsilon = 1e-05
sam_radius = 0.05
norm_floor = 1e-06
MESH = pl.DeviceIdType.MESH
F32, BF16 = jnp.float32, jnp.bfloat16
VMEM, SMEM = pltpu.VMEM, pltpu.SMEM
DMA = pltpu.SemaphoreType.DMA
LIMIT = 60 << 20


class Plan:
    def __init__(self, nd, nc, channels, side):
        self.nd, self.nc, self.ch, self.side = nd, nc, channels, side
        self.cb, self.db, self.px = channels // nc, channels // nd, side * side
        self.ny = 2
        self.nz = nd // 2


def split(v):
    hi = v.astype(BF16)
    return hi, (v - hi.astype(F32)).astype(BF16)


def dot(a, b):
    return lax.dot_general(a, b, (((1,), (0,)), ((), ())), preferred_element_type=F32)


def dot_nt(a, b):
    return lax.dot_general(a, b, (((1,), (1,)), ((), ())), preferred_element_type=F32)


def edge_masks(side, px):
    lane = lax.broadcasted_iota(jnp.int32, (1, px), 1)
    col = lax.rem(lane, side)
    row = lax.div(lane, side)
    one = jnp.ones((1, px), F32)
    zero = jnp.zeros((1, px), F32)
    rows = {-1: jnp.where(row >= 1, one, zero), 0: None, 1: jnp.where(row < side - 1, one, zero)}
    cols = {-1: jnp.where(col >= 1, one, zero), 0: None, 1: jnp.where(col < side - 1, one, zero)}
    return rows, cols


def moved(v, lanes, mask):
    if lanes:
        v = pltpu.roll(v, (-lanes) % v.shape[1], axis=1)
    return v if mask is None else v * mask


def shifts(v, side, sign=1, taps=(-1, 0, 1)):
    rows, cols = edge_masks(side, v.shape[1])
    by_col = {s: moved(v, s, cols[s]) for s in (-1, 0, 1)}
    return [moved(by_col[sign * s], sign * r * side, rows[sign * r]) for r in taps for s in (-1, 0, 1)]


def gather_taps(prod, side, n):
    rows, cols = edge_masks(side, prod.shape[1])
    total = None
    for j, s in enumerate((-1, 0, 1)):
        part = None
        for i, r in enumerate((-1, 0, 1)):
            t = 3 * i + j
            m = moved(prod[t * n : (t + 1) * n], r * side, rows[r])
            part = m if part is None else part + m
        m = moved(part, s, cols[s])
        total = m if total is None else total + m
    return total


def sigmoid(t):
    return 1.0 / (1.0 + jnp.exp(-t))


def silu_and_slope(pre):
    s = sigmoid(pre)
    return pre * s, s * (1.0 + pre * (1.0 - s))


def lanes_sum(v):
    return jnp.sum(v, axis=1, keepdims=True)


def valid_map(flag, side, px):
    lane = lax.broadcasted_iota(jnp.int32, (1, px), 1)
    half = (lax.rem(lane, side) < side // 2) & (lax.div(lane, side) < side // 2)
    return jnp.where(half, jnp.ones((1, px), F32), flag)


def diagonal(n):
    return lax.broadcasted_iota(jnp.int32, (n, n), 0) == lax.broadcasted_iota(jnp.int32, (n, n), 1)


def to_row(col):
    return jnp.sum(jnp.where(diagonal(col.shape[0]), col, 0.0), axis=0, keepdims=True)


def to_col(row):
    return jnp.sum(jnp.where(diagonal(row.shape[1]), row, 0.0), axis=1, keepdims=True)


def stacked(rows, n):
    at = lax.broadcasted_iota(jnp.int32, (8, n), 0)
    out = jnp.zeros((8, n), F32)
    for k, row in enumerate(rows):
        out = jnp.where(at == k, row, out)
    return out


def send(src, dst, ss, rs, device):
    return pltpu.make_async_remote_copy(
        src_ref=src, dst_ref=dst, send_sem=ss, recv_sem=rs, device_id=device, device_id_type=MESH
    )


def here():
    return lax.axis_index("dp"), lax.axis_index("chan")


def greet(p):
    d, c = here()
    barrier = pltpu.get_barrier_semaphore()
    for j in range(1, p.nd):
        pl.semaphore_signal(barrier, inc=1, device_id=(lax.rem(d + j, p.nd), c), device_id_type=MESH)
    for j in range(1, p.nc):
        pl.semaphore_signal(barrier, inc=1, device_id=(d, lax.rem(c + j, p.nc)), device_id_type=MESH)
    pl.semaphore_wait(barrier, p.nd - 1 + p.nc - 1)


class ToAll:
    def __init__(self, axis, n, tile, slots, ss, rs):
        d, c = here()
        self.n, self.tile, self.slots, self.ss, self.rs = n, tile, slots, ss, rs
        self.me = d if axis == "dp" else c
        self.device = (lambda o: (o, c)) if axis == "dp" else (lambda o: (d, o))

    def start(self):
        self.slots[self.me] = self.tile[...]
        for j in range(1, self.n):
            to = lax.rem(self.me + j, self.n)
            send(self.tile, self.slots.at[self.me], self.ss.at[j], self.rs.at[self.me], self.device(to)).start()

    def finish(self):
        for j in range(1, self.n):
            other = lax.rem(self.me + j, self.n)
            send(self.tile, self.slots.at[other], self.ss.at[j], self.rs.at[other], self.device(other)).wait()

    def total(self):
        total = self.slots[0]
        for j in range(1, self.n):
            total = total + self.slots[j]
        return total


class Line:
    def __init__(self, p, view, ss, rs, sides=True):
        self.p, self.view, self.ss, self.rs, self.sides = p, view, ss, rs, sides
        d, self.c = here()
        self.z, self.y = lax.div(d, p.ny), lax.rem(d, p.ny)

    def copy(self, zs, sem, z_to, y_to):
        slot = zs * self.p.ny + self.y
        return send(self.view(slot), self.view(slot), self.ss.at[sem, zs], self.rs.at[slot], (z_to * self.p.ny + y_to, self.c))

    def up(self, zs):
        return self.copy(zs, 0, lax.min(self.z + 1, self.p.nz - 1), self.y)

    def down(self, zs):
        return self.copy(zs, 1, lax.max(self.z - 1, 0), self.y)

    def side(self, zs):
        return self.copy(zs, 2, self.z, 1 - self.y)

    def got(self, zs, y):
        slot = zs * self.p.ny + y
        send(self.view(slot), self.view(slot), self.ss.at[0, 0], self.rs.at[slot], (self.z * self.p.ny + 1 - self.y, self.c)).wait_recv()

    def hand_on(self, zs):
        pl.when((zs <= self.z) & (self.z < self.p.nz - 1))(lambda: self.up(zs).start())
        pl.when((zs >= self.z) & (self.z > 0))(lambda: self.down(zs).start())
        if self.sides:
            self.side(zs).start()

    def drain(self):
        for zs in range(self.p.nz):
            pl.when((zs <= self.z) & (self.z < self.p.nz - 1))(lambda: self.up(zs).wait_send())
            pl.when((zs >= self.z) & (self.z > 0))(lambda: self.down(zs).wait_send())
            if self.sides:
                self.side(zs).wait_send()


def nearest(z, k):
    t = lax.div(z, 2)
    low = z + t * (3 - 2 * z)
    first = 1 - lax.min(lax.div(k, 2), 1)
    place = k + low * first * (1 - 2 * k)
    return place * (1 - 2 * t) + 3 * t


class ChanSum:
    def __init__(self, p, r):
        self.p, self.r = p, r
        d, c = here()
        k = lax.rem(c, 2)
        self.hb = p.db // 2
        self.across, self.far = (d, c + 1 - 2 * k), (d, lax.rem(c + 2, 4))
        self.mine = pl.multiple_of(k * self.hb, 8)
        self.yours = pl.multiple_of((1 - k) * self.hb, 8)

    def first(self, i):
        r = self.r
        return send(r.part.at[i, pl.ds(self.yours, self.hb)], r.near.at[i], r.cs1.at[i], r.cr1.at[i], self.across)

    def second(self, i):
        r = self.r
        return send(r.half.at[i], r.away.at[i], r.cs2.at[i], r.cr2.at[i], self.far)

    def third(self, i, rows):
        r = self.r
        mine = r.sums.at[i, pl.ds(self.mine, self.hb)]
        return send(mine, r.sums.at[i, pl.ds(rows, self.hb)], r.cs3.at[i], r.cr3.at[i], self.across)

    def chip(self, i):
        r = self.r
        self.first(i).wait()
        r.half[i] = r.part[i, pl.ds(self.mine, self.hb)] + r.near[i]
        self.second(i).start()

    def cross(self, i):
        r = self.r
        self.second(i).wait()
        r.sums[i, pl.ds(self.mine, self.hb)] = r.half[i] + r.away[i]
        self.third(i, self.mine).start()

    def done(self, i):
        self.third(i, self.yours).wait()

    def advance(self, j, n, item):
        at = lambda m: item(lax.clamp(0, m, n - 1))
        pl.when((j >= 1) & (j < n + 1))(lambda: self.chip(at(j - 1)))
        pl.when((j >= 3) & (j < n + 3))(lambda: self.cross(at(j - 3)))
        pl.when((j >= 4) & (j < n + 4))(lambda: self.done(at(j - 4)))


class ImageSum:
    def __init__(self, p, part, near, acc, away, s1, r1, s2, r2):
        self.p, self.part, self.buf1, self.acc, self.buf2 = p, part, near, acc, away
        self.s1, self.r1, self.s2, self.r2 = s1, r1, s2, r2
        d, self.c = here()
        self.z, self.y = lax.div(d, p.ny), lax.rem(d, p.ny)

    def near(self, zs):
        side = 1 - self.y
        return send(self.part.at[zs * self.p.ny + side], self.buf1.at[zs], self.s1.at[zs], self.r1.at[zs],
                    (self.z * self.p.ny + side, self.c))

    def away(self, zs, slot):
        return send(self.acc.at[zs], self.buf2.at[slot], self.s2.at[zs], self.r2.at[slot], (zs * self.p.ny + self.y, self.c))

    def spread(self, zs):
        self.near(zs).wait()
        self.acc[zs] = self.part[zs * self.p.ny + self.y] + self.buf1[zs]
        pl.when(zs != self.z)(lambda: self.away(zs, self.z).start())

    def total(self):
        total = self.acc[self.z]
        for j in range(1, self.p.nz):
            other = lax.rem(self.z + j, self.p.nz)
            self.away(other, other).wait()
            total = total + self.buf2[other]
        return total


def scratch_of(p):
    nd, nc, cb, db, px, nz, ny = p.nd, p.nc, p.cb, p.db, p.px, p.nz, p.ny
    rows = px // nc
    f = lambda *s: VMEM(s, F32)
    h = lambda *s: VMEM(s, BF16)
    return dict(
        k1w=f(9, cb, 256), k2w=f(9, db, p.ch), ks=f(nc, cb, 9 * db), b2=f(cb, 9 * db),
        a1=f(9 * db, cb), a2=f(9 * db, cb), g1=f(9 * db, cb), g2=f(9 * db, cb),
        a_cat=h(2, 9 * db, 3 * cb), bm=h(2, cb, 9 * db), b2m=h(2, cb, 9 * db), colh=h(2, 9 * db, px), coll=h(2, 9 * db, px),
        xs=f(nc, rows, cb), rx=f(nc, rows, cb), xin=f(nd, cb, px), act1=f(nd, cb, px), slope1=f(nd, cb, px),
        call=f(nc, nd, cb, px),
        part=f(3 * nd, db, px), near=f(3 * nd, db // 2, px), half=f(3 * nd, db // 2, px), away=f(3 * nd, db // 2, px),
        sums=f(3 * nd, db, px), slope2=f(nd, db, px), dpre=f(nd, db, px), add1=f(2, cb, px), add2=f(2, db, px),
        outp=f(nd, cb, px), outn=f(nz, cb, px), outc=f(nz, cb, px), outw=f(nz, cb, px),
        inp=f(nd, cb, px), inn=f(nz, cb, px), inc=f(nz, cb, px), inw=f(nz, cb, px),
        dall=f(nd, nd, db, px), act2=f(ny, nd, db, px), own2=f(nd, db, px), left=h(9 * cb, 6 * px), right=h(p.ch, 6 * px),
        stage=f(9 * cb, p.ch),
        par=f(8, cb), pars=f(nc, 8, cb), stat=f(8, cb), stats=f(nd, 8, cb), msg=f(8, cb), msgs=f(nd, 8, cb),
        sq=f(8, 128), sqs=f(nc, 8, 128), vec=f(8, cb), vecs=f(nd, 8, cb),
        k1_sem=DMA, k2_sem=DMA, g1_sem=DMA, g2_sem=DMA,
        xs_s=DMA((nc,)), xs_r=DMA((nc,)), ks_s=DMA((nc,)), ks_r=DMA,
        par_s=DMA((nc,)), par_r=DMA((nc,)), stat_s=DMA((nd,)), stat_r=DMA((nd,)), msg_s=DMA((nd,)), msg_r=DMA((nd,)),
        sq_s=DMA((nc,)), sq_r=DMA((nc,)), vec_s=DMA((nd,)), vec_r=DMA((nd,)),
        x_s=DMA((3, nz)), x_r=DMA((nd,)), c_s=DMA((3, nz)), c_r=DMA((nd,)), d_s=DMA((3, nz)), d_r=DMA((nd,)),
        cs1=DMA((3 * nd,)), cr1=DMA((3 * nd,)), cs2=DMA((3 * nd,)), cr2=DMA((3 * nd,)), cs3=DMA((3 * nd,)), cr3=DMA((3 * nd,)),
        o_s1=DMA((nz,)), o_r1=DMA((nz,)), o_s2=DMA((nz,)), o_r2=DMA((nz,)),
        i_s1=DMA((nz,)), i_r1=DMA((nz,)), i_s2=DMA((nz,)), i_r2=DMA((nz,)),
        call_s=DMA((2, nd)), call_r=DMA((2, nd)), own_s=DMA, f_s=DMA((3, nz)), f_r=DMA((nd,)), col_s=DMA((nz,)), act_s=DMA((3, nd)), act_r=DMA((ny, nd)),
        far_s=DMA((nd,)), far_r=DMA((nd,)), core_s=DMA((2, nd)), core_r=DMA((2, nd)), in_s=DMA((nc,)), in_r=DMA((nc,)),
    )


FARS = (3, 6, 12)
OUTS_AT = (24, 25, 26, 27)
ACT = (44, 8, 4)
LINE_AT = (5, 9, 12)
SIDE_AT = (6, 11, 14, 17)
NEAR_AT = 15
SUMS_AT = (18, 20, 22, 24)
ROWS_AT = 28

ARGS = ("x", "cot", "k1", "k2", "gain1", "shift1", "gain2", "shift2", "groups")
OUTS = ("block_out", "input_grad", "g1_out", "g2_out", "small")


def step_kernel(p, names, *refs):
    r = types.SimpleNamespace(**dict(zip(names, refs)))
    cb, db, px, side, nd, nc, nz, ny = p.cb, p.db, p.px, p.side, p.nd, p.nc, p.nz, p.ny
    d, c = here()
    z, y = lax.div(d, ny), lax.rem(d, ny)
    k = lax.rem(c, 2)
    far, across = lax.rem(c + 2, 4), c + 1 - 2 * k
    last = 6 - c - far - across
    rows = px // nc
    owner = (1 - lax.div(z, 2)) * (2 - 2 * lax.rem(z, 2)) + lax.div(z, 2) * (1 + 2 * lax.rem(z, 2))
    origin = lambda c: (1 - c // 2) * (1 + c % 2) + c // 2 * 3 * (c % 2)
    start_z = (1 - lax.div(c, 2)) * (1 + k) + lax.div(c, 2) * 3 * k
    first = owner * cb + y * db
    slots = [origin(q) * ny + j for q in range(nc) for j in range(ny)]
    image = lambda j: nearest(z, lax.div(j, 2)) * ny + y + lax.rem(j, 2) * (1 - 2 * y)

    base = lax.min(lax.div(first, 128), (p.ch - 256) // 128) * 128
    k1_copy = pltpu.make_async_copy(r.k1.at[:, :, pl.ds(pl.multiple_of(base, 128), 256)], r.k1w, r.k1_sem)
    k1_copy.start()
    k2_rows = pl.ds(pl.multiple_of(y * db, 8), db)
    k2_copy = pltpu.make_async_copy(r.k2.at[:, k2_rows], r.k2w, r.k2_sem)
    pl.when(c == owner)(lambda: k2_copy.start())
    greet(p)

    for j in range(nc):
        r.xs[j] = r.x[:, j * cb : (j + 1) * cb]
    a2a = lambda j: send(r.xs.at[lax.rem(c + j, nc)], r.rx.at[c], r.xs_s.at[j], r.xs_r.at[c], (d, lax.rem(c + j, nc)))
    for j in range(1, nc):
        a2a(j).start()
    r.rx[c] = r.xs[c]
    r.par[...] = stacked([r.gain2[...].reshape(1, cb), r.shift2[...].reshape(1, cb)], cb)
    params = ToAll("chan", nc, r.par, r.pars, r.par_s, r.par_r)
    params.start()
    flag = jnp.full((1, 1), jnp.where(r.groups[0] == 1, 1.0, 0.0), F32)
    mine = valid_map(flag, side, px)
    r.call[c, d] = r.cot[...].T * mine

    def meet(line, step, then=None):
        def one(zs):
            line.got(zs, y)
            line.hand_on(zs)
            if then is not None:
                then(zs)

        pl.when(z >= step)(lambda: one(lax.max(z - step, 0)))
        pl.when(z + step < nz)(lambda: one(lax.min(z + step, nz - 1)))

    cots = Line(p, lambda s: r.call.at[c, s], r.c_s, r.c_r)
    cots.hand_on(z)
    own_cot = lambda q: send(r.call.at[q, d], r.call.at[q, d], r.own_s, r.f_r.at[d], (d, far))
    fars = Line(p, lambda s: r.call.at[far, s], r.f_s, r.f_r, False)
    column = lambda q, zs: send(
        r.call.at[q, zs * ny + 1 - y], r.call.at[q, zs * ny + 1 - y], r.col_s.at[zs], r.f_r.at[zs * ny + 1 - y], (d, far)
    )
    call_copy = lambda lane, q, i: send(
        r.call.at[q, i], r.call.at[q, i], r.call_s.at[lane, i], r.call_r.at[lane, i], (d, across)
    )

    @pl.when(c == owner)
    def _():
        k2_copy.wait()
        for j in range(nc):
            r.ks[j] = r.k2w[:, :, j * cb : (j + 1) * cb].reshape(9 * db, cb).T

    for j in range(1, nc):
        a2a(j).wait_send()
        other = lax.rem(c + j, nc)
        send(r.xs.at[other], r.rx.at[other], r.xs_s.at[j], r.xs_r.at[other], (d, other)).wait_recv()
    r.xin[d] = r.rx[...].reshape(px, cb).T
    ins = Line(p, lambda s: r.xin.at[s], r.x_s, r.x_r)

    count = lanes_sum(mine)
    total = lanes_sum(r.xin[d] * mine)
    off = r.xin[d] - total / count
    r.stat[...] = stacked([to_row(total), to_row(lanes_sum(mine * off * off)), jnp.broadcast_to(flag, (1, cb))], cb)
    stats = ToAll("dp", nd, r.stat, r.stats, r.stat_s, r.stat_r)
    stats.start()
    ins.hand_on(z)

    piece = lambda j: send(r.ks.at[lax.rem(c + j, nc)], r.b2, r.ks_s.at[j], r.ks_r, (d, lax.rem(c + j, nc)))

    @pl.when(c == owner)
    def _():
        for j in range(1, nc):
            piece(j).start()

    k1_copy.wait()
    turn = lax.rem(256 - (first - base), 256)
    b1 = jnp.concatenate([pltpu.roll(r.k1w[t], turn, axis=1)[:, :db] for t in range(9)], axis=1)
    hi, lo = split(b1)
    r.bm[0], r.bm[1] = hi, lo
    r.a1[...] = b1.T
    hi, lo = split(r.a1[...])
    r.a_cat[0] = jnp.concatenate([hi, hi, lo], axis=1)

    meet(cots, 1)
    own_cot(c).start()
    stats.finish()

    def val_of(i):
        return valid_map(r.stats[i, 2:3, 0:1], side, px)

    counts = [jnp.sum(val_of(i), keepdims=True) for i in range(nd)]
    pixels = functools.reduce(jnp.add, counts)
    center = functools.reduce(jnp.add, [r.stats[i, 0:1] for i in range(nd)]) / pixels
    spread = [r.stats[i, 1:2] + counts[i] * (r.stats[i, 0:1] / counts[i] - center) ** 2 for i in range(nd)]
    center1, rs1 = to_col(center), to_col(lax.rsqrt(functools.reduce(jnp.add, spread) / pixels + epsilon))
    gain1, shift1 = to_col(r.gain1[...].reshape(1, cb)), to_col(r.shift1[...].reshape(1, cb))

    chan = ChanSum(p, r)

    def first_map(i, gain, shift):
        val = val_of(i)
        act, slope = silu_and_slope((r.xin[i] - center1) * rs1 * gain + shift)
        act = act * val
        r.act1[i], r.slope1[i] = act, slope * val
        ah, al = split(act)
        prod = dot(r.a_cat[0], jnp.concatenate([ah, al, ah], axis=0))
        r.part[i] = gather_taps(prod, side, db) * val
        chan.first(i).start()

    def second_back(i, first):
        ch, cl = split(r.call[c, i])
        prod = dot(r.a_cat[1], jnp.concatenate([ch, cl, ch], axis=0))
        r.part[first + i] = gather_taps(prod, side, db) * val_of(i)
        chan.first(first + i).start()

    def back_item(j):
        return nd + image(j)

    def set_back(a2):
        for t in range(9):
            hi, lo = split(a2[(8 - t) * db : (9 - t) * db])
            r.a_cat[1, t * db : (t + 1) * db] = jnp.concatenate([hi, hi, lo], axis=1)

    def second_block():
        @pl.when(c == owner)
        def _():
            r.b2[...] = r.ks[c]

        @pl.when(c != owner)
        def _():
            send(r.ks.at[0], r.b2, r.ks_s.at[0], r.ks_r, (d, owner)).wait_recv()

        r.a2[...] = r.b2[...].T
        set_back(r.a2)
        b2h, b2l = split(r.b2[...])
        r.b2m[0], r.b2m[1] = b2h, b2l

    def forward(kk, _):
        zs = nearest(z, kk)
        first_map(zs * ny + y, gain1, shift1)
        chan.advance(2 * kk, nd, image)
        meet(ins, kk + 1)
        pl.when(kk == 0)(lambda: meet(cots, 2))
        pl.when(kk == 1)(lambda: meet(cots, 3))
        pl.when(kk == 1)(second_block)
        ins.got(zs, 1 - y)
        first_map(zs * ny + 1 - y, gain1, shift1)
        chan.advance(2 * kk + 1, nd, image)

        @pl.when(kk > 0)
        def _():
            before = nearest(z, lax.max(kk - 1, 0))
            second_back(before * ny + y, nd)
            chan.advance(2 * kk - 2, nd, back_item)
            cots.got(before, 1 - y)
            second_back(before * ny + 1 - y, nd)
            chan.advance(2 * kk - 1, nd, back_item)

        return 0

    lax.fori_loop(0, nz, forward, 0)
    furthest = nearest(z, nz - 1)
    chan.advance(nd, nd, image)
    second_back(furthest * ny + y, nd)
    chan.advance(nd - 2, nd, back_item)
    chan.advance(nd + 1, nd, image)
    cots.got(furthest, 1 - y)
    second_back(furthest * ny + 1 - y, nd)
    chan.advance(nd - 1, nd, back_item)
    chan.advance(nd + 2, nd, image)
    chan.advance(nd, nd, back_item)
    chan.advance(nd + 3, nd, image)

    params.finish()
    both = [r.pars[owner, j : j + 1] for j in range(2)]
    gain2, shift2 = (to_col(jnp.where(y == 0, v[:, :db], v[:, cb - db :])) for v in both)

    def add_up(i, carry):
        return carry + lanes_sum(r.sums[i] * val_of(i))

    chan.advance(nd + 1, nd, back_item)
    center2 = lax.fori_loop(0, nd, add_up, jnp.zeros((db, 1), F32)) / pixels

    def add_squares(i, carry):
        off = r.sums[i] - center2
        return carry + lanes_sum(val_of(i) * off * off)

    chan.advance(nd + 2, nd, back_item)
    rs2 = lax.rsqrt(lax.fori_loop(0, nd, add_squares, jnp.zeros((db, 1), F32)) / pixels + epsilon)

    chan.advance(nd + 3, nd, back_item)
    own_cot(far).wait_recv()
    fars.hand_on(z)
    for zs in range(nz):
        column(c, zs).start()

    def inner_sums(i, carry):
        val = val_of(i)
        scaled = (r.sums[i] - center2) * rs2
        act, slope = silu_and_slope(scaled * gain2 + shift2)
        r.own2[i] = act * val
        dpre = r.sums[nd + i] * (slope * val)
        r.dpre[i] = dpre
        return carry[0] + lanes_sum(dpre), carry[1] + lanes_sum(dpre * scaled)

    zero = jnp.zeros((db, 1), F32)
    sh2, gg2 = lax.fori_loop(0, nd, inner_sums, (zero, zero))

    outs = ImageSum(p, r.outp, r.outn, r.outc, r.outw, r.o_s1, r.o_r1, r.o_s2, r.o_r2)

    def set_cols(w, maps):
        for t, m in enumerate(maps):
            hi, lo = split(m)
            r.colh[w, t * db : (t + 1) * db] = hi
            r.coll[w, t * db : (t + 1) * db] = lo

    def im2col_dot(w, which):
        return dot(which[0], r.colh[w]) + dot(which[0], r.coll[w]) + dot(which[1], r.colh[w])

    def wgrad(w, other):
        oh, ol = split(other)
        left = jnp.concatenate([r.colh[w], r.colh[w], r.coll[w]], axis=1)
        return dot_nt(left, jnp.concatenate([oh, ol, oh], axis=1))

    r.g1[...] = jnp.zeros_like(r.g1)
    r.g2[...] = jnp.zeros_like(r.g2)
    change_item = lambda j: 2 * nd + j

    def settle(t):
        for step in range(1, nz):
            pl.when(t == FARS[step - 1])(lambda: meet(fars, step))

    def gradients(i, carry):
        scaled = (r.sums[i] - center2) * rs2
        dinner = gain2 * rs2 * (r.dpre[i] - val_of(i) * (sh2 + scaled * gg2) / pixels)
        set_cols(0, shifts(r.own2[i], side))
        set_cols(1, shifts(dinner, side, -1))
        r.outp[i] = im2col_dot(0, (r.b2m[0], r.b2m[1]))
        r.g2[...] += wgrad(0, r.call[c, i])
        r.g1[...] += wgrad(1, r.act1[i])
        dpre1 = im2col_dot(1, (r.bm[0], r.bm[1])) * r.slope1[i]
        scaled1 = (r.xin[i] - center1) * rs1
        pl.when(lax.rem(i, 2) == 1 - y)(lambda: outs.near(lax.div(i, 2)).start())
        call_copy(0, c, i).start()
        settle(i)
        return carry[0] + lanes_sum(dpre1), carry[1] + lanes_sum(dpre1 * scaled1)

    zero = jnp.zeros((cb, 1), F32)
    sh1, gg1 = lax.fori_loop(0, nd, gradients, (zero, zero))
    set_back(r.g2)

    square = jnp.sum(r.g1[...] * r.g1[...] + r.g2[...] * r.g2[...], keepdims=True)
    square = square + jnp.where(c == 0, jnp.sum(sh2 * sh2 + gg2 * gg2, keepdims=True), 0.0)
    r.msg[...] = stacked([to_row(sh1), to_row(gg1), jnp.broadcast_to(square, (1, cb))], cb)
    over_dp = ToAll("dp", nd, r.msg, r.msgs, r.msg_s, r.msg_r)
    over_dp.start()

    def change(j, _):
        second_back(j, 2 * nd)
        chan.advance(j, nd, change_item)
        return 0

    lax.fori_loop(0, nd // 2, change, 0)
    over_dp.finish()
    total = over_dp.total()
    sh1, gg1 = to_col(total[0:1]), to_col(total[1:2])
    square = total[2:3, 0:1] + jnp.sum(sh1 * sh1 + gg1 * gg1, keepdims=True)
    r.sq[...] = jnp.broadcast_to(square, (8, 128))
    over_chan = ToAll("chan", nc, r.sq, r.sqs, r.sq_s, r.sq_r)
    over_chan.start()
    lax.fori_loop(nd // 2, nd, change, 0)
    over_chan.finish()
    square = over_chan.total()[0:1, 0:1]
    norm = jnp.sqrt(square)
    factor = sam_radius * lax.rsqrt(square + norm_floor)

    gain1, shift1 = gain1 + factor * gg1, shift1 + factor * sh1
    gain2, shift2 = gain2 + factor * gg2, shift2 + factor * sh2
    r.a1[...] += factor * r.g1[...]
    hi, lo = split(r.a1[...])
    r.a_cat[0] = jnp.concatenate([hi, hi, lo], axis=1)

    act_copy = lambda sem, ys, i, z_to, y_to: send(
        r.act2.at[ys, i], r.act2.at[ys, i], r.act_s.at[sem, i], r.act_r.at[ys, i], (z_to * ny + y_to, c)
    )
    act_up = lambda i: act_copy(0, y, i, lax.min(z + 1, nz - 1), y)
    act_down = lambda i: act_copy(1, y, i, lax.max(z - 1, 0), y)
    act_side = lambda i: act_copy(2, y, i, z, 1 - y)

    def act_hand_on(i):
        pl.when((z >= start_z) & (z < nz - 1))(lambda: act_up(i).start())
        pl.when((z <= start_z) & (z > 0))(lambda: act_down(i).start())
        act_side(i).start()

    def second_act(i):
        val = val_of(i)
        act, slope = silu_and_slope((r.sums[i] - center2) * rs2 * gain2 + shift2)
        r.slope2[i] = slope * val
        r.own2[i] = act * val

    def far_to_core(j):
        zs = nearest(z, lax.div(j, 2))
        pl.when(lax.rem(j, 2) == 1)(lambda: column(far, zs).wait_recv())
        call_copy(1, far, image(j)).start()

    away = lax.max(z - start_z, start_z - z)

    def act_step(t):
        for i in range(nd):

            @pl.when((away > 0) & (t == lax.div(ACT[0] + ACT[1] * away + ACT[2] * i, 4)))
            def _():
                act_copy(0, y, i, z, 1 - y).wait_recv()
                act_hand_on(i)

    pair = lambda s, q: r.dall.at[s, pl.ds(2 * q, 2)]
    grads = Line(p, lambda s: pair(s, c), r.d_s, r.d_r)
    to_far = lambda s, q: send(pair(s, q), pair(s, q), r.far_s.at[s], r.far_r.at[s], (d, far))
    to_core = lambda lane, s, q: send(pair(s, q), pair(s, q), r.core_s.at[lane, s], r.core_r.at[lane, s], (d, across))

    def over_chan_too(s):
        to_far(s, c).start()
        to_core(0, s, c).start()

    def meet_sides(step):
        def one(zs):
            grads.got(zs, 1 - y)
            over_chan_too(zs * ny + 1 - y)

        pl.when(z >= step)(lambda: one(lax.max(z - step, 0)))
        if step > 0:
            pl.when(z + step < nz)(lambda: one(lax.min(z + step, nz - 1)))

    hi, lo = split(r.a1[...].T)
    r.bm[0], r.bm[1] = hi, lo
    ins_grad = ImageSum(p, r.inp, r.inn, r.inc, r.inw, r.i_s1, r.i_r1, r.i_s2, r.i_r2)
    r.add1[...] = jnp.zeros_like(r.add1)
    r.add2[...] = jnp.zeros_like(r.add2)

    def inner_grad(i):
        second_act(i)
        dpre = (r.sums[nd + i] + factor * r.sums[2 * nd + i]) * r.slope2[i]
        r.dall[d, i] = gain2 * rs2 * dpre
        r.add2[0] += dpre
        r.add2[1] += dpre * ((r.sums[i] - center2) * rs2)

        @pl.when(z == start_z)
        def _():
            r.act2[y, i] = r.own2[i]
            act_hand_on(i)

    def rows_grad(i):
        set_cols(1, shifts(r.dall[d, i], side, -1))
        dact1 = im2col_dot(1, (r.bm[0], r.bm[1]))
        r.inp[i] = dact1
        dpre1 = dact1 * r.slope1[i]
        r.add1[0] += dpre1
        r.add1[1] += dpre1 * ((r.xin[i] - center1) * rs1)

    same = lambda j: j

    def start(j, _):
        settle(nd + j)
        first_map(j, gain1, shift1)
        chan.advance(nd + j, nd, change_item)
        chan.advance(j, nd, same)
        return 0

    def steady(j, _):
        first_map(j, gain1, shift1)
        chan.advance(j, nd, same)
        settle(nd + j)
        inner_grad(j - 4)
        far_to_core(j - 4)
        act_step(j)
        return 0

    def end(j, _):
        chan.advance(j, nd, same)
        settle(nd + j)
        inner_grad(j - 4)
        far_to_core(j - 4)
        act_step(j)
        return 0

    lax.fori_loop(0, 4, start, 0)
    lax.fori_loop(4, nd, steady, 0)
    lax.fori_loop(nd, nd + 4, end, 0)
    grads.hand_on(z)
    back = lambda j: send(r.xs.at[lax.rem(c + j, nc)], r.rx.at[c], r.in_s.at[j], r.in_r.at[c], (d, lax.rem(c + j, nc)))

    def input_rows():
        grad = (gain1 * rs1 * (ins_grad.total() * r.slope1[d]) + r.call[c, d]).T
        for j in range(nc):
            r.xs[j] = grad[j * rows : (j + 1) * rows]
        for j in range(1, nc):
            back(j).start()
        r.rx[c] = r.xs[c]

    def gather_grads(u):
        for step in range(1, nz):
            pl.when(u == LINE_AT[step - 1])(lambda: meet(grads, step, lambda zs: over_chan_too(zs * ny + y)))
        for step in range(nz):
            pl.when(u == SIDE_AT[step])(lambda: meet_sides(step))

        @pl.when(u == NEAR_AT)
        def _():
            for o in range(nz):
                ins_grad.near(nearest(z, nz - 1 - o)).start()

        for o in range(nz):
            pl.when(u == SUMS_AT[o])(lambda: ins_grad.spread(nearest(z, nz - 1 - o)))
        pl.when(u == ROWS_AT)(input_rows)
        for zs in range(nz):
            pl.when(u == OUTS_AT[zs])(lambda: outs.spread(zs))

    def all_rows(i, _):
        rows_grad(i)
        act_step(nd + 4 + i)
        gather_grads(i)
        return 0

    lax.fori_loop(0, nd, all_rows, 0)
    sh1, gg1 = lanes_sum(r.add1[0]), lanes_sum(r.add1[1])
    sh2, gg2 = lanes_sum(r.add2[0]), lanes_sum(r.add2[1])

    pad = jnp.zeros((1, cb - db), F32)
    wide = lambda col: jnp.concatenate([to_row(col), pad], axis=1)
    r.vec[...] = stacked([to_row(sh1), to_row(gg1), wide(sh2), wide(gg2)], cb)
    vectors = ToAll("dp", nd, r.vec, r.vecs, r.vec_s, r.vec_r)
    vectors.start()

    def kernel_grad(images, left_of, rights_of, between):
        def put_left(m):
            for j, i in enumerate(images):
                lanes = slice(3 * j * px, 3 * (j + 1) * px)
                for t, v in enumerate(shifts(left_of(i), side, 1, (m - 1,))):
                    hi, lo = split(v)
                    r.left[(3 * m + t) * cb : (3 * m + t + 1) * cb, lanes] = jnp.concatenate([hi, hi, lo], axis=1)

        def add(m):
            third = slice(3 * m * cb, 3 * (m + 1) * cb)
            r.stage[third] += dot_nt(r.left[third], r.right[...])

        for j, i in enumerate(images):
            lanes = slice(3 * j * px, 3 * (j + 1) * px)
            at = 0
            for v in rights_of(i):
                n = v.shape[0]
                hi, lo = split(v)
                r.right[at : at + n, lanes] = jnp.concatenate([hi, lo, hi], axis=1)
                at += n
        put_left(0)
        add(0)
        put_left(1)
        between(0)
        add(1)
        put_left(2)
        between(1)
        add(2)
        between(2)

    r.stage[...] = jnp.zeros_like(r.stage)

    def second_kernel(q, _):
        zs = nearest(z, q)
        for j in range(2):
            act_copy(0, 1 - y, 2 * q + j, z, 1 - y).wait_recv()
            call_copy(0, across, 2 * q + j).wait_recv()
            call_copy(1, last, 2 * q + j).wait_recv()

        def between(m):
            u = nd + 3 * q + m
            act_step(nd + 4 + u)
            gather_grads(u)

        kernel_grad(
            [2 * q, 2 * q + 1],
            lambda i: jnp.concatenate([r.act2[0, i], r.act2[1, i]], axis=0),
            lambda i: [r.call[j, i] for j in range(nc)],
            between,
        )
        return 0

    lax.fori_loop(0, nz, second_kernel, 0)
    g2_copy = pltpu.make_async_copy(r.stage, r.g2_out, r.g2_sem)
    g2_copy.start()

    gather_grads(20)
    g2_copy.wait()
    r.stage[...] = jnp.zeros_like(r.stage)

    def first_kernel(j, _):
        @pl.when(j == 1)
        def _():
            for o in range(1, nd):
                to_core(0, lax.rem(d + o, nd), across).wait_recv()

        @pl.when(j == 2)
        def _():
            for o in range(1, nd):
                s = lax.rem(d + o, nd)
                to_far(s, far).wait_recv()
                to_core(1, s, far).start()

        @pl.when(j == 3)
        def _():
            for o in range(1, nd):
                to_core(1, lax.rem(d + o, nd), last).wait_recv()

        q = jnp.where(j == 0, c, jnp.where(j == 1, across, jnp.where(j == 2, far, last)))

        def between(m):
            gather_grads(21 + 3 * j + m)

        kernel_grad([2 * q, 2 * q + 1], lambda i: r.act1[i], lambda i: [r.dall[s, i] for s in slots], between)
        return 0

    lax.fori_loop(0, nc, first_kernel, 0)
    gather_grads(33)
    r.block_out[...] = ((r.xin[d] + outs.total()) * mine).T
    g1_copy = pltpu.make_async_copy(r.stage, r.g1_out, r.g1_sem)
    g1_copy.start()

    vectors.finish()
    total = vectors.total()
    rows_of = lambda j: jnp.concatenate([r.vecs[start_z * ny + q, j : j + 1, :db] for q in range(ny)], axis=1)
    r.small[...] = stacked([total[0:1], total[1:2], rows_of(2), rows_of(3), jnp.broadcast_to(norm, (1, cb))], cb)
    for j in range(1, nc):
        back(j).wait_send()
        other = lax.rem(c + j, nc)
        send(r.xs.at[other], r.rx.at[other], r.in_s.at[0], r.in_r.at[other], (d, other)).wait_recv()
    for j in range(nc):
        r.input_grad[:, j * cb : (j + 1) * cb] = r.rx[j]

    own_cot(c).wait_send()
    for line in (ins, cots, fars, grads):
        line.drain()
    for zs in range(nz):
        column(c, zs).wait_send()

    @pl.when(c == owner)
    def _():
        for j in range(1, nc):
            piece(j).wait_send()

    def sent(i, _):
        call_copy(0, c, i).wait_send()
        call_copy(1, far, i).wait_send()
        pl.when((z >= start_z) & (z < nz - 1))(lambda: act_up(i).wait_send())
        pl.when((z <= start_z) & (z > 0))(lambda: act_down(i).wait_send())
        act_side(i).wait_send()
        return 0

    lax.fori_loop(0, nd, sent, 0)
    for j in range(1, nd):
        s = lax.rem(d + j, nd)
        to_far(s, c).wait_send()
        to_core(0, s, c).wait_send()
        to_core(1, s, far).wait_send()
    g1_copy.wait()


def close_kernel(pieces, small, block_in, rows_in, first_in, second_in, block_out, rows_out, first_out, second_out,
                 gg1, sh1, gg2, sh2, norm, first, second, vec, sems, side_sems):
    cut = first_in.shape[0] // pieces
    legs = []
    for j in range(pieces):
        part = pl.ds(j * cut, cut)
        for k, (src, mid, dst) in enumerate(((second_in, second, second_out), (first_in, first, first_out))):
            legs.append((
                pltpu.make_async_copy(src.at[part], mid.at[part], sems.at[0, k, j]),
                pltpu.make_async_copy(mid.at[part], dst.at[part], sems.at[1, k, j]),
            ))
    sides = [pltpu.make_async_copy(a, b, side_sems.at[j])
             for j, (a, b) in enumerate(((small, vec), (block_in, block_out), (rows_in, rows_out)))]
    for cp in sides:
        cp.start()
    for come, _ in legs:
        come.start()
    sides[0].wait()
    for j, ref in enumerate((sh1, gg1, sh2, gg2)):
        ref[...] = vec[j : j + 1].reshape(vec.shape[1])
    norm[0] = jnp.sum(vec[4:5, 0:1])
    for come, go in legs:
        come.wait()
        go.start()
    for _, go in legs:
        go.wait()
    for cp in sides[1:]:
        cp.wait()


def fused_on_device(p, image_rows, groups, conv_first, conv_second, gain_first, shift_first, gain_second, shift_second, cotangent):
    cb, px = p.cb, p.px
    rows = px // p.nc
    scratch = scratch_of(p)
    out = lambda *s: jax.ShapeDtypeStruct(s, F32)
    any_, vmem, smem = (pl.BlockSpec(memory_space=m) for m in (pl.ANY, VMEM, SMEM))
    large = (out(px, cb), out(rows, p.ch), out(9 * cb, p.ch), out(9 * cb, p.ch))
    block_out, input_grad, g1, g2, small = pl.pallas_call(
        functools.partial(step_kernel, p, ARGS + OUTS + tuple(scratch)),
        out_shape=large + (out(8, cb),),
        in_specs=[vmem, vmem, any_, any_, vmem, vmem, vmem, vmem, smem],
        out_specs=(vmem, vmem, any_, any_, vmem),
        scratch_shapes=list(scratch.values()),
        compiler_params=pltpu.CompilerParams(collective_id=0, has_side_effects=True, vmem_limit_bytes=LIMIT),
    )(
        image_rows.reshape(rows, p.ch), cotangent.reshape(px, cb), conv_first.reshape(9, cb, p.ch),
        conv_second.reshape(9, cb, p.ch), gain_first, shift_first, gain_second, shift_second, groups,
    )
    pieces = 6
    block_out, input_grad, g1, g2, gg1, sh1, gg2, sh2, norm = pl.pallas_call(
        functools.partial(close_kernel, pieces),
        out_shape=large + (out(cb),) * 4 + (out(1),),
        in_specs=[any_] * 5,
        out_specs=(vmem, vmem, any_, any_) + (vmem,) * 4 + (smem,),
        scratch_shapes=[VMEM((9 * cb, p.ch), F32), VMEM((9 * cb, p.ch), F32), VMEM((8, cb), F32), DMA((2, 2, pieces)), DMA((3,))],
        compiler_params=pltpu.CompilerParams(vmem_limit_bytes=LIMIT),
    )(small, block_out, input_grad, g1, g2)
    return (
        block_out.reshape(cotangent.shape), input_grad.reshape(image_rows.shape),
        g1.reshape(conv_first.shape), g2.reshape(conv_second.shape), gg1, sh1, gg2, sh2, norm.reshape(()),
    )


def valid_pixels(groups, extent_full):
    places = jnp.arange(extent_full, dtype=jnp.int32)
    extent = jnp.where(groups == 1, extent_full, extent_full // 2).astype(jnp.int32)
    inside = places[None, :] < extent[:, None]
    return (inside[:, :, None] & inside[:, None, :]).astype(jnp.float32)[..., None]


def convolve(values, kernel):
    return lax.conv_general_dilated(
        values,
        kernel,
        (1, 1),
        "SAME",
        dimension_numbers=("NHWC", "HWIO", "NHWC"),
        precision=lax.Precision.HIGHEST,
    )


def silu_slope(preact):
    sigmoid = jax.nn.sigmoid(preact)
    return sigmoid * (1.0 + preact * (1.0 - sigmoid))


def batch_moments(values, validity):
    summed, squares, pixels = lax.psum(
        (
            jnp.sum(values * validity, axis=(0, 1, 2)),
            jnp.sum(validity * values * values, axis=(0, 1, 2)),
            jnp.sum(validity),
        ),
        "dp",
    )
    center = summed / pixels
    spread = squares / pixels - center * center
    return (center, lax.rsqrt(spread + epsilon), pixels)


def project_over_chan(values, kernel):
    return lax.psum_scatter(convolve(values, kernel), "chan", scatter_dimension=3, tiled=True)


def conv_backward(upstream, values, kernel):
    columns = lax.all_gather(upstream, "chan", axis=3, tiled=True)
    offset = jnp.int32(0)
    inputs_grad = jnp.zeros_like(values)
    kernel_grad = jnp.zeros_like(kernel)
    breadth = columns.shape[3]
    kernel_part = lax.dynamic_slice_in_dim(kernel, offset, breadth, 3)
    primal, pull = jax.vjp(convolve, values, kernel_part)
    values_part, kernel_part_grad = pull(columns)
    kernel_grad = lax.dynamic_update_slice_in_dim(kernel_grad, kernel_part_grad, offset, 3)
    return (inputs_grad + values_part, kernel_grad)


def batch_sums(dpre, scaled):
    return lax.psum((jnp.sum(dpre, axis=(0, 1, 2)), jnp.sum(dpre * scaled, axis=(0, 1, 2))), "dp")


def plain_on_device(
    image_rows,
    groups,
    conv_first,
    conv_second,
    gain_first,
    shift_first,
    gain_second,
    shift_second,
    cotangent,
):
    inputs = lax.all_to_all(image_rows, "chan", split_axis=3, concat_axis=1, tiled=True)
    validity = valid_pixels(groups, inputs.shape[1])
    cot_valid = cotangent * validity
    center_one, rscale_one, pixels = batch_moments(inputs, validity)
    scaled_one = (inputs - center_one) * rscale_one
    pre_one = scaled_one * gain_first + shift_first
    act_one = jax.nn.silu(pre_one) * validity
    inner = project_over_chan(act_one, conv_first) * validity
    center_two, rscale_two, pixels_again = batch_moments(inner, validity)
    scaled_two = (inner - center_two) * rscale_two
    pre_two = scaled_two * gain_second + shift_second
    act_two = jax.nn.silu(pre_two) * validity
    block_out = inputs * validity + project_over_chan(act_two, conv_second) * validity
    dact_two, kernel_two_part = conv_backward(cot_valid, act_two, conv_second)
    dpre_two = dact_two * validity * silu_slope(pre_two)
    shift_two_grad, gain_two_grad = batch_sums(dpre_two, scaled_two)
    dinner = (
        gain_second
        * rscale_two
        * (dpre_two - validity * (shift_two_grad + scaled_two * gain_two_grad) / pixels)
    )
    dact_one, kernel_one_part = conv_backward(dinner, act_one, conv_first)
    dpre_one = dact_one * validity * silu_slope(pre_one)
    shift_one_grad, gain_one_grad = batch_sums(dpre_one, scaled_one)
    small_squares = (
        jnp.sum(gain_one_grad**2)
        + jnp.sum(shift_one_grad**2)
        + jnp.sum(gain_two_grad**2)
        + jnp.sum(shift_two_grad**2)
    )
    kernel_one_sum, kernel_two_sum = lax.psum((kernel_one_part, kernel_two_part), "dp")
    local_sq = jnp.sum(kernel_one_sum**2) + jnp.sum(kernel_two_sum**2) + small_squares
    squares = lax.psum(local_sq, "chan")
    factor = sam_radius * lax.rsqrt(squares + norm_floor)
    kernel_one = conv_first + factor * kernel_one_sum
    kernel_two = conv_second + factor * kernel_two_sum
    grad_norm = jnp.sqrt(squares)
    moved_gain_one = gain_first + factor * gain_one_grad
    moved_shift_one = shift_first + factor * shift_one_grad
    moved_gain_two = gain_second + factor * gain_two_grad
    moved_shift_two = shift_second + factor * shift_two_grad
    pre_one_new = scaled_one * moved_gain_one + moved_shift_one
    act_one_new = jax.nn.silu(pre_one_new) * validity
    inner_new = project_over_chan(act_one_new, kernel_one) * validity
    scaled_two_new = (inner_new - center_two) * rscale_two
    pre_two_new = scaled_two_new * moved_gain_two + moved_shift_two
    act_two_new = jax.nn.silu(pre_two_new) * validity
    dact_two_new, kernel_two_grad = conv_backward(cot_valid, act_two_new, kernel_two)
    dpre_two_new = dact_two_new * validity * silu_slope(pre_two_new)
    gain_two_new_grad = jnp.sum(dpre_two_new * scaled_two_new, axis=(0, 1, 2))
    shift_two_new_grad = jnp.sum(dpre_two_new, axis=(0, 1, 2))
    dinner_new = moved_gain_two * rscale_two * dpre_two_new
    dact_one_new, kernel_one_grad = conv_backward(dinner_new, act_one_new, kernel_one)
    dpre_one_new = dact_one_new * validity * silu_slope(pre_one_new)
    gain_one_new_grad = jnp.sum(dpre_one_new * scaled_one, axis=(0, 1, 2))
    shift_one_new_grad = jnp.sum(dpre_one_new, axis=(0, 1, 2))
    inputs_grad = moved_gain_one * rscale_one * dpre_one_new + cot_valid
    input_grad = lax.all_to_all(inputs_grad, "chan", split_axis=1, concat_axis=3, tiled=True)
    (
        kernel_one_grad,
        kernel_two_grad,
        gain_one_new_grad,
        shift_one_new_grad,
        gain_two_new_grad,
        shift_two_new_grad,
    ) = lax.psum(
        (
            kernel_one_grad,
            kernel_two_grad,
            gain_one_new_grad,
            shift_one_new_grad,
            gain_two_new_grad,
            shift_two_new_grad,
        ),
        "dp",
    )
    return (
        block_out,
        input_grad,
        kernel_one_grad,
        kernel_two_grad,
        gain_one_new_grad,
        shift_one_new_grad,
        gain_two_new_grad,
        shift_two_new_grad,
        grad_norm,
    )


def solution(mesh):
    nd, nc = mesh.shape["dp"], mesh.shape["chan"]

    def on_device(image_rows, *rest):
        images, side, channels = image_rows.shape[0], image_rows.shape[2], image_rows.shape[3]
        fits = images == 1 and nc == 4 and nd == 2 * nc and channels // nd % 16 == 0 and side * side == 256
        if not fits:
            return plain_on_device(image_rows, *rest)
        return fused_on_device(Plan(nd, nc, channels, side), image_rows, *rest)

    return jax.shard_map(
        on_device,
        mesh=mesh,
        in_specs=(
            P("dp", "chan", None, None),
            P("dp"),
            P(None, None, "chan", None),
            P(None, None, "chan", None),
            P("chan"),
            P("chan"),
            P("chan"),
            P("chan"),
            P("dp", None, None, "chan"),
        ),
        out_specs=(
            P("dp", None, None, "chan"),
            P("dp", "chan", None, None),
            P(None, None, "chan", None),
            P(None, None, "chan", None),
            P("chan"),
            P("chan"),
            P("chan"),
            P("chan"),
            P(),
        ),
        check_vma=False,
    )
```

```python
import functools
import types

import jax
import jax.numpy as jnp
from jax import lax
from jax.experimental import pallas as pl
from jax.experimental.pallas import tpu as pltpu
from jax.sharding import PartitionSpec as P

epsilon = 1e-05
sam_radius = 0.05
norm_floor = 1e-06
MESH = pl.DeviceIdType.MESH
F32, BF16 = jnp.float32, jnp.bfloat16
VMEM, SMEM = pltpu.VMEM, pltpu.SMEM
DMA = pltpu.SemaphoreType.DMA
LIMIT = 60 << 20


class Plan:
    def __init__(self, nd, nc, channels, side):
        self.nd, self.nc, self.ch, self.side = nd, nc, channels, side
        self.cb, self.db, self.px = channels // nc, channels // nd, side * side
        self.ny = 2
        self.nz = nd // 2


def split(v):
    hi = v.astype(BF16)
    return hi, (v - hi.astype(F32)).astype(BF16)


def dot(a, b):
    return lax.dot_general(a, b, (((1,), (0,)), ((), ())), preferred_element_type=F32)


def dot_nt(a, b):
    return lax.dot_general(a, b, (((1,), (1,)), ((), ())), preferred_element_type=F32)


def edge_masks(side, px):
    lane = lax.broadcasted_iota(jnp.int32, (1, px), 1)
    col = lax.rem(lane, side)
    row = lax.div(lane, side)
    one = jnp.ones((1, px), F32)
    zero = jnp.zeros((1, px), F32)
    rows = {-1: jnp.where(row >= 1, one, zero), 0: None, 1: jnp.where(row < side - 1, one, zero)}
    cols = {-1: jnp.where(col >= 1, one, zero), 0: None, 1: jnp.where(col < side - 1, one, zero)}
    return rows, cols


def moved(v, lanes, mask):
    if lanes:
        v = pltpu.roll(v, (-lanes) % v.shape[1], axis=1)
    return v if mask is None else v * mask


def shifts(v, side, sign=1, taps=(-1, 0, 1)):
    rows, cols = edge_masks(side, v.shape[1])
    by_col = {s: moved(v, s, cols[s]) for s in (-1, 0, 1)}
    return [moved(by_col[sign * s], sign * r * side, rows[sign * r]) for r in taps for s in (-1, 0, 1)]


def gather_taps(prod, side, n):
    rows, cols = edge_masks(side, prod.shape[1])
    total = None
    for j, s in enumerate((-1, 0, 1)):
        part = None
        for i, r in enumerate((-1, 0, 1)):
            t = 3 * i + j
            m = moved(prod[t * n : (t + 1) * n], r * side, rows[r])
            part = m if part is None else part + m
        m = moved(part, s, cols[s])
        total = m if total is None else total + m
    return total


def sigmoid(t):
    return 1.0 / (1.0 + jnp.exp(-t))


def silu_and_slope(pre):
    s = sigmoid(pre)
    return pre * s, s * (1.0 + pre * (1.0 - s))


def lanes_sum(v):
    return jnp.sum(v, axis=1, keepdims=True)


def valid_map(flag, side, px):
    lane = lax.broadcasted_iota(jnp.int32, (1, px), 1)
    half = (lax.rem(lane, side) < side // 2) & (lax.div(lane, side) < side // 2)
    return jnp.where(half, jnp.ones((1, px), F32), flag)


def diagonal(n):
    return lax.broadcasted_iota(jnp.int32, (n, n), 0) == lax.broadcasted_iota(jnp.int32, (n, n), 1)


def to_row(col):
    return jnp.sum(jnp.where(diagonal(col.shape[0]), col, 0.0), axis=0, keepdims=True)


def to_col(row):
    return jnp.sum(jnp.where(diagonal(row.shape[1]), row, 0.0), axis=1, keepdims=True)


def stacked(rows, n):
    at = lax.broadcasted_iota(jnp.int32, (8, n), 0)
    out = jnp.zeros((8, n), F32)
    for k, row in enumerate(rows):
        out = jnp.where(at == k, row, out)
    return out


def send(src, dst, ss, rs, device):
    return pltpu.make_async_remote_copy(
        src_ref=src, dst_ref=dst, send_sem=ss, recv_sem=rs, device_id=device, device_id_type=MESH
    )


def here():
    return lax.axis_index("dp"), lax.axis_index("chan")


def greet(p):
    d, c = here()
    barrier = pltpu.get_barrier_semaphore()
    for j in range(1, p.nd):
        pl.semaphore_signal(barrier, inc=1, device_id=(lax.rem(d + j, p.nd), c), device_id_type=MESH)
    for j in range(1, p.nc):
        pl.semaphore_signal(barrier, inc=1, device_id=(d, lax.rem(c + j, p.nc)), device_id_type=MESH)
    pl.semaphore_wait(barrier, p.nd - 1 + p.nc - 1)


class ToAll:
    def __init__(self, axis, n, tile, slots, ss, rs):
        d, c = here()
        self.n, self.tile, self.slots, self.ss, self.rs = n, tile, slots, ss, rs
        self.me = d if axis == "dp" else c
        self.device = (lambda o: (o, c)) if axis == "dp" else (lambda o: (d, o))

    def start(self):
        self.slots[self.me] = self.tile[...]
        for j in range(1, self.n):
            to = lax.rem(self.me + j, self.n)
            send(self.tile, self.slots.at[self.me], self.ss.at[j], self.rs.at[self.me], self.device(to)).start()

    def finish(self):
        for j in range(1, self.n):
            other = lax.rem(self.me + j, self.n)
            send(self.tile, self.slots.at[other], self.ss.at[j], self.rs.at[other], self.device(other)).wait()

    def total(self):
        total = self.slots[0]
        for j in range(1, self.n):
            total = total + self.slots[j]
        return total


class Line:
    def __init__(self, p, view, ss, rs, sides=True):
        self.p, self.view, self.ss, self.rs, self.sides = p, view, ss, rs, sides
        d, self.c = here()
        self.z, self.y = lax.div(d, p.ny), lax.rem(d, p.ny)

    def copy(self, zs, sem, z_to, y_to):
        slot = zs * self.p.ny + self.y
        return send(self.view(slot), self.view(slot), self.ss.at[sem, zs], self.rs.at[slot], (z_to * self.p.ny + y_to, self.c))

    def up(self, zs):
        return self.copy(zs, 0, lax.min(self.z + 1, self.p.nz - 1), self.y)

    def down(self, zs):
        return self.copy(zs, 1, lax.max(self.z - 1, 0), self.y)

    def side(self, zs):
        return self.copy(zs, 2, self.z, 1 - self.y)

    def got(self, zs, y):
        slot = zs * self.p.ny + y
        send(self.view(slot), self.view(slot), self.ss.at[0, 0], self.rs.at[slot], (self.z * self.p.ny + 1 - self.y, self.c)).wait_recv()

    def hand_on(self, zs):
        pl.when((zs <= self.z) & (self.z < self.p.nz - 1))(lambda: self.up(zs).start())
        pl.when((zs >= self.z) & (self.z > 0))(lambda: self.down(zs).start())
        if self.sides:
            self.side(zs).start()

    def drain(self):
        for zs in range(self.p.nz):
            pl.when((zs <= self.z) & (self.z < self.p.nz - 1))(lambda: self.up(zs).wait_send())
            pl.when((zs >= self.z) & (self.z > 0))(lambda: self.down(zs).wait_send())
            if self.sides:
                self.side(zs).wait_send()


def nearest(z, k):
    t = lax.div(z, 2)
    low = z + t * (3 - 2 * z)
    first = 1 - lax.min(lax.div(k, 2), 1)
    place = k + low * first * (1 - 2 * k)
    return place * (1 - 2 * t) + 3 * t


class ChanSum:
    def __init__(self, p, r):
        self.p, self.r = p, r
        d, c = here()
        k = lax.rem(c, 2)
        self.hb = p.db // 2
        self.across, self.far = (d, c + 1 - 2 * k), (d, lax.rem(c + 2, 4))
        self.mine = pl.multiple_of(k * self.hb, 8)
        self.yours = pl.multiple_of((1 - k) * self.hb, 8)

    def first(self, i):
        r = self.r
        return send(r.part.at[i, pl.ds(self.yours, self.hb)], r.near.at[i], r.cs1.at[i], r.cr1.at[i], self.across)

    def second(self, i):
        r = self.r
        return send(r.half.at[i], r.away.at[i], r.cs2.at[i], r.cr2.at[i], self.far)

    def third(self, i, rows):
        r = self.r
        mine = r.sums.at[i, pl.ds(self.mine, self.hb)]
        return send(mine, r.sums.at[i, pl.ds(rows, self.hb)], r.cs3.at[i], r.cr3.at[i], self.across)

    def chip(self, i):
        r = self.r
        self.first(i).wait()
        r.half[i] = r.part[i, pl.ds(self.mine, self.hb)] + r.near[i]
        self.second(i).start()

    def cross(self, i):
        r = self.r
        self.second(i).wait()
        r.sums[i, pl.ds(self.mine, self.hb)] = r.half[i] + r.away[i]
        self.third(i, self.mine).start()

    def done(self, i):
        self.third(i, self.yours).wait()

    def advance(self, j, n, item):
        at = lambda m: item(lax.clamp(0, m, n - 1))
        pl.when((j >= 1) & (j < n + 1))(lambda: self.chip(at(j - 1)))
        pl.when((j >= 3) & (j < n + 3))(lambda: self.cross(at(j - 3)))
        pl.when((j >= 4) & (j < n + 4))(lambda: self.done(at(j - 4)))


class ImageSum:
    def __init__(self, p, part, near, acc, away, s1, r1, s2, r2):
        self.p, self.part, self.buf1, self.acc, self.buf2 = p, part, near, acc, away
        self.s1, self.r1, self.s2, self.r2 = s1, r1, s2, r2
        d, self.c = here()
        self.z, self.y = lax.div(d, p.ny), lax.rem(d, p.ny)

    def near(self, zs):
        side = 1 - self.y
        return send(self.part.at[zs * self.p.ny + side], self.buf1.at[zs], self.s1.at[zs], self.r1.at[zs],
                    (self.z * self.p.ny + side, self.c))

    def away(self, zs, slot):
        return send(self.acc.at[zs], self.buf2.at[slot], self.s2.at[zs], self.r2.at[slot], (zs * self.p.ny + self.y, self.c))

    def spread(self, zs):
        self.near(zs).wait()
        self.acc[zs] = self.part[zs * self.p.ny + self.y] + self.buf1[zs]
        pl.when(zs != self.z)(lambda: self.away(zs, self.z).start())

    def total(self):
        total = self.acc[self.z]
        for j in range(1, self.p.nz):
            other = lax.rem(self.z + j, self.p.nz)
            self.away(other, other).wait()
            total = total + self.buf2[other]
        return total


def scratch_of(p):
    nd, nc, cb, db, px, nz, ny = p.nd, p.nc, p.cb, p.db, p.px, p.nz, p.ny
    rows = px // nc
    f = lambda *s: VMEM(s, F32)
    h = lambda *s: VMEM(s, BF16)
    return dict(
        k1w=f(9, cb, 256), k2w=f(9, db, p.ch), ks=f(nc, cb, 9 * db), b2=f(cb, 9 * db),
        a1=f(9 * db, cb), a2=f(9 * db, cb), g1=f(9 * db, cb), g2=f(9 * db, cb),
        a_cat=h(2, 9 * db, 3 * cb), bm=h(2, cb, 9 * db), b2m=h(2, cb, 9 * db), colh=h(2, 9 * db, px), coll=h(2, 9 * db, px),
        xs=f(nc, rows, cb), rx=f(nc, rows, cb), xin=f(nd, cb, px), act1=f(nd, cb, px), slope1=f(nd, cb, px),
        call=f(nc, nd, cb, px),
        part=f(3 * nd, db, px), near=f(3 * nd, db // 2, px), half=f(3 * nd, db // 2, px), away=f(3 * nd, db // 2, px),
        sums=f(3 * nd, db, px), slope2=f(nd, db, px), dpre=f(nd, db, px), add1=f(2, cb, px), add2=f(2, db, px),
        outp=f(nd, cb, px), outn=f(nz, cb, px), outc=f(nz, cb, px), outw=f(nz, cb, px),
        inp=f(nd, cb, px), inn=f(nz, cb, px), inc=f(nz, cb, px), inw=f(nz, cb, px),
        dall=f(nd, nd, db, px), act2=f(ny, nd, db, px), own2=f(nd, db, px), left=h(9 * cb, 6 * px), right=h(p.ch, 6 * px),
        stage=f(9 * cb, p.ch),
        par=f(8, cb), pars=f(nc, 8, cb), stat=f(8, cb), stats=f(nd, 8, cb), msg=f(8, cb), msgs=f(nd, 8, cb),
        sq=f(8, 128), sqs=f(nc, 8, 128), vec=f(8, cb), vecs=f(nd, 8, cb),
        k1_sem=DMA, k2_sem=DMA, g1_sem=DMA, g2_sem=DMA,
        xs_s=DMA((nc,)), xs_r=DMA((nc,)), ks_s=DMA((nc,)), ks_r=DMA,
        par_s=DMA((nc,)), par_r=DMA((nc,)), stat_s=DMA((nd,)), stat_r=DMA((nd,)), msg_s=DMA((nd,)), msg_r=DMA((nd,)),
        sq_s=DMA((nc,)), sq_r=DMA((nc,)), vec_s=DMA((nd,)), vec_r=DMA((nd,)),
        x_s=DMA((3, nz)), x_r=DMA((nd,)), c_s=DMA((3, nz)), c_r=DMA((nd,)), d_s=DMA((3, nz)), d_r=DMA((nd,)),
        cs1=DMA((3 * nd,)), cr1=DMA((3 * nd,)), cs2=DMA((3 * nd,)), cr2=DMA((3 * nd,)), cs3=DMA((3 * nd,)), cr3=DMA((3 * nd,)),
        o_s1=DMA((nz,)), o_r1=DMA((nz,)), o_s2=DMA((nz,)), o_r2=DMA((nz,)),
        i_s1=DMA((nz,)), i_r1=DMA((nz,)), i_s2=DMA((nz,)), i_r2=DMA((nz,)),
        call_s=DMA((2, nd)), call_r=DMA((2, nd)), own_s=DMA, f_s=DMA((3, nz)), f_r=DMA((nd,)), col_s=DMA((nz,)), act_s=DMA((3, nd)), act_r=DMA((ny, nd)),
        far_s=DMA((nd,)), far_r=DMA((nd,)), core_s=DMA((2, nd)), core_r=DMA((2, nd)), in_s=DMA((nc,)), in_r=DMA((nc,)),
    )


FARS = (3, 9, 13)
OUTS_AT = (24, 25, 26, 27)
ACT = (44, 8, 4)
LINE_AT = (5, 9, 12)
SIDE_AT = (6, 11, 14, 17)
NEAR_AT = 15
SUMS_AT = (18, 20, 22, 24)
ROWS_AT = 28

ARGS = ("x", "cot", "k1", "k2", "gain1", "shift1", "gain2", "shift2", "groups")
OUTS = ("block_out", "input_grad", "g1_out", "g2_out", "small")


def step_kernel(p, names, *refs):
    r = types.SimpleNamespace(**dict(zip(names, refs)))
    cb, db, px, side, nd, nc, nz, ny = p.cb, p.db, p.px, p.side, p.nd, p.nc, p.nz, p.ny
    d, c = here()
    z, y = lax.div(d, ny), lax.rem(d, ny)
    k = lax.rem(c, 2)
    far, across = lax.rem(c + 2, 4), c + 1 - 2 * k
    last = 6 - c - far - across
    rows = px // nc
    owner = (1 - lax.div(z, 2)) * (2 - 2 * lax.rem(z, 2)) + lax.div(z, 2) * (1 + 2 * lax.rem(z, 2))
    origin = lambda c: (1 - c // 2) * (1 + c % 2) + c // 2 * 3 * (c % 2)
    start_z = (1 - lax.div(c, 2)) * (1 + k) + lax.div(c, 2) * 3 * k
    first = owner * cb + y * db
    slots = [origin(q) * ny + j for q in range(nc) for j in range(ny)]
    image = lambda j: nearest(z, lax.div(j, 2)) * ny + y + lax.rem(j, 2) * (1 - 2 * y)

    base = lax.min(lax.div(first, 128), (p.ch - 256) // 128) * 128
    k1_copy = pltpu.make_async_copy(r.k1.at[:, :, pl.ds(pl.multiple_of(base, 128), 256)], r.k1w, r.k1_sem)
    k1_copy.start()
    k2_rows = pl.ds(pl.multiple_of(y * db, 8), db)
    k2_copy = pltpu.make_async_copy(r.k2.at[:, k2_rows], r.k2w, r.k2_sem)
    pl.when(c == owner)(lambda: k2_copy.start())
    greet(p)

    for j in range(nc):
        r.xs[j] = r.x[:, j * cb : (j + 1) * cb]
    a2a = lambda j: send(r.xs.at[lax.rem(c + j, nc)], r.rx.at[c], r.xs_s.at[j], r.xs_r.at[c], (d, lax.rem(c + j, nc)))
    for j in range(1, nc):
        a2a(j).start()
    r.rx[c] = r.xs[c]
    r.par[...] = stacked([r.gain2[...].reshape(1, cb), r.shift2[...].reshape(1, cb)], cb)
    params = ToAll("chan", nc, r.par, r.pars, r.par_s, r.par_r)
    params.start()
    flag = jnp.full((1, 1), jnp.where(r.groups[0] == 1, 1.0, 0.0), F32)
    mine = valid_map(flag, side, px)
    r.call[c, d] = r.cot[...].T * mine

    def meet(line, step, then=None):
        def one(zs):
            line.got(zs, y)
            line.hand_on(zs)
            if then is not None:
                then(zs)

        pl.when(z >= step)(lambda: one(lax.max(z - step, 0)))
        pl.when(z + step < nz)(lambda: one(lax.min(z + step, nz - 1)))

    cots = Line(p, lambda s: r.call.at[c, s], r.c_s, r.c_r)
    cots.hand_on(z)
    own_cot = lambda q: send(r.call.at[q, d], r.call.at[q, d], r.own_s, r.f_r.at[d], (d, far))
    fars = Line(p, lambda s: r.call.at[far, s], r.f_s, r.f_r, False)
    column = lambda q, zs: send(
        r.call.at[q, zs * ny + 1 - y], r.call.at[q, zs * ny + 1 - y], r.col_s.at[zs], r.f_r.at[zs * ny + 1 - y], (d, far)
    )
    call_copy = lambda lane, q, i: send(
        r.call.at[q, i], r.call.at[q, i], r.call_s.at[lane, i], r.call_r.at[lane, i], (d, across)
    )

    @pl.when(c == owner)
    def _():
        k2_copy.wait()
        for j in range(nc):
            r.ks[j] = r.k2w[:, :, j * cb : (j + 1) * cb].reshape(9 * db, cb).T

    for j in range(1, nc):
        a2a(j).wait_send()
        other = lax.rem(c + j, nc)
        send(r.xs.at[other], r.rx.at[other], r.xs_s.at[j], r.xs_r.at[other], (d, other)).wait_recv()
    r.xin[d] = r.rx[...].reshape(px, cb).T
    ins = Line(p, lambda s: r.xin.at[s], r.x_s, r.x_r)

    count = lanes_sum(mine)
    total = lanes_sum(r.xin[d] * mine)
    off = r.xin[d] - total / count
    r.stat[...] = stacked([to_row(total), to_row(lanes_sum(mine * off * off)), jnp.broadcast_to(flag, (1, cb))], cb)
    stats = ToAll("dp", nd, r.stat, r.stats, r.stat_s, r.stat_r)
    stats.start()
    ins.hand_on(z)

    piece = lambda j: send(r.ks.at[lax.rem(c + j, nc)], r.b2, r.ks_s.at[j], r.ks_r, (d, lax.rem(c + j, nc)))

    @pl.when(c == owner)
    def _():
        for j in range(1, nc):
            piece(j).start()

    k1_copy.wait()
    turn = lax.rem(256 - (first - base), 256)
    b1 = jnp.concatenate([pltpu.roll(r.k1w[t], turn, axis=1)[:, :db] for t in range(9)], axis=1)
    hi, lo = split(b1)
    r.bm[0], r.bm[1] = hi, lo
    r.a1[...] = b1.T
    hi, lo = split(r.a1[...])
    r.a_cat[0] = jnp.concatenate([hi, hi, lo], axis=1)

    meet(cots, 1)
    own_cot(c).start()
    stats.finish()

    def val_of(i):
        return valid_map(r.stats[i, 2:3, 0:1], side, px)

    counts = [jnp.sum(val_of(i), keepdims=True) for i in range(nd)]
    pixels = functools.reduce(jnp.add, counts)
    center = functools.reduce(jnp.add, [r.stats[i, 0:1] for i in range(nd)]) / pixels
    spread = [r.stats[i, 1:2] + counts[i] * (r.stats[i, 0:1] / counts[i] - center) ** 2 for i in range(nd)]
    center1, rs1 = to_col(center), to_col(lax.rsqrt(functools.reduce(jnp.add, spread) / pixels + epsilon))
    gain1, shift1 = to_col(r.gain1[...].reshape(1, cb)), to_col(r.shift1[...].reshape(1, cb))

    chan = ChanSum(p, r)

    def first_map(i, gain, shift):
        val = val_of(i)
        act, slope = silu_and_slope((r.xin[i] - center1) * rs1 * gain + shift)
        act = act * val
        r.act1[i], r.slope1[i] = act, slope * val
        ah, al = split(act)
        prod = dot(r.a_cat[0], jnp.concatenate([ah, al, ah], axis=0))
        r.part[i] = gather_taps(prod, side, db) * val
        chan.first(i).start()

    def second_back(i, first):
        ch, cl = split(r.call[c, i])
        prod = dot(r.a_cat[1], jnp.concatenate([ch, cl, ch], axis=0))
        r.part[first + i] = gather_taps(prod, side, db) * val_of(i)
        chan.first(first + i).start()

    def back_item(j):
        return nd + image(j)

    def set_back(a2):
        for t in range(9):
            hi, lo = split(a2[(8 - t) * db : (9 - t) * db])
            r.a_cat[1, t * db : (t + 1) * db] = jnp.concatenate([hi, hi, lo], axis=1)

    def second_block():
        @pl.when(c == owner)
        def _():
            r.b2[...] = r.ks[c]

        @pl.when(c != owner)
        def _():
            send(r.ks.at[0], r.b2, r.ks_s.at[0], r.ks_r, (d, owner)).wait_recv()

        r.a2[...] = r.b2[...].T
        set_back(r.a2)
        b2h, b2l = split(r.b2[...])
        r.b2m[0], r.b2m[1] = b2h, b2l

    def forward(kk, _):
        zs = nearest(z, kk)
        first_map(zs * ny + y, gain1, shift1)
        chan.advance(2 * kk, nd, image)
        meet(ins, kk + 1)
        pl.when(kk == 0)(lambda: meet(cots, 2))
        pl.when(kk == 1)(lambda: meet(cots, 3))
        pl.when(kk == 1)(second_block)
        ins.got(zs, 1 - y)
        first_map(zs * ny + 1 - y, gain1, shift1)
        chan.advance(2 * kk + 1, nd, image)

        @pl.when(kk > 0)
        def _():
            before = nearest(z, lax.max(kk - 1, 0))
            second_back(before * ny + y, nd)
            chan.advance(2 * kk - 2, nd, back_item)
            cots.got(before, 1 - y)
            second_back(before * ny + 1 - y, nd)
            chan.advance(2 * kk - 1, nd, back_item)

        return 0

    lax.fori_loop(0, nz, forward, 0)
    furthest = nearest(z, nz - 1)
    chan.advance(nd, nd, image)
    second_back(furthest * ny + y, nd)
    chan.advance(nd - 2, nd, back_item)
    chan.advance(nd + 1, nd, image)
    cots.got(furthest, 1 - y)
    second_back(furthest * ny + 1 - y, nd)
    chan.advance(nd - 1, nd, back_item)
    chan.advance(nd + 2, nd, image)
    chan.advance(nd, nd, back_item)
    chan.advance(nd + 3, nd, image)

    params.finish()
    both = [r.pars[owner, j : j + 1] for j in range(2)]
    gain2, shift2 = (to_col(jnp.where(y == 0, v[:, :db], v[:, cb - db :])) for v in both)

    def add_up(i, carry):
        return carry + lanes_sum(r.sums[i] * val_of(i))

    chan.advance(nd + 1, nd, back_item)
    center2 = lax.fori_loop(0, nd, add_up, jnp.zeros((db, 1), F32)) / pixels

    def add_squares(i, carry):
        off = r.sums[i] - center2
        return carry + lanes_sum(val_of(i) * off * off)

    chan.advance(nd + 2, nd, back_item)
    rs2 = lax.rsqrt(lax.fori_loop(0, nd, add_squares, jnp.zeros((db, 1), F32)) / pixels + epsilon)

    chan.advance(nd + 3, nd, back_item)
    own_cot(far).wait_recv()
    fars.hand_on(z)
    for zs in range(nz):
        column(c, zs).start()

    def inner_sums(i, carry):
        val = val_of(i)
        scaled = (r.sums[i] - center2) * rs2
        act, slope = silu_and_slope(scaled * gain2 + shift2)
        r.own2[i] = act * val
        dpre = r.sums[nd + i] * (slope * val)
        r.dpre[i] = dpre
        return carry[0] + lanes_sum(dpre), carry[1] + lanes_sum(dpre * scaled)

    zero = jnp.zeros((db, 1), F32)
    sh2, gg2 = lax.fori_loop(0, nd, inner_sums, (zero, zero))

    outs = ImageSum(p, r.outp, r.outn, r.outc, r.outw, r.o_s1, r.o_r1, r.o_s2, r.o_r2)

    def set_cols(w, maps):
        for t, m in enumerate(maps):
            hi, lo = split(m)
            r.colh[w, t * db : (t + 1) * db] = hi
            r.coll[w, t * db : (t + 1) * db] = lo

    def im2col_dot(w, which):
        return dot(which[0], r.colh[w]) + dot(which[0], r.coll[w]) + dot(which[1], r.colh[w])

    def wgrad(w, other):
        oh, ol = split(other)
        left = jnp.concatenate([r.colh[w], r.colh[w], r.coll[w]], axis=1)
        return dot_nt(left, jnp.concatenate([oh, ol, oh], axis=1))

    r.g1[...] = jnp.zeros_like(r.g1)
    r.g2[...] = jnp.zeros_like(r.g2)
    change_item = lambda j: 2 * nd + j

    def settle(t):
        for step in range(1, nz):
            pl.when(t == FARS[step - 1])(lambda: meet(fars, step))

    def gradients(i, carry):
        scaled = (r.sums[i] - center2) * rs2
        dinner = gain2 * rs2 * (r.dpre[i] - val_of(i) * (sh2 + scaled * gg2) / pixels)
        set_cols(0, shifts(r.own2[i], side))
        set_cols(1, shifts(dinner, side, -1))
        r.outp[i] = im2col_dot(0, (r.b2m[0], r.b2m[1]))
        r.g2[...] += wgrad(0, r.call[c, i])
        r.g1[...] += wgrad(1, r.act1[i])
        dpre1 = im2col_dot(1, (r.bm[0], r.bm[1])) * r.slope1[i]
        scaled1 = (r.xin[i] - center1) * rs1
        pl.when((lax.rem(i, 2) == 1 - y) & (i < 2 * nz - 2))(lambda: outs.near(lax.div(i, 2)).start())
        call_copy(0, c, i).start()
        settle(i)
        return carry[0] + lanes_sum(dpre1), carry[1] + lanes_sum(dpre1 * scaled1)

    zero = jnp.zeros((cb, 1), F32)
    sh1, gg1 = lax.fori_loop(0, nd, gradients, (zero, zero))
    set_back(r.g2)

    square = jnp.sum(r.g1[...] * r.g1[...] + r.g2[...] * r.g2[...], keepdims=True)
    square = square + jnp.where(c == 0, jnp.sum(sh2 * sh2 + gg2 * gg2, keepdims=True), 0.0)
    r.msg[...] = stacked([to_row(sh1), to_row(gg1), jnp.broadcast_to(square, (1, cb))], cb)
    over_dp = ToAll("dp", nd, r.msg, r.msgs, r.msg_s, r.msg_r)
    over_dp.start()
    outs.near(nz - 1).start()

    def change(j, _):
        second_back(j, 2 * nd)
        chan.advance(j, nd, change_item)
        return 0

    lax.fori_loop(0, nd // 2, change, 0)
    over_dp.finish()
    total = over_dp.total()
    sh1, gg1 = to_col(total[0:1]), to_col(total[1:2])
    square = total[2:3, 0:1] + jnp.sum(sh1 * sh1 + gg1 * gg1, keepdims=True)
    r.sq[...] = jnp.broadcast_to(square, (8, 128))
    over_chan = ToAll("chan", nc, r.sq, r.sqs, r.sq_s, r.sq_r)
    over_chan.start()
    lax.fori_loop(nd // 2, nd, change, 0)
    over_chan.finish()
    square = over_chan.total()[0:1, 0:1]
    norm = jnp.sqrt(square)
    factor = sam_radius * lax.rsqrt(square + norm_floor)

    gain1, shift1 = gain1 + factor * gg1, shift1 + factor * sh1
    gain2, shift2 = gain2 + factor * gg2, shift2 + factor * sh2
    r.a1[...] += factor * r.g1[...]
    hi, lo = split(r.a1[...])
    r.a_cat[0] = jnp.concatenate([hi, hi, lo], axis=1)

    act_copy = lambda sem, ys, i, z_to, y_to: send(
        r.act2.at[ys, i], r.act2.at[ys, i], r.act_s.at[sem, i], r.act_r.at[ys, i], (z_to * ny + y_to, c)
    )
    act_up = lambda i: act_copy(0, y, i, lax.min(z + 1, nz - 1), y)
    act_down = lambda i: act_copy(1, y, i, lax.max(z - 1, 0), y)
    act_side = lambda i: act_copy(2, y, i, z, 1 - y)

    def act_hand_on(i):
        pl.when((z >= start_z) & (z < nz - 1))(lambda: act_up(i).start())
        pl.when((z <= start_z) & (z > 0))(lambda: act_down(i).start())
        act_side(i).start()

    def second_act(i):
        val = val_of(i)
        act, slope = silu_and_slope((r.sums[i] - center2) * rs2 * gain2 + shift2)
        r.slope2[i] = slope * val
        r.own2[i] = act * val

    def far_to_core(j):
        zs = nearest(z, lax.div(j, 2))
        pl.when(lax.rem(j, 2) == 1)(lambda: column(far, zs).wait_recv())
        call_copy(1, far, image(j)).start()

    away = lax.max(z - start_z, start_z - z)

    def act_step(t):
        for i in range(nd):

            @pl.when((away > 0) & (t == lax.div(ACT[0] + ACT[1] * away + ACT[2] * i, 4)))
            def _():
                act_copy(0, y, i, z, 1 - y).wait_recv()
                act_hand_on(i)

    pair = lambda s, q: r.dall.at[s, pl.ds(2 * q, 2)]
    grads = Line(p, lambda s: pair(s, c), r.d_s, r.d_r)
    to_far = lambda s, q: send(pair(s, q), pair(s, q), r.far_s.at[s], r.far_r.at[s], (d, far))
    to_core = lambda lane, s, q: send(pair(s, q), pair(s, q), r.core_s.at[lane, s], r.core_r.at[lane, s], (d, across))

    def over_chan_too(s):
        to_far(s, c).start()
        to_core(0, s, c).start()

    def meet_sides(step):
        def one(zs):
            grads.got(zs, 1 - y)
            over_chan_too(zs * ny + 1 - y)

        pl.when(z >= step)(lambda: one(lax.max(z - step, 0)))
        if step > 0:
            pl.when(z + step < nz)(lambda: one(lax.min(z + step, nz - 1)))

    hi, lo = split(r.a1[...].T)
    r.bm[0], r.bm[1] = hi, lo
    ins_grad = ImageSum(p, r.inp, r.inn, r.inc, r.inw, r.i_s1, r.i_r1, r.i_s2, r.i_r2)
    r.add1[...] = jnp.zeros_like(r.add1)
    r.add2[...] = jnp.zeros_like(r.add2)

    def inner_grad(i):
        second_act(i)
        dpre = (r.sums[nd + i] + factor * r.sums[2 * nd + i]) * r.slope2[i]
        r.dall[d, i] = gain2 * rs2 * dpre
        r.add2[0] += dpre
        r.add2[1] += dpre * ((r.sums[i] - center2) * rs2)

        @pl.when(z == start_z)
        def _():
            r.act2[y, i] = r.own2[i]
            act_hand_on(i)

    def rows_grad(i):
        set_cols(1, shifts(r.dall[d, i], side, -1))
        dact1 = im2col_dot(1, (r.bm[0], r.bm[1]))
        r.inp[i] = dact1
        dpre1 = dact1 * r.slope1[i]
        r.add1[0] += dpre1
        r.add1[1] += dpre1 * ((r.xin[i] - center1) * rs1)

    same = lambda j: j

    def start(j, _):
        settle(nd + j)
        first_map(j, gain1, shift1)
        chan.advance(nd + j, nd, change_item)
        chan.advance(j, nd, same)
        return 0

    def steady(j, _):
        first_map(j, gain1, shift1)
        chan.advance(j, nd, same)
        settle(nd + j)
        inner_grad(j - 4)
        far_to_core(j - 4)
        act_step(j)
        return 0

    def end(j, _):
        chan.advance(j, nd, same)
        settle(nd + j)
        inner_grad(j - 4)
        far_to_core(j - 4)
        act_step(j)
        return 0

    lax.fori_loop(0, 4, start, 0)
    lax.fori_loop(4, nd, steady, 0)
    lax.fori_loop(nd, nd + 4, end, 0)
    grads.hand_on(z)
    back = lambda j: send(r.xs.at[lax.rem(c + j, nc)], r.rx.at[c], r.in_s.at[j], r.in_r.at[c], (d, lax.rem(c + j, nc)))

    def input_rows():
        grad = (gain1 * rs1 * (ins_grad.total() * r.slope1[d]) + r.call[c, d]).T
        for j in range(nc):
            r.xs[j] = grad[j * rows : (j + 1) * rows]
        for j in range(1, nc):
            back(j).start()
        r.rx[c] = r.xs[c]

    def gather_grads(u):
        for step in range(1, nz):
            pl.when(u == LINE_AT[step - 1])(lambda: meet(grads, step, lambda zs: over_chan_too(zs * ny + y)))
        for step in range(nz):
            pl.when(u == SIDE_AT[step])(lambda: meet_sides(step))

        @pl.when(u == NEAR_AT)
        def _():
            for o in range(nz):
                ins_grad.near(nearest(z, nz - 1 - o)).start()

        for o in range(nz):
            pl.when(u == SUMS_AT[o])(lambda: ins_grad.spread(nearest(z, nz - 1 - o)))
        pl.when(u == ROWS_AT)(input_rows)
        for zs in range(nz):
            pl.when(u == OUTS_AT[zs])(lambda: outs.spread(zs))

    def all_rows(i, _):
        rows_grad(i)
        act_step(nd + 4 + i)
        gather_grads(i)
        return 0

    lax.fori_loop(0, nd, all_rows, 0)
    sh1, gg1 = lanes_sum(r.add1[0]), lanes_sum(r.add1[1])
    sh2, gg2 = lanes_sum(r.add2[0]), lanes_sum(r.add2[1])

    pad = jnp.zeros((1, cb - db), F32)
    wide = lambda col: jnp.concatenate([to_row(col), pad], axis=1)
    r.vec[...] = stacked([to_row(sh1), to_row(gg1), wide(sh2), wide(gg2)], cb)
    vectors = ToAll("dp", nd, r.vec, r.vecs, r.vec_s, r.vec_r)
    vectors.start()

    def kernel_grad(images, left_of, rights_of, between):
        def put_left(m):
            for j, i in enumerate(images):
                lanes = slice(3 * j * px, 3 * (j + 1) * px)
                for t, v in enumerate(shifts(left_of(i), side, 1, (m - 1,))):
                    hi, lo = split(v)
                    r.left[(3 * m + t) * cb : (3 * m + t + 1) * cb, lanes] = jnp.concatenate([hi, hi, lo], axis=1)

        def add(m):
            third = slice(3 * m * cb, 3 * (m + 1) * cb)
            r.stage[third] += dot_nt(r.left[third], r.right[...])

        for j, i in enumerate(images):
            lanes = slice(3 * j * px, 3 * (j + 1) * px)
            at = 0
            for v in rights_of(i):
                n = v.shape[0]
                hi, lo = split(v)
                r.right[at : at + n, lanes] = jnp.concatenate([hi, lo, hi], axis=1)
                at += n
        put_left(0)
        add(0)
        put_left(1)
        between(0)
        add(1)
        put_left(2)
        between(1)
        add(2)
        between(2)

    r.stage[...] = jnp.zeros_like(r.stage)

    def second_kernel(q, _):
        zs = nearest(z, q)
        for j in range(2):
            act_copy(0, 1 - y, 2 * q + j, z, 1 - y).wait_recv()
            call_copy(0, across, 2 * q + j).wait_recv()
            call_copy(1, last, 2 * q + j).wait_recv()

        def between(m):
            u = nd + 3 * q + m
            act_step(nd + 4 + u)
            gather_grads(u)

        kernel_grad(
            [2 * q, 2 * q + 1],
            lambda i: jnp.concatenate([r.act2[0, i], r.act2[1, i]], axis=0),
            lambda i: [r.call[j, i] for j in range(nc)],
            between,
        )
        return 0

    lax.fori_loop(0, nz, second_kernel, 0)
    g2_copy = pltpu.make_async_copy(r.stage, r.g2_out, r.g2_sem)
    g2_copy.start()

    gather_grads(20)
    g2_copy.wait()
    r.stage[...] = jnp.zeros_like(r.stage)

    def first_kernel(j, _):
        @pl.when(j == 1)
        def _():
            for o in range(1, nd):
                to_core(0, lax.rem(d + o, nd), across).wait_recv()

        @pl.when(j == 2)
        def _():
            for o in range(1, nd):
                s = lax.rem(d + o, nd)
                to_far(s, far).wait_recv()
                to_core(1, s, far).start()

        @pl.when(j == 3)
        def _():
            for o in range(1, nd):
                to_core(1, lax.rem(d + o, nd), last).wait_recv()

        q = jnp.where(j == 0, c, jnp.where(j == 1, across, jnp.where(j == 2, far, last)))

        def between(m):
            gather_grads(21 + 3 * j + m)

        kernel_grad([2 * q, 2 * q + 1], lambda i: r.act1[i], lambda i: [r.dall[s, i] for s in slots], between)
        return 0

    lax.fori_loop(0, nc, first_kernel, 0)
    gather_grads(33)
    r.block_out[...] = ((r.xin[d] + outs.total()) * mine).T
    g1_copy = pltpu.make_async_copy(r.stage, r.g1_out, r.g1_sem)
    g1_copy.start()

    vectors.finish()
    total = vectors.total()
    rows_of = lambda j: jnp.concatenate([r.vecs[start_z * ny + q, j : j + 1, :db] for q in range(ny)], axis=1)
    r.small[...] = stacked([total[0:1], total[1:2], rows_of(2), rows_of(3), jnp.broadcast_to(norm, (1, cb))], cb)
    for j in range(1, nc):
        back(j).wait_send()
        other = lax.rem(c + j, nc)
        send(r.xs.at[other], r.rx.at[other], r.in_s.at[0], r.in_r.at[other], (d, other)).wait_recv()
    for j in range(nc):
        r.input_grad[:, j * cb : (j + 1) * cb] = r.rx[j]

    own_cot(c).wait_send()
    for line in (ins, cots, fars, grads):
        line.drain()
    for zs in range(nz):
        column(c, zs).wait_send()

    @pl.when(c == owner)
    def _():
        for j in range(1, nc):
            piece(j).wait_send()

    def sent(i, _):
        call_copy(0, c, i).wait_send()
        call_copy(1, far, i).wait_send()
        pl.when((z >= start_z) & (z < nz - 1))(lambda: act_up(i).wait_send())
        pl.when((z <= start_z) & (z > 0))(lambda: act_down(i).wait_send())
        act_side(i).wait_send()
        return 0

    lax.fori_loop(0, nd, sent, 0)
    for j in range(1, nd):
        s = lax.rem(d + j, nd)
        to_far(s, c).wait_send()
        to_core(0, s, c).wait_send()
        to_core(1, s, far).wait_send()
    g1_copy.wait()


def close_kernel(pieces, small, block_in, rows_in, first_in, second_in, block_out, rows_out, first_out, second_out,
                 gg1, sh1, gg2, sh2, norm, first, second, vec, sems, side_sems):
    cut = first_in.shape[0] // pieces
    legs = []
    for j in range(pieces):
        part = pl.ds(j * cut, cut)
        for k, (src, mid, dst) in enumerate(((second_in, second, second_out), (first_in, first, first_out))):
            legs.append((
                pltpu.make_async_copy(src.at[part], mid.at[part], sems.at[0, k, j]),
                pltpu.make_async_copy(mid.at[part], dst.at[part], sems.at[1, k, j]),
            ))
    sides = [pltpu.make_async_copy(a, b, side_sems.at[j])
             for j, (a, b) in enumerate(((small, vec), (block_in, block_out), (rows_in, rows_out)))]
    for cp in sides:
        cp.start()
    for come, _ in legs:
        come.start()
    sides[0].wait()
    for j, ref in enumerate((sh1, gg1, sh2, gg2)):
        ref[...] = vec[j : j + 1].reshape(vec.shape[1])
    norm[0] = jnp.sum(vec[4:5, 0:1])
    for come, go in legs:
        come.wait()
        go.start()
    for _, go in legs:
        go.wait()
    for cp in sides[1:]:
        cp.wait()


def fused_on_device(p, image_rows, groups, conv_first, conv_second, gain_first, shift_first, gain_second, shift_second, cotangent):
    cb, px = p.cb, p.px
    rows = px // p.nc
    scratch = scratch_of(p)
    out = lambda *s: jax.ShapeDtypeStruct(s, F32)
    any_, vmem, smem = (pl.BlockSpec(memory_space=m) for m in (pl.ANY, VMEM, SMEM))
    large = (out(px, cb), out(rows, p.ch), out(9 * cb, p.ch), out(9 * cb, p.ch))
    block_out, input_grad, g1, g2, small = pl.pallas_call(
        functools.partial(step_kernel, p, ARGS + OUTS + tuple(scratch)),
        out_shape=large + (out(8, cb),),
        in_specs=[vmem, vmem, any_, any_, vmem, vmem, vmem, vmem, smem],
        out_specs=(vmem, vmem, any_, any_, vmem),
        scratch_shapes=list(scratch.values()),
        compiler_params=pltpu.CompilerParams(collective_id=0, has_side_effects=True, vmem_limit_bytes=LIMIT),
    )(
        image_rows.reshape(rows, p.ch), cotangent.reshape(px, cb), conv_first.reshape(9, cb, p.ch),
        conv_second.reshape(9, cb, p.ch), gain_first, shift_first, gain_second, shift_second, groups,
    )
    pieces = 6
    block_out, input_grad, g1, g2, gg1, sh1, gg2, sh2, norm = pl.pallas_call(
        functools.partial(close_kernel, pieces),
        out_shape=large + (out(cb),) * 4 + (out(1),),
        in_specs=[any_] * 5,
        out_specs=(vmem, vmem, any_, any_) + (vmem,) * 4 + (smem,),
        scratch_shapes=[VMEM((9 * cb, p.ch), F32), VMEM((9 * cb, p.ch), F32), VMEM((8, cb), F32), DMA((2, 2, pieces)), DMA((3,))],
        compiler_params=pltpu.CompilerParams(vmem_limit_bytes=LIMIT),
    )(small, block_out, input_grad, g1, g2)
    return (
        block_out.reshape(cotangent.shape), input_grad.reshape(image_rows.shape),
        g1.reshape(conv_first.shape), g2.reshape(conv_second.shape), gg1, sh1, gg2, sh2, norm.reshape(()),
    )


def valid_pixels(groups, extent_full):
    places = jnp.arange(extent_full, dtype=jnp.int32)
    extent = jnp.where(groups == 1, extent_full, extent_full // 2).astype(jnp.int32)
    inside = places[None, :] < extent[:, None]
    return (inside[:, :, None] & inside[:, None, :]).astype(jnp.float32)[..., None]


def convolve(values, kernel):
    return lax.conv_general_dilated(
        values,
        kernel,
        (1, 1),
        "SAME",
        dimension_numbers=("NHWC", "HWIO", "NHWC"),
        precision=lax.Precision.HIGHEST,
    )


def silu_slope(preact):
    sigmoid = jax.nn.sigmoid(preact)
    return sigmoid * (1.0 + preact * (1.0 - sigmoid))


def batch_moments(values, validity):
    summed, squares, pixels = lax.psum(
        (
            jnp.sum(values * validity, axis=(0, 1, 2)),
            jnp.sum(validity * values * values, axis=(0, 1, 2)),
            jnp.sum(validity),
        ),
        "dp",
    )
    center = summed / pixels
    spread = squares / pixels - center * center
    return (center, lax.rsqrt(spread + epsilon), pixels)


def project_over_chan(values, kernel):
    return lax.psum_scatter(convolve(values, kernel), "chan", scatter_dimension=3, tiled=True)


def conv_backward(upstream, values, kernel):
    columns = lax.all_gather(upstream, "chan", axis=3, tiled=True)
    offset = jnp.int32(0)
    inputs_grad = jnp.zeros_like(values)
    kernel_grad = jnp.zeros_like(kernel)
    breadth = columns.shape[3]
    kernel_part = lax.dynamic_slice_in_dim(kernel, offset, breadth, 3)
    primal, pull = jax.vjp(convolve, values, kernel_part)
    values_part, kernel_part_grad = pull(columns)
    kernel_grad = lax.dynamic_update_slice_in_dim(kernel_grad, kernel_part_grad, offset, 3)
    return (inputs_grad + values_part, kernel_grad)


def batch_sums(dpre, scaled):
    return lax.psum((jnp.sum(dpre, axis=(0, 1, 2)), jnp.sum(dpre * scaled, axis=(0, 1, 2))), "dp")


def plain_on_device(
    image_rows,
    groups,
    conv_first,
    conv_second,
    gain_first,
    shift_first,
    gain_second,
    shift_second,
    cotangent,
):
    inputs = lax.all_to_all(image_rows, "chan", split_axis=3, concat_axis=1, tiled=True)
    validity = valid_pixels(groups, inputs.shape[1])
    cot_valid = cotangent * validity
    center_one, rscale_one, pixels = batch_moments(inputs, validity)
    scaled_one = (inputs - center_one) * rscale_one
    pre_one = scaled_one * gain_first + shift_first
    act_one = jax.nn.silu(pre_one) * validity
    inner = project_over_chan(act_one, conv_first) * validity
    center_two, rscale_two, pixels_again = batch_moments(inner, validity)
    scaled_two = (inner - center_two) * rscale_two
    pre_two = scaled_two * gain_second + shift_second
    act_two = jax.nn.silu(pre_two) * validity
    block_out = inputs * validity + project_over_chan(act_two, conv_second) * validity
    dact_two, kernel_two_part = conv_backward(cot_valid, act_two, conv_second)
    dpre_two = dact_two * validity * silu_slope(pre_two)
    shift_two_grad, gain_two_grad = batch_sums(dpre_two, scaled_two)
    dinner = (
        gain_second
        * rscale_two
        * (dpre_two - validity * (shift_two_grad + scaled_two * gain_two_grad) / pixels)
    )
    dact_one, kernel_one_part = conv_backward(dinner, act_one, conv_first)
    dpre_one = dact_one * validity * silu_slope(pre_one)
    shift_one_grad, gain_one_grad = batch_sums(dpre_one, scaled_one)
    small_squares = (
        jnp.sum(gain_one_grad**2)
        + jnp.sum(shift_one_grad**2)
        + jnp.sum(gain_two_grad**2)
        + jnp.sum(shift_two_grad**2)
    )
    kernel_one_sum, kernel_two_sum = lax.psum((kernel_one_part, kernel_two_part), "dp")
    local_sq = jnp.sum(kernel_one_sum**2) + jnp.sum(kernel_two_sum**2) + small_squares
    squares = lax.psum(local_sq, "chan")
    factor = sam_radius * lax.rsqrt(squares + norm_floor)
    kernel_one = conv_first + factor * kernel_one_sum
    kernel_two = conv_second + factor * kernel_two_sum
    grad_norm = jnp.sqrt(squares)
    moved_gain_one = gain_first + factor * gain_one_grad
    moved_shift_one = shift_first + factor * shift_one_grad
    moved_gain_two = gain_second + factor * gain_two_grad
    moved_shift_two = shift_second + factor * shift_two_grad
    pre_one_new = scaled_one * moved_gain_one + moved_shift_one
    act_one_new = jax.nn.silu(pre_one_new) * validity
    inner_new = project_over_chan(act_one_new, kernel_one) * validity
    scaled_two_new = (inner_new - center_two) * rscale_two
    pre_two_new = scaled_two_new * moved_gain_two + moved_shift_two
    act_two_new = jax.nn.silu(pre_two_new) * validity
    dact_two_new, kernel_two_grad = conv_backward(cot_valid, act_two_new, kernel_two)
    dpre_two_new = dact_two_new * validity * silu_slope(pre_two_new)
    gain_two_new_grad = jnp.sum(dpre_two_new * scaled_two_new, axis=(0, 1, 2))
    shift_two_new_grad = jnp.sum(dpre_two_new, axis=(0, 1, 2))
    dinner_new = moved_gain_two * rscale_two * dpre_two_new
    dact_one_new, kernel_one_grad = conv_backward(dinner_new, act_one_new, kernel_one)
    dpre_one_new = dact_one_new * validity * silu_slope(pre_one_new)
    gain_one_new_grad = jnp.sum(dpre_one_new * scaled_one, axis=(0, 1, 2))
    shift_one_new_grad = jnp.sum(dpre_one_new, axis=(0, 1, 2))
    inputs_grad = moved_gain_one * rscale_one * dpre_one_new + cot_valid
    input_grad = lax.all_to_all(inputs_grad, "chan", split_axis=1, concat_axis=3, tiled=True)
    (
        kernel_one_grad,
        kernel_two_grad,
        gain_one_new_grad,
        shift_one_new_grad,
        gain_two_new_grad,
        shift_two_new_grad,
    ) = lax.psum(
        (
            kernel_one_grad,
            kernel_two_grad,
            gain_one_new_grad,
            shift_one_new_grad,
            gain_two_new_grad,
            shift_two_new_grad,
        ),
        "dp",
    )
    return (
        block_out,
        input_grad,
        kernel_one_grad,
        kernel_two_grad,
        gain_one_new_grad,
        shift_one_new_grad,
        gain_two_new_grad,
        shift_two_new_grad,
        grad_norm,
    )


def solution(mesh):
    nd, nc = mesh.shape["dp"], mesh.shape["chan"]

    def on_device(image_rows, *rest):
        images, side, channels = image_rows.shape[0], image_rows.shape[2], image_rows.shape[3]
        fits = images == 1 and nc == 4 and nd == 2 * nc and channels // nd % 16 == 0 and side * side == 256
        if not fits:
            return plain_on_device(image_rows, *rest)
        return fused_on_device(Plan(nd, nc, channels, side), image_rows, *rest)

    return jax.shard_map(
        on_device,
        mesh=mesh,
        in_specs=(
            P("dp", "chan", None, None),
            P("dp"),
            P(None, None, "chan", None),
            P(None, None, "chan", None),
            P("chan"),
            P("chan"),
            P("chan"),
            P("chan"),
            P("dp", None, None, "chan"),
        ),
        out_specs=(
            P("dp", None, None, "chan"),
            P("dp", "chan", None, None),
            P(None, None, "chan", None),
            P(None, None, "chan", None),
            P("chan"),
            P("chan"),
            P("chan"),
            P("chan"),
            P(),
        ),
        check_vma=False,
    )
```

```python
import functools
import types

import jax
import jax.numpy as jnp
from jax import lax
from jax.experimental import pallas as pl
from jax.experimental.pallas import tpu as pltpu
from jax.sharding import PartitionSpec as P

epsilon = 1e-05
sam_radius = 0.05
norm_floor = 1e-06
MESH = pl.DeviceIdType.MESH
F32, BF16 = jnp.float32, jnp.bfloat16
VMEM, SMEM = pltpu.VMEM, pltpu.SMEM
DMA = pltpu.SemaphoreType.DMA
LIMIT = 60 << 20


class Plan:
    def __init__(self, nd, nc, channels, side):
        self.nd, self.nc, self.ch, self.side = nd, nc, channels, side
        self.cb, self.db, self.px = channels // nc, channels // nd, side * side
        self.ny = 2
        self.nz = nd // 2


def split(v):
    hi = v.astype(BF16)
    return hi, (v - hi.astype(F32)).astype(BF16)


def dot(a, b):
    return lax.dot_general(a, b, (((1,), (0,)), ((), ())), preferred_element_type=F32)


def dot_nt(a, b):
    return lax.dot_general(a, b, (((1,), (1,)), ((), ())), preferred_element_type=F32)


def edge_masks(side, px):
    lane = lax.broadcasted_iota(jnp.int32, (1, px), 1)
    col = lax.rem(lane, side)
    row = lax.div(lane, side)
    one = jnp.ones((1, px), F32)
    zero = jnp.zeros((1, px), F32)
    rows = {-1: jnp.where(row >= 1, one, zero), 0: None, 1: jnp.where(row < side - 1, one, zero)}
    cols = {-1: jnp.where(col >= 1, one, zero), 0: None, 1: jnp.where(col < side - 1, one, zero)}
    return rows, cols


def moved(v, lanes, mask):
    if lanes:
        v = pltpu.roll(v, (-lanes) % v.shape[1], axis=1)
    return v if mask is None else v * mask


def shifts(v, side, sign=1, taps=(-1, 0, 1)):
    rows, cols = edge_masks(side, v.shape[1])
    by_col = {s: moved(v, s, cols[s]) for s in (-1, 0, 1)}
    return [moved(by_col[sign * s], sign * r * side, rows[sign * r]) for r in taps for s in (-1, 0, 1)]


def gather_taps(prod, side, n):
    rows, cols = edge_masks(side, prod.shape[1])
    total = None
    for j, s in enumerate((-1, 0, 1)):
        part = None
        for i, r in enumerate((-1, 0, 1)):
            t = 3 * i + j
            m = moved(prod[t * n : (t + 1) * n], r * side, rows[r])
            part = m if part is None else part + m
        m = moved(part, s, cols[s])
        total = m if total is None else total + m
    return total


def sigmoid(t):
    return 1.0 / (1.0 + jnp.exp(-t))


def silu_and_slope(pre):
    s = sigmoid(pre)
    return pre * s, s * (1.0 + pre * (1.0 - s))


def lanes_sum(v):
    return jnp.sum(v, axis=1, keepdims=True)


def valid_map(flag, side, px):
    lane = lax.broadcasted_iota(jnp.int32, (1, px), 1)
    half = (lax.rem(lane, side) < side // 2) & (lax.div(lane, side) < side // 2)
    return jnp.where(half, jnp.ones((1, px), F32), flag)


def diagonal(n):
    return lax.broadcasted_iota(jnp.int32, (n, n), 0) == lax.broadcasted_iota(jnp.int32, (n, n), 1)


def to_row(col):
    return jnp.sum(jnp.where(diagonal(col.shape[0]), col, 0.0), axis=0, keepdims=True)


def to_col(row):
    return jnp.sum(jnp.where(diagonal(row.shape[1]), row, 0.0), axis=1, keepdims=True)


def stacked(rows, n):
    at = lax.broadcasted_iota(jnp.int32, (8, n), 0)
    out = jnp.zeros((8, n), F32)
    for k, row in enumerate(rows):
        out = jnp.where(at == k, row, out)
    return out


def send(src, dst, ss, rs, device):
    return pltpu.make_async_remote_copy(
        src_ref=src, dst_ref=dst, send_sem=ss, recv_sem=rs, device_id=device, device_id_type=MESH
    )


def here():
    return lax.axis_index("dp"), lax.axis_index("chan")


def greet(p):
    d, c = here()
    barrier = pltpu.get_barrier_semaphore()
    for j in range(1, p.nd):
        pl.semaphore_signal(barrier, inc=1, device_id=(lax.rem(d + j, p.nd), c), device_id_type=MESH)
    for j in range(1, p.nc):
        pl.semaphore_signal(barrier, inc=1, device_id=(d, lax.rem(c + j, p.nc)), device_id_type=MESH)
    pl.semaphore_wait(barrier, p.nd - 1 + p.nc - 1)


class ToAll:
    def __init__(self, axis, n, tile, slots, ss, rs):
        d, c = here()
        self.n, self.tile, self.slots, self.ss, self.rs = n, tile, slots, ss, rs
        self.me = d if axis == "dp" else c
        self.device = (lambda o: (o, c)) if axis == "dp" else (lambda o: (d, o))

    def start(self):
        self.slots[self.me] = self.tile[...]
        for j in range(1, self.n):
            to = lax.rem(self.me + j, self.n)
            send(self.tile, self.slots.at[self.me], self.ss.at[j], self.rs.at[self.me], self.device(to)).start()

    def finish(self):
        for j in range(1, self.n):
            other = lax.rem(self.me + j, self.n)
            send(self.tile, self.slots.at[other], self.ss.at[j], self.rs.at[other], self.device(other)).wait()

    def total(self):
        total = self.slots[0]
        for j in range(1, self.n):
            total = total + self.slots[j]
        return total


class Line:
    def __init__(self, p, view, ss, rs, sides=True):
        self.p, self.view, self.ss, self.rs, self.sides = p, view, ss, rs, sides
        d, self.c = here()
        self.z, self.y = lax.div(d, p.ny), lax.rem(d, p.ny)

    def copy(self, zs, sem, z_to, y_to):
        slot = zs * self.p.ny + self.y
        return send(self.view(slot), self.view(slot), self.ss.at[sem, zs], self.rs.at[slot], (z_to * self.p.ny + y_to, self.c))

    def up(self, zs):
        return self.copy(zs, 0, lax.min(self.z + 1, self.p.nz - 1), self.y)

    def down(self, zs):
        return self.copy(zs, 1, lax.max(self.z - 1, 0), self.y)

    def side(self, zs):
        return self.copy(zs, 2, self.z, 1 - self.y)

    def got(self, zs, y):
        slot = zs * self.p.ny + y
        send(self.view(slot), self.view(slot), self.ss.at[0, 0], self.rs.at[slot], (self.z * self.p.ny + 1 - self.y, self.c)).wait_recv()

    def hand_on(self, zs):
        pl.when((zs <= self.z) & (self.z < self.p.nz - 1))(lambda: self.up(zs).start())
        pl.when((zs >= self.z) & (self.z > 0))(lambda: self.down(zs).start())
        if self.sides:
            self.side(zs).start()

    def drain(self):
        for zs in range(self.p.nz):
            pl.when((zs <= self.z) & (self.z < self.p.nz - 1))(lambda: self.up(zs).wait_send())
            pl.when((zs >= self.z) & (self.z > 0))(lambda: self.down(zs).wait_send())
            if self.sides:
                self.side(zs).wait_send()


def nearest(z, k):
    t = lax.div(z, 2)
    low = z + t * (3 - 2 * z)
    first = 1 - lax.min(lax.div(k, 2), 1)
    place = k + low * first * (1 - 2 * k)
    return place * (1 - 2 * t) + 3 * t


class ChanSum:
    def __init__(self, p, r):
        self.p, self.r = p, r
        d, c = here()
        k = lax.rem(c, 2)
        self.hb = p.db // 2
        self.across, self.far = (d, c + 1 - 2 * k), (d, lax.rem(c + 2, 4))
        self.mine = pl.multiple_of(k * self.hb, 8)
        self.yours = pl.multiple_of((1 - k) * self.hb, 8)

    def first(self, i):
        r = self.r
        return send(r.part.at[i, pl.ds(self.yours, self.hb)], r.near.at[i], r.cs1.at[i], r.cr1.at[i], self.across)

    def second(self, i):
        r = self.r
        return send(r.half.at[i], r.away.at[i], r.cs2.at[i], r.cr2.at[i], self.far)

    def third(self, i, rows):
        r = self.r
        mine = r.sums.at[i, pl.ds(self.mine, self.hb)]
        return send(mine, r.sums.at[i, pl.ds(rows, self.hb)], r.cs3.at[i], r.cr3.at[i], self.across)

    def chip(self, i):
        r = self.r
        self.first(i).wait()
        r.half[i] = r.part[i, pl.ds(self.mine, self.hb)] + r.near[i]
        self.second(i).start()

    def cross(self, i):
        r = self.r
        self.second(i).wait()
        r.sums[i, pl.ds(self.mine, self.hb)] = r.half[i] + r.away[i]
        self.third(i, self.mine).start()

    def done(self, i):
        self.third(i, self.yours).wait()

    def advance(self, j, n, item):
        at = lambda m: item(lax.clamp(0, m, n - 1))
        pl.when((j >= 1) & (j < n + 1))(lambda: self.chip(at(j - 1)))
        pl.when((j >= 3) & (j < n + 3))(lambda: self.cross(at(j - 3)))
        pl.when((j >= 4) & (j < n + 4))(lambda: self.done(at(j - 4)))


class ImageSum:
    def __init__(self, p, part, near, acc, away, s1, r1, s2, r2):
        self.p, self.part, self.buf1, self.acc, self.buf2 = p, part, near, acc, away
        self.s1, self.r1, self.s2, self.r2 = s1, r1, s2, r2
        d, self.c = here()
        self.z, self.y = lax.div(d, p.ny), lax.rem(d, p.ny)

    def near(self, zs):
        side = 1 - self.y
        return send(self.part.at[zs * self.p.ny + side], self.buf1.at[zs], self.s1.at[zs], self.r1.at[zs],
                    (self.z * self.p.ny + side, self.c))

    def away(self, zs, slot):
        return send(self.acc.at[zs], self.buf2.at[slot], self.s2.at[zs], self.r2.at[slot], (zs * self.p.ny + self.y, self.c))

    def spread(self, zs):
        self.near(zs).wait()
        self.acc[zs] = self.part[zs * self.p.ny + self.y] + self.buf1[zs]
        pl.when(zs != self.z)(lambda: self.away(zs, self.z).start())

    def total(self):
        total = self.acc[self.z]
        for j in range(1, self.p.nz):
            other = lax.rem(self.z + j, self.p.nz)
            self.away(other, other).wait()
            total = total + self.buf2[other]
        return total


def scratch_of(p):
    nd, nc, cb, db, px, nz, ny = p.nd, p.nc, p.cb, p.db, p.px, p.nz, p.ny
    rows = px // nc
    f = lambda *s: VMEM(s, F32)
    h = lambda *s: VMEM(s, BF16)
    return dict(
        k1w=f(9, cb, 256), k2w=f(9, db, p.ch), ks=f(nc, cb, 9 * db), b2=f(cb, 9 * db),
        a1=f(9 * db, cb), a2=f(9 * db, cb), g1=f(9 * db, cb), g2=f(9 * db, cb),
        a_cat=h(2, 9 * db, 3 * cb), bm=h(2, cb, 9 * db), b2m=h(2, cb, 9 * db), colh=h(2, 9 * db, px), coll=h(2, 9 * db, px),
        xs=f(nc, rows, cb), rx=f(nc, rows, cb), xin=f(nd, cb, px), act1=f(nd, cb, px), slope1=f(nd, cb, px),
        call=f(nc, nd, cb, px),
        part=f(3 * nd, db, px), near=f(3 * nd, db // 2, px), half=f(3 * nd, db // 2, px), away=f(3 * nd, db // 2, px),
        sums=f(3 * nd, db, px), slope2=f(nd, db, px), dpre=f(nd, db, px), add1=f(2, cb, px), add2=f(2, db, px),
        outp=f(nd, cb, px), outn=f(nz, cb, px), outc=f(nz, cb, px), outw=f(nz, cb, px),
        inp=f(nd, cb, px), inn=f(nz, cb, px), inc=f(nz, cb, px), inw=f(nz, cb, px),
        dall=f(nd, nd, db, px), act2=f(ny, nd, db, px), own2=f(nd, db, px), left=h(9 * cb, 6 * px), right=h(p.ch, 6 * px),
        stage=f(9 * cb, p.ch),
        par=f(8, cb), pars=f(nc, 8, cb), stat=f(8, cb), stats=f(nd, 8, cb), msg=f(8, cb), msgs=f(nd, 8, cb),
        sq=f(8, 128), sqs=f(nc, 8, 128), vec=f(8, cb), vecs=f(nd, 8, cb),
        k1_sem=DMA, k2_sem=DMA, g1_sem=DMA, g2_sem=DMA,
        xs_s=DMA((nc,)), xs_r=DMA((nc,)), ks_s=DMA((nc,)), ks_r=DMA,
        par_s=DMA((nc,)), par_r=DMA((nc,)), stat_s=DMA((nd,)), stat_r=DMA((nd,)), msg_s=DMA((nd,)), msg_r=DMA((nd,)),
        sq_s=DMA((nc,)), sq_r=DMA((nc,)), vec_s=DMA((nd,)), vec_r=DMA((nd,)),
        x_s=DMA((3, nz)), x_r=DMA((nd,)), c_s=DMA((3, nz)), c_r=DMA((nd,)), d_s=DMA((3, nz)), d_r=DMA((nd,)),
        cs1=DMA((3 * nd,)), cr1=DMA((3 * nd,)), cs2=DMA((3 * nd,)), cr2=DMA((3 * nd,)), cs3=DMA((3 * nd,)), cr3=DMA((3 * nd,)),
        o_s1=DMA((nz,)), o_r1=DMA((nz,)), o_s2=DMA((nz,)), o_r2=DMA((nz,)),
        i_s1=DMA((nz,)), i_r1=DMA((nz,)), i_s2=DMA((nz,)), i_r2=DMA((nz,)),
        call_s=DMA((2, nd)), call_r=DMA((2, nd)), own_s=DMA, f_s=DMA((3, nz)), f_r=DMA((nd,)), col_s=DMA((nz,)), act_s=DMA((3, nd)), act_r=DMA((ny, nd)),
        far_s=DMA((nd,)), far_r=DMA((nd,)), core_s=DMA((2, nd)), core_r=DMA((2, nd)), in_s=DMA((nc,)), in_r=DMA((nc,)),
    )


FARS = (3, 9, 13)
OUTS_AT = (24, 25, 26, 27)
ACT = (44, 8, 4)
LINE_AT = (5, 9, 12)
SIDE_AT = (6, 11, 14, 17)
NEAR_AT = 15
SUMS_AT = (18, 20, 22, 24)
ROWS_AT = 28

ARGS = ("x", "cot", "k1", "k2", "gain1", "shift1", "gain2", "shift2", "groups")
OUTS = ("block_out", "input_grad", "g1_out", "g2_out", "small")


def step_kernel(p, names, *refs):
    r = types.SimpleNamespace(**dict(zip(names, refs)))
    cb, db, px, side, nd, nc, nz, ny = p.cb, p.db, p.px, p.side, p.nd, p.nc, p.nz, p.ny
    d, c = here()
    z, y = lax.div(d, ny), lax.rem(d, ny)
    k = lax.rem(c, 2)
    far, across = lax.rem(c + 2, 4), c + 1 - 2 * k
    last = 6 - c - far - across
    rows = px // nc
    owner = (1 - lax.div(z, 2)) * (2 - 2 * lax.rem(z, 2)) + lax.div(z, 2) * (1 + 2 * lax.rem(z, 2))
    origin = lambda c: (1 - c // 2) * (1 + c % 2) + c // 2 * 3 * (c % 2)
    start_z = (1 - lax.div(c, 2)) * (1 + k) + lax.div(c, 2) * 3 * k
    first = owner * cb + y * db
    slots = [origin(q) * ny + j for q in range(nc) for j in range(ny)]
    image = lambda j: nearest(z, lax.div(j, 2)) * ny + y + lax.rem(j, 2) * (1 - 2 * y)

    base = lax.min(lax.div(first, 128), (p.ch - 256) // 128) * 128
    k1_copy = pltpu.make_async_copy(r.k1.at[:, :, pl.ds(pl.multiple_of(base, 128), 256)], r.k1w, r.k1_sem)
    k1_copy.start()
    k2_rows = pl.ds(pl.multiple_of(y * db, 8), db)
    k2_copy = pltpu.make_async_copy(r.k2.at[:, k2_rows], r.k2w, r.k2_sem)
    pl.when(c == owner)(lambda: k2_copy.start())
    greet(p)

    for j in range(nc):
        r.xs[j] = r.x[:, j * cb : (j + 1) * cb]
    a2a = lambda j: send(r.xs.at[lax.rem(c + j, nc)], r.rx.at[c], r.xs_s.at[j], r.xs_r.at[c], (d, lax.rem(c + j, nc)))
    for j in range(1, nc):
        a2a(j).start()
    r.rx[c] = r.xs[c]
    r.par[...] = stacked([r.gain2[...].reshape(1, cb), r.shift2[...].reshape(1, cb)], cb)
    params = ToAll("chan", nc, r.par, r.pars, r.par_s, r.par_r)
    params.start()
    flag = jnp.full((1, 1), jnp.where(r.groups[0] == 1, 1.0, 0.0), F32)
    mine = valid_map(flag, side, px)
    r.call[c, d] = r.cot[...].T * mine

    def meet(line, step, then=None):
        def one(zs):
            line.got(zs, y)
            line.hand_on(zs)
            if then is not None:
                then(zs)

        pl.when(z >= step)(lambda: one(lax.max(z - step, 0)))
        pl.when(z + step < nz)(lambda: one(lax.min(z + step, nz - 1)))

    cots = Line(p, lambda s: r.call.at[c, s], r.c_s, r.c_r)
    cots.hand_on(z)
    own_cot = lambda q: send(r.call.at[q, d], r.call.at[q, d], r.own_s, r.f_r.at[d], (d, far))
    fars = Line(p, lambda s: r.call.at[far, s], r.f_s, r.f_r, False)
    column = lambda q, zs: send(
        r.call.at[q, zs * ny + 1 - y], r.call.at[q, zs * ny + 1 - y], r.col_s.at[zs], r.f_r.at[zs * ny + 1 - y], (d, far)
    )
    call_copy = lambda lane, q, i: send(
        r.call.at[q, i], r.call.at[q, i], r.call_s.at[lane, i], r.call_r.at[lane, i], (d, across)
    )

    @pl.when(c == owner)
    def _():
        k2_copy.wait()
        for j in range(nc):
            r.ks[j] = r.k2w[:, :, j * cb : (j + 1) * cb].reshape(9 * db, cb).T

    for j in range(1, nc):
        a2a(j).wait_send()
        other = lax.rem(c + j, nc)
        send(r.xs.at[other], r.rx.at[other], r.xs_s.at[j], r.xs_r.at[other], (d, other)).wait_recv()
    r.xin[d] = r.rx[...].reshape(px, cb).T
    ins = Line(p, lambda s: r.xin.at[s], r.x_s, r.x_r)

    count = lanes_sum(mine)
    total = lanes_sum(r.xin[d] * mine)
    off = r.xin[d] - total / count
    r.stat[...] = stacked([to_row(total), to_row(lanes_sum(mine * off * off)), jnp.broadcast_to(flag, (1, cb))], cb)
    stats = ToAll("dp", nd, r.stat, r.stats, r.stat_s, r.stat_r)
    stats.start()
    ins.hand_on(z)

    piece = lambda j: send(r.ks.at[lax.rem(c + j, nc)], r.b2, r.ks_s.at[j], r.ks_r, (d, lax.rem(c + j, nc)))

    @pl.when(c == owner)
    def _():
        for j in range(1, nc):
            piece(j).start()

    k1_copy.wait()
    turn = lax.rem(256 - (first - base), 256)
    b1 = jnp.concatenate([pltpu.roll(r.k1w[t], turn, axis=1)[:, :db] for t in range(9)], axis=1)
    hi, lo = split(b1)
    r.bm[0], r.bm[1] = hi, lo
    r.a1[...] = b1.T
    hi, lo = split(r.a1[...])
    r.a_cat[0] = jnp.concatenate([hi, hi, lo], axis=1)

    meet(cots, 1)
    own_cot(c).start()
    stats.finish()

    def val_of(i):
        return valid_map(r.stats[i, 2:3, 0:1], side, px)

    counts = [jnp.sum(val_of(i), keepdims=True) for i in range(nd)]
    pixels = functools.reduce(jnp.add, counts)
    center = functools.reduce(jnp.add, [r.stats[i, 0:1] for i in range(nd)]) / pixels
    spread = [r.stats[i, 1:2] + counts[i] * (r.stats[i, 0:1] / counts[i] - center) ** 2 for i in range(nd)]
    center1, rs1 = to_col(center), to_col(lax.rsqrt(functools.reduce(jnp.add, spread) / pixels + epsilon))
    gain1, shift1 = to_col(r.gain1[...].reshape(1, cb)), to_col(r.shift1[...].reshape(1, cb))

    chan = ChanSum(p, r)

    def first_map(i, gain, shift):
        val = val_of(i)
        act, slope = silu_and_slope((r.xin[i] - center1) * rs1 * gain + shift)
        act = act * val
        r.act1[i], r.slope1[i] = act, slope * val
        ah, al = split(act)
        prod = dot(r.a_cat[0], jnp.concatenate([ah, al, ah], axis=0))
        r.part[i] = gather_taps(prod, side, db) * val
        chan.first(i).start()

    def second_back(i, first):
        ch, cl = split(r.call[c, i])
        prod = dot(r.a_cat[1], jnp.concatenate([ch, cl, ch], axis=0))
        r.part[first + i] = gather_taps(prod, side, db) * val_of(i)
        chan.first(first + i).start()

    def back_item(j):
        return nd + image(j)

    def set_back(a2):
        for t in range(9):
            hi, lo = split(a2[(8 - t) * db : (9 - t) * db])
            r.a_cat[1, t * db : (t + 1) * db] = jnp.concatenate([hi, hi, lo], axis=1)

    def second_block():
        @pl.when(c == owner)
        def _():
            r.b2[...] = r.ks[c]

        @pl.when(c != owner)
        def _():
            send(r.ks.at[0], r.b2, r.ks_s.at[0], r.ks_r, (d, owner)).wait_recv()

        r.a2[...] = r.b2[...].T
        set_back(r.a2)
        b2h, b2l = split(r.b2[...])
        r.b2m[0], r.b2m[1] = b2h, b2l

    def forward(kk, _):
        zs = nearest(z, kk)
        first_map(zs * ny + y, gain1, shift1)
        chan.advance(2 * kk, nd, image)
        meet(ins, kk + 1)
        pl.when(kk == 0)(lambda: meet(cots, 2))
        pl.when(kk == 1)(lambda: meet(cots, 3))
        pl.when(kk == 1)(second_block)
        ins.got(zs, 1 - y)
        first_map(zs * ny + 1 - y, gain1, shift1)
        chan.advance(2 * kk + 1, nd, image)

        @pl.when(kk > 0)
        def _():
            before = nearest(z, lax.max(kk - 1, 0))
            second_back(before * ny + y, nd)
            chan.advance(2 * kk - 2, nd, back_item)
            cots.got(before, 1 - y)
            second_back(before * ny + 1 - y, nd)
            chan.advance(2 * kk - 1, nd, back_item)

        return 0

    lax.fori_loop(0, nz, forward, 0)
    furthest = nearest(z, nz - 1)
    chan.advance(nd, nd, image)
    second_back(furthest * ny + y, nd)
    chan.advance(nd - 2, nd, back_item)
    chan.advance(nd + 1, nd, image)
    cots.got(furthest, 1 - y)
    second_back(furthest * ny + 1 - y, nd)
    chan.advance(nd - 1, nd, back_item)
    chan.advance(nd + 2, nd, image)
    chan.advance(nd, nd, back_item)
    chan.advance(nd + 3, nd, image)

    params.finish()
    both = [r.pars[owner, j : j + 1] for j in range(2)]
    gain2, shift2 = (to_col(jnp.where(y == 0, v[:, :db], v[:, cb - db :])) for v in both)

    def add_up(i, carry):
        return carry + lanes_sum(r.sums[i] * val_of(i))

    chan.advance(nd + 1, nd, back_item)
    center2 = lax.fori_loop(0, nd, add_up, jnp.zeros((db, 1), F32)) / pixels

    def add_squares(i, carry):
        off = r.sums[i] - center2
        return carry + lanes_sum(val_of(i) * off * off)

    chan.advance(nd + 2, nd, back_item)
    rs2 = lax.rsqrt(lax.fori_loop(0, nd, add_squares, jnp.zeros((db, 1), F32)) / pixels + epsilon)

    chan.advance(nd + 3, nd, back_item)
    own_cot(far).wait_recv()
    fars.hand_on(z)
    for zs in range(nz):
        column(c, zs).start()

    def inner_sums(i, carry):
        val = val_of(i)
        scaled = (r.sums[i] - center2) * rs2
        act, slope = silu_and_slope(scaled * gain2 + shift2)
        r.own2[i] = act * val
        dpre = r.sums[nd + i] * (slope * val)
        r.dpre[i] = dpre
        return carry[0] + lanes_sum(dpre), carry[1] + lanes_sum(dpre * scaled)

    zero = jnp.zeros((db, 1), F32)
    sh2, gg2 = lax.fori_loop(0, nd, inner_sums, (zero, zero))

    outs = ImageSum(p, r.outp, r.outn, r.outc, r.outw, r.o_s1, r.o_r1, r.o_s2, r.o_r2)

    def set_cols(w, maps):
        for t, m in enumerate(maps):
            hi, lo = split(m)
            r.colh[w, t * db : (t + 1) * db] = hi
            r.coll[w, t * db : (t + 1) * db] = lo

    def im2col_dot(w, which):
        return dot(which[0], r.colh[w]) + dot(which[0], r.coll[w]) + dot(which[1], r.colh[w])

    def wgrad(w, other):
        oh, ol = split(other)
        left = jnp.concatenate([r.colh[w], r.colh[w], r.coll[w]], axis=1)
        return dot_nt(left, jnp.concatenate([oh, ol, oh], axis=1))

    r.g1[...] = jnp.zeros_like(r.g1)
    r.g2[...] = jnp.zeros_like(r.g2)
    change_item = lambda j: 2 * nd + j

    def settle(t):
        for step in range(1, nz):
            pl.when(t == FARS[step - 1])(lambda: meet(fars, step))

    def gradients(i, carry):
        scaled = (r.sums[i] - center2) * rs2
        dinner = gain2 * rs2 * (r.dpre[i] - val_of(i) * (sh2 + scaled * gg2) / pixels)
        set_cols(0, shifts(r.own2[i], side))
        set_cols(1, shifts(dinner, side, -1))
        r.outp[i] = im2col_dot(0, (r.b2m[0], r.b2m[1]))
        r.g2[...] += wgrad(0, r.call[c, i])
        r.g1[...] += wgrad(1, r.act1[i])
        dpre1 = im2col_dot(1, (r.bm[0], r.bm[1])) * r.slope1[i]
        scaled1 = (r.xin[i] - center1) * rs1
        pl.when((lax.rem(i, 2) == 1 - y) & (i < 2 * nz - 2))(lambda: outs.near(lax.div(i, 2)).start())
        call_copy(0, c, i).start()
        settle(i)
        return carry[0] + lanes_sum(dpre1), carry[1] + lanes_sum(dpre1 * scaled1)

    zero = jnp.zeros((cb, 1), F32)
    sh1, gg1 = lax.fori_loop(0, nd, gradients, (zero, zero))
    set_back(r.g2)

    square = jnp.sum(r.g1[...] * r.g1[...] + r.g2[...] * r.g2[...], keepdims=True)
    square = square + jnp.where(c == 0, jnp.sum(sh2 * sh2 + gg2 * gg2, keepdims=True), 0.0)
    r.msg[...] = stacked([to_row(sh1), to_row(gg1), jnp.broadcast_to(square, (1, cb))], cb)
    over_dp = ToAll("dp", nd, r.msg, r.msgs, r.msg_s, r.msg_r)
    over_dp.start()
    outs.near(nz - 1).start()

    def change(j, _):
        second_back(j, 2 * nd)
        chan.advance(j, nd, change_item)
        return 0

    lax.fori_loop(0, nd // 2, change, 0)
    over_dp.finish()
    total = over_dp.total()
    sh1, gg1 = to_col(total[0:1]), to_col(total[1:2])
    square = total[2:3, 0:1] + jnp.sum(sh1 * sh1 + gg1 * gg1, keepdims=True)
    r.sq[...] = jnp.broadcast_to(square, (8, 128))
    over_chan = ToAll("chan", nc, r.sq, r.sqs, r.sq_s, r.sq_r)
    over_chan.start()
    lax.fori_loop(nd // 2, nd, change, 0)
    over_chan.finish()
    square = over_chan.total()[0:1, 0:1]
    norm = jnp.sqrt(square)
    factor = sam_radius * lax.rsqrt(square + norm_floor)

    gain1, shift1 = gain1 + factor * gg1, shift1 + factor * sh1
    gain2, shift2 = gain2 + factor * gg2, shift2 + factor * sh2
    r.a1[...] += factor * r.g1[...]
    hi, lo = split(r.a1[...])
    r.a_cat[0] = jnp.concatenate([hi, hi, lo], axis=1)

    act_copy = lambda sem, ys, i, z_to, y_to: send(
        r.act2.at[ys, i], r.act2.at[ys, i], r.act_s.at[sem, i], r.act_r.at[ys, i], (z_to * ny + y_to, c)
    )
    act_up = lambda i: act_copy(0, y, i, lax.min(z + 1, nz - 1), y)
    act_down = lambda i: act_copy(1, y, i, lax.max(z - 1, 0), y)
    act_side = lambda i: act_copy(2, y, i, z, 1 - y)

    def act_hand_on(i):
        pl.when((z >= start_z) & (z < nz - 1))(lambda: act_up(i).start())
        pl.when((z <= start_z) & (z > 0))(lambda: act_down(i).start())
        act_side(i).start()

    def second_act(i):
        val = val_of(i)
        act, slope = silu_and_slope((r.sums[i] - center2) * rs2 * gain2 + shift2)
        r.slope2[i] = slope * val
        r.own2[i] = act * val

    def far_to_core(j):
        zs = nearest(z, lax.div(j, 2))
        pl.when(lax.rem(j, 2) == 1)(lambda: column(far, zs).wait_recv())
        call_copy(1, far, image(j)).start()

    away = lax.max(z - start_z, start_z - z)

    def act_step(t):
        for i in range(nd):

            @pl.when((away > 0) & (t == lax.div(ACT[0] + ACT[1] * away + ACT[2] * i, 4)))
            def _():
                act_copy(0, y, i, z, 1 - y).wait_recv()
                act_hand_on(i)

    pair = lambda s, q: r.dall.at[s, pl.ds(2 * q, 2)]
    grads = Line(p, lambda s: pair(s, c), r.d_s, r.d_r)
    to_far = lambda s, q: send(pair(s, q), pair(s, q), r.far_s.at[s], r.far_r.at[s], (d, far))
    to_core = lambda lane, s, q: send(pair(s, q), pair(s, q), r.core_s.at[lane, s], r.core_r.at[lane, s], (d, across))

    def over_chan_too(s):
        to_far(s, c).start()
        to_core(0, s, c).start()

    def meet_sides(step):
        def one(zs):
            grads.got(zs, 1 - y)
            over_chan_too(zs * ny + 1 - y)

        pl.when(z >= step)(lambda: one(lax.max(z - step, 0)))
        if step > 0:
            pl.when(z + step < nz)(lambda: one(lax.min(z + step, nz - 1)))

    hi, lo = split(r.a1[...].T)
    r.bm[0], r.bm[1] = hi, lo
    ins_grad = ImageSum(p, r.inp, r.inn, r.inc, r.inw, r.i_s1, r.i_r1, r.i_s2, r.i_r2)
    r.add1[...] = jnp.zeros_like(r.add1)
    r.add2[...] = jnp.zeros_like(r.add2)

    def inner_grad(i):
        second_act(i)
        dpre = (r.sums[nd + i] + factor * r.sums[2 * nd + i]) * r.slope2[i]
        r.dall[d, i] = gain2 * rs2 * dpre
        r.add2[0] += dpre
        r.add2[1] += dpre * ((r.sums[i] - center2) * rs2)

        @pl.when(z == start_z)
        def _():
            r.act2[y, i] = r.own2[i]
            act_hand_on(i)

    def rows_grad(i):
        set_cols(1, shifts(r.dall[d, i], side, -1))
        dact1 = im2col_dot(1, (r.bm[0], r.bm[1]))
        r.inp[i] = dact1
        dpre1 = dact1 * r.slope1[i]
        r.add1[0] += dpre1
        r.add1[1] += dpre1 * ((r.xin[i] - center1) * rs1)

    same = lambda j: j

    def start(j, _):
        settle(nd + j)
        first_map(j, gain1, shift1)
        chan.advance(nd + j, nd, change_item)
        chan.advance(j, nd, same)
        return 0

    def steady(j, _):
        first_map(j, gain1, shift1)
        chan.advance(j, nd, same)
        settle(nd + j)
        inner_grad(j - 4)
        act_step(j)
        return 0

    def end(j, _):
        chan.advance(j, nd, same)
        settle(nd + j)
        inner_grad(j - 4)
        act_step(j)
        return 0

    lax.fori_loop(0, 4, start, 0)
    lax.fori_loop(4, nd, steady, 0)
    lax.fori_loop(nd, nd + 4, end, 0)
    grads.hand_on(z)
    back = lambda j: send(r.xs.at[lax.rem(c + j, nc)], r.rx.at[c], r.in_s.at[j], r.in_r.at[c], (d, lax.rem(c + j, nc)))

    def input_rows():
        grad = (gain1 * rs1 * (ins_grad.total() * r.slope1[d]) + r.call[c, d]).T
        for j in range(nc):
            r.xs[j] = grad[j * rows : (j + 1) * rows]
        for j in range(1, nc):
            back(j).start()
        r.rx[c] = r.xs[c]

    def gather_grads(u):
        for step in range(1, nz):
            pl.when(u == LINE_AT[step - 1])(lambda: meet(grads, step, lambda zs: over_chan_too(zs * ny + y)))
        for step in range(nz):
            pl.when(u == SIDE_AT[step])(lambda: meet_sides(step))

        @pl.when(u == NEAR_AT)
        def _():
            for o in range(nz):
                ins_grad.near(nearest(z, nz - 1 - o)).start()

        for o in range(nz):
            pl.when(u == SUMS_AT[o])(lambda: ins_grad.spread(nearest(z, nz - 1 - o)))
        pl.when(u == ROWS_AT)(input_rows)
        for zs in range(nz):
            pl.when(u == OUTS_AT[zs])(lambda: outs.spread(zs))

    def all_rows(i, _):
        far_to_core(i)
        rows_grad(i)
        act_step(nd + 4 + i)
        gather_grads(i)
        return 0

    lax.fori_loop(0, nd, all_rows, 0)
    sh1, gg1 = lanes_sum(r.add1[0]), lanes_sum(r.add1[1])
    sh2, gg2 = lanes_sum(r.add2[0]), lanes_sum(r.add2[1])

    pad = jnp.zeros((1, cb - db), F32)
    wide = lambda col: jnp.concatenate([to_row(col), pad], axis=1)
    r.vec[...] = stacked([to_row(sh1), to_row(gg1), wide(sh2), wide(gg2)], cb)
    vectors = ToAll("dp", nd, r.vec, r.vecs, r.vec_s, r.vec_r)
    vectors.start()

    def kernel_grad(images, left_of, rights_of, between):
        def put_left(m):
            for j, i in enumerate(images):
                lanes = slice(3 * j * px, 3 * (j + 1) * px)
                for t, v in enumerate(shifts(left_of(i), side, 1, (m - 1,))):
                    hi, lo = split(v)
                    r.left[(3 * m + t) * cb : (3 * m + t + 1) * cb, lanes] = jnp.concatenate([hi, hi, lo], axis=1)

        def add(m):
            third = slice(3 * m * cb, 3 * (m + 1) * cb)
            r.stage[third] += dot_nt(r.left[third], r.right[...])

        for j, i in enumerate(images):
            lanes = slice(3 * j * px, 3 * (j + 1) * px)
            at = 0
            for v in rights_of(i):
                n = v.shape[0]
                hi, lo = split(v)
                r.right[at : at + n, lanes] = jnp.concatenate([hi, lo, hi], axis=1)
                at += n
        put_left(0)
        add(0)
        put_left(1)
        between(0)
        add(1)
        put_left(2)
        between(1)
        add(2)
        between(2)

    r.stage[...] = jnp.zeros_like(r.stage)

    def second_kernel(q, _):
        zs = nearest(z, q)
        for j in range(2):
            act_copy(0, 1 - y, 2 * q + j, z, 1 - y).wait_recv()
            call_copy(0, across, 2 * q + j).wait_recv()
            call_copy(1, last, 2 * q + j).wait_recv()

        def between(m):
            u = nd + 3 * q + m
            act_step(nd + 4 + u)
            gather_grads(u)

        kernel_grad(
            [2 * q, 2 * q + 1],
            lambda i: jnp.concatenate([r.act2[0, i], r.act2[1, i]], axis=0),
            lambda i: [r.call[j, i] for j in range(nc)],
            between,
        )
        return 0

    lax.fori_loop(0, nz, second_kernel, 0)
    g2_copy = pltpu.make_async_copy(r.stage, r.g2_out, r.g2_sem)
    g2_copy.start()

    gather_grads(20)
    g2_copy.wait()
    r.stage[...] = jnp.zeros_like(r.stage)

    def first_kernel(j, _):
        @pl.when(j == 1)
        def _():
            for o in range(1, nd):
                to_core(0, lax.rem(d + o, nd), across).wait_recv()

        @pl.when(j == 2)
        def _():
            for o in range(1, nd):
                s = lax.rem(d + o, nd)
                to_far(s, far).wait_recv()
                to_core(1, s, far).start()

        @pl.when(j == 3)
        def _():
            for o in range(1, nd):
                to_core(1, lax.rem(d + o, nd), last).wait_recv()

        q = jnp.where(j == 0, c, jnp.where(j == 1, across, jnp.where(j == 2, far, last)))

        def between(m):
            gather_grads(21 + 3 * j + m)

        kernel_grad([2 * q, 2 * q + 1], lambda i: r.act1[i], lambda i: [r.dall[s, i] for s in slots], between)
        return 0

    lax.fori_loop(0, nc, first_kernel, 0)
    gather_grads(33)
    r.block_out[...] = ((r.xin[d] + outs.total()) * mine).T
    g1_copy = pltpu.make_async_copy(r.stage, r.g1_out, r.g1_sem)
    g1_copy.start()

    vectors.finish()
    total = vectors.total()
    rows_of = lambda j: jnp.concatenate([r.vecs[start_z * ny + q, j : j + 1, :db] for q in range(ny)], axis=1)
    r.small[...] = stacked([total[0:1], total[1:2], rows_of(2), rows_of(3), jnp.broadcast_to(norm, (1, cb))], cb)
    for j in range(1, nc):
        back(j).wait_send()
        other = lax.rem(c + j, nc)
        send(r.xs.at[other], r.rx.at[other], r.in_s.at[0], r.in_r.at[other], (d, other)).wait_recv()
    for j in range(nc):
        r.input_grad[:, j * cb : (j + 1) * cb] = r.rx[j]

    own_cot(c).wait_send()
    for line in (ins, cots, fars, grads):
        line.drain()
    for zs in range(nz):
        column(c, zs).wait_send()

    @pl.when(c == owner)
    def _():
        for j in range(1, nc):
            piece(j).wait_send()

    def sent(i, _):
        call_copy(0, c, i).wait_send()
        call_copy(1, far, i).wait_send()
        pl.when((z >= start_z) & (z < nz - 1))(lambda: act_up(i).wait_send())
        pl.when((z <= start_z) & (z > 0))(lambda: act_down(i).wait_send())
        act_side(i).wait_send()
        return 0

    lax.fori_loop(0, nd, sent, 0)
    for j in range(1, nd):
        s = lax.rem(d + j, nd)
        to_far(s, c).wait_send()
        to_core(0, s, c).wait_send()
        to_core(1, s, far).wait_send()
    g1_copy.wait()


def close_kernel(pieces, small, block_in, rows_in, first_in, second_in, block_out, rows_out, first_out, second_out,
                 gg1, sh1, gg2, sh2, norm, first, second, vec, sems, side_sems):
    cut = first_in.shape[0] // pieces
    legs = []
    for j in range(pieces):
        part = pl.ds(j * cut, cut)
        for k, (src, mid, dst) in enumerate(((second_in, second, second_out), (first_in, first, first_out))):
            legs.append((
                pltpu.make_async_copy(src.at[part], mid.at[part], sems.at[0, k, j]),
                pltpu.make_async_copy(mid.at[part], dst.at[part], sems.at[1, k, j]),
            ))
    sides = [pltpu.make_async_copy(a, b, side_sems.at[j])
             for j, (a, b) in enumerate(((small, vec), (block_in, block_out), (rows_in, rows_out)))]
    for cp in sides:
        cp.start()
    for come, _ in legs:
        come.start()
    sides[0].wait()
    for j, ref in enumerate((sh1, gg1, sh2, gg2)):
        ref[...] = vec[j : j + 1].reshape(vec.shape[1])
    norm[0] = jnp.sum(vec[4:5, 0:1])
    for come, go in legs:
        come.wait()
        go.start()
    for _, go in legs:
        go.wait()
    for cp in sides[1:]:
        cp.wait()


def fused_on_device(p, image_rows, groups, conv_first, conv_second, gain_first, shift_first, gain_second, shift_second, cotangent):
    cb, px = p.cb, p.px
    rows = px // p.nc
    scratch = scratch_of(p)
    out = lambda *s: jax.ShapeDtypeStruct(s, F32)
    any_, vmem, smem = (pl.BlockSpec(memory_space=m) for m in (pl.ANY, VMEM, SMEM))
    large = (out(px, cb), out(rows, p.ch), out(9 * cb, p.ch), out(9 * cb, p.ch))
    block_out, input_grad, g1, g2, small = pl.pallas_call(
        functools.partial(step_kernel, p, ARGS + OUTS + tuple(scratch)),
        out_shape=large + (out(8, cb),),
        in_specs=[vmem, vmem, any_, any_, vmem, vmem, vmem, vmem, smem],
        out_specs=(vmem, vmem, any_, any_, vmem),
        scratch_shapes=list(scratch.values()),
        compiler_params=pltpu.CompilerParams(collective_id=0, has_side_effects=True, vmem_limit_bytes=LIMIT),
    )(
        image_rows.reshape(rows, p.ch), cotangent.reshape(px, cb), conv_first.reshape(9, cb, p.ch),
        conv_second.reshape(9, cb, p.ch), gain_first, shift_first, gain_second, shift_second, groups,
    )
    pieces = 6
    block_out, input_grad, g1, g2, gg1, sh1, gg2, sh2, norm = pl.pallas_call(
        functools.partial(close_kernel, pieces),
        out_shape=large + (out(cb),) * 4 + (out(1),),
        in_specs=[any_] * 5,
        out_specs=(vmem, vmem, any_, any_) + (vmem,) * 4 + (smem,),
        scratch_shapes=[VMEM((9 * cb, p.ch), F32), VMEM((9 * cb, p.ch), F32), VMEM((8, cb), F32), DMA((2, 2, pieces)), DMA((3,))],
        compiler_params=pltpu.CompilerParams(vmem_limit_bytes=LIMIT),
    )(small, block_out, input_grad, g1, g2)
    return (
        block_out.reshape(cotangent.shape), input_grad.reshape(image_rows.shape),
        g1.reshape(conv_first.shape), g2.reshape(conv_second.shape), gg1, sh1, gg2, sh2, norm.reshape(()),
    )


def valid_pixels(groups, extent_full):
    places = jnp.arange(extent_full, dtype=jnp.int32)
    extent = jnp.where(groups == 1, extent_full, extent_full // 2).astype(jnp.int32)
    inside = places[None, :] < extent[:, None]
    return (inside[:, :, None] & inside[:, None, :]).astype(jnp.float32)[..., None]


def convolve(values, kernel):
    return lax.conv_general_dilated(
        values,
        kernel,
        (1, 1),
        "SAME",
        dimension_numbers=("NHWC", "HWIO", "NHWC"),
        precision=lax.Precision.HIGHEST,
    )


def silu_slope(preact):
    sigmoid = jax.nn.sigmoid(preact)
    return sigmoid * (1.0 + preact * (1.0 - sigmoid))


def batch_moments(values, validity):
    summed, squares, pixels = lax.psum(
        (
            jnp.sum(values * validity, axis=(0, 1, 2)),
            jnp.sum(validity * values * values, axis=(0, 1, 2)),
            jnp.sum(validity),
        ),
        "dp",
    )
    center = summed / pixels
    spread = squares / pixels - center * center
    return (center, lax.rsqrt(spread + epsilon), pixels)


def project_over_chan(values, kernel):
    return lax.psum_scatter(convolve(values, kernel), "chan", scatter_dimension=3, tiled=True)


def conv_backward(upstream, values, kernel):
    columns = lax.all_gather(upstream, "chan", axis=3, tiled=True)
    offset = jnp.int32(0)
    inputs_grad = jnp.zeros_like(values)
    kernel_grad = jnp.zeros_like(kernel)
    breadth = columns.shape[3]
    kernel_part = lax.dynamic_slice_in_dim(kernel, offset, breadth, 3)
    primal, pull = jax.vjp(convolve, values, kernel_part)
    values_part, kernel_part_grad = pull(columns)
    kernel_grad = lax.dynamic_update_slice_in_dim(kernel_grad, kernel_part_grad, offset, 3)
    return (inputs_grad + values_part, kernel_grad)


def batch_sums(dpre, scaled):
    return lax.psum((jnp.sum(dpre, axis=(0, 1, 2)), jnp.sum(dpre * scaled, axis=(0, 1, 2))), "dp")


def plain_on_device(
    image_rows,
    groups,
    conv_first,
    conv_second,
    gain_first,
    shift_first,
    gain_second,
    shift_second,
    cotangent,
):
    inputs = lax.all_to_all(image_rows, "chan", split_axis=3, concat_axis=1, tiled=True)
    validity = valid_pixels(groups, inputs.shape[1])
    cot_valid = cotangent * validity
    center_one, rscale_one, pixels = batch_moments(inputs, validity)
    scaled_one = (inputs - center_one) * rscale_one
    pre_one = scaled_one * gain_first + shift_first
    act_one = jax.nn.silu(pre_one) * validity
    inner = project_over_chan(act_one, conv_first) * validity
    center_two, rscale_two, pixels_again = batch_moments(inner, validity)
    scaled_two = (inner - center_two) * rscale_two
    pre_two = scaled_two * gain_second + shift_second
    act_two = jax.nn.silu(pre_two) * validity
    block_out = inputs * validity + project_over_chan(act_two, conv_second) * validity
    dact_two, kernel_two_part = conv_backward(cot_valid, act_two, conv_second)
    dpre_two = dact_two * validity * silu_slope(pre_two)
    shift_two_grad, gain_two_grad = batch_sums(dpre_two, scaled_two)
    dinner = (
        gain_second
        * rscale_two
        * (dpre_two - validity * (shift_two_grad + scaled_two * gain_two_grad) / pixels)
    )
    dact_one, kernel_one_part = conv_backward(dinner, act_one, conv_first)
    dpre_one = dact_one * validity * silu_slope(pre_one)
    shift_one_grad, gain_one_grad = batch_sums(dpre_one, scaled_one)
    small_squares = (
        jnp.sum(gain_one_grad**2)
        + jnp.sum(shift_one_grad**2)
        + jnp.sum(gain_two_grad**2)
        + jnp.sum(shift_two_grad**2)
    )
    kernel_one_sum, kernel_two_sum = lax.psum((kernel_one_part, kernel_two_part), "dp")
    local_sq = jnp.sum(kernel_one_sum**2) + jnp.sum(kernel_two_sum**2) + small_squares
    squares = lax.psum(local_sq, "chan")
    factor = sam_radius * lax.rsqrt(squares + norm_floor)
    kernel_one = conv_first + factor * kernel_one_sum
    kernel_two = conv_second + factor * kernel_two_sum
    grad_norm = jnp.sqrt(squares)
    moved_gain_one = gain_first + factor * gain_one_grad
    moved_shift_one = shift_first + factor * shift_one_grad
    moved_gain_two = gain_second + factor * gain_two_grad
    moved_shift_two = shift_second + factor * shift_two_grad
    pre_one_new = scaled_one * moved_gain_one + moved_shift_one
    act_one_new = jax.nn.silu(pre_one_new) * validity
    inner_new = project_over_chan(act_one_new, kernel_one) * validity
    scaled_two_new = (inner_new - center_two) * rscale_two
    pre_two_new = scaled_two_new * moved_gain_two + moved_shift_two
    act_two_new = jax.nn.silu(pre_two_new) * validity
    dact_two_new, kernel_two_grad = conv_backward(cot_valid, act_two_new, kernel_two)
    dpre_two_new = dact_two_new * validity * silu_slope(pre_two_new)
    gain_two_new_grad = jnp.sum(dpre_two_new * scaled_two_new, axis=(0, 1, 2))
    shift_two_new_grad = jnp.sum(dpre_two_new, axis=(0, 1, 2))
    dinner_new = moved_gain_two * rscale_two * dpre_two_new
    dact_one_new, kernel_one_grad = conv_backward(dinner_new, act_one_new, kernel_one)
    dpre_one_new = dact_one_new * validity * silu_slope(pre_one_new)
    gain_one_new_grad = jnp.sum(dpre_one_new * scaled_one, axis=(0, 1, 2))
    shift_one_new_grad = jnp.sum(dpre_one_new, axis=(0, 1, 2))
    inputs_grad = moved_gain_one * rscale_one * dpre_one_new + cot_valid
    input_grad = lax.all_to_all(inputs_grad, "chan", split_axis=1, concat_axis=3, tiled=True)
    (
        kernel_one_grad,
        kernel_two_grad,
        gain_one_new_grad,
        shift_one_new_grad,
        gain_two_new_grad,
        shift_two_new_grad,
    ) = lax.psum(
        (
            kernel_one_grad,
            kernel_two_grad,
            gain_one_new_grad,
            shift_one_new_grad,
            gain_two_new_grad,
            shift_two_new_grad,
        ),
        "dp",
    )
    return (
        block_out,
        input_grad,
        kernel_one_grad,
        kernel_two_grad,
        gain_one_new_grad,
        shift_one_new_grad,
        gain_two_new_grad,
        shift_two_new_grad,
        grad_norm,
    )


def solution(mesh):
    nd, nc = mesh.shape["dp"], mesh.shape["chan"]

    def on_device(image_rows, *rest):
        images, side, channels = image_rows.shape[0], image_rows.shape[2], image_rows.shape[3]
        fits = images == 1 and nc == 4 and nd == 2 * nc and channels // nd % 16 == 0 and side * side == 256
        if not fits:
            return plain_on_device(image_rows, *rest)
        return fused_on_device(Plan(nd, nc, channels, side), image_rows, *rest)

    return jax.shard_map(
        on_device,
        mesh=mesh,
        in_specs=(
            P("dp", "chan", None, None),
            P("dp"),
            P(None, None, "chan", None),
            P(None, None, "chan", None),
            P("chan"),
            P("chan"),
            P("chan"),
            P("chan"),
            P("dp", None, None, "chan"),
        ),
        out_specs=(
            P("dp", None, None, "chan"),
            P("dp", "chan", None, None),
            P(None, None, "chan", None),
            P(None, None, "chan", None),
            P("chan"),
            P("chan"),
            P("chan"),
            P("chan"),
            P(),
        ),
        check_vma=False,
    )
```
